128 devices in a mesh: inl: 16 (over x, z), xl: 8 (over y, core).
Axes of the slice: x: 4, y: 4, z: 4, core: 2. Of those that a mesh axis runs over, the one named last changes fastest.
Arguments:
- traces: bfloat16 [65536, 2048], P(('inl', 'xl')), may hold values from -6 to 6
- dest_tile: int32 [65536, 1], P(('inl', 'xl')), may hold values from 0 to 127; in each aligned block of 512 rows (0 to 511, 512 to 1023, ...) at most 6 rows name the same one
- bin_in_tile: int32 [65536], P(('inl', 'xl')), may hold values from 0 to 383
- fold: int32 [256, 192], P('inl', 'xl'), may hold values from 1 to 8
- thresholds: float32 [3, 7], replicated, may hold values from 0.05 to 0.8
Outputs:
- denoised: float32 [256, 192, 2048], P('inl', 'xl')
The draws below stay inside these ranges and needn't reach their ends.
Inputs may be any that keep to these rules, and one draw needn't show every extreme that they name: `dest_tile`: in each shot group of 512 traces no tile is named more than 6 times, a bound that some block reaches.
All inputs are finite; a program needn't handle non-finite values.
Results may differ from the reference program's by a relative error of at most 0.0003.
Values may be sent and summed in bfloat16 or wider, within the bound.
No kernel may reach another device: no remote copies, remote signals or barrier semaphores. Data moves between devices by JAX's collectives and lax.ppermute only.
A program may use at most 128 MiB of HBM per device.

```python
import math
import jax
import jax.numpy as jnp
import numpy as np
from jax import lax

NT = 2048
IC = 16
XC = 24
TR_DEV = 512
LEVELS = 3
BANDS = 7
CAP = 6
TRACES = 65536
INLINES = 256
CROSSLINES = 192
N_INL = 16
N_XL = 8


def plant(result, key, smallest, top_value):
    place = [jax.random.randint(jax.random.fold_in(key, axis), (), 0, length) for axis, length in enumerate(result.shape)]
    longest = result.shape.index(max(result.shape))
    beside = place[:longest] + [(place[longest] + 1) % result.shape[longest]] + place[longest + 1:]
    return result.at[tuple(place)].set(smallest).at[tuple(beside)].set(top_value)


def level_of(own_key, dims, cuts, smallest, largest):
    def one(axis_at, blocks):
        draws = jax.random.uniform(jax.random.fold_in(jax.random.fold_in(own_key, 6), axis_at), (blocks,), jnp.float32, smallest / len(cuts), largest / len(cuts))
        return jnp.repeat(jnp.exp(draws), dims[axis_at] // blocks).reshape((-1,) + (1,) * (len(dims) - axis_at - 1))

    loudness = one(*cuts[0])
    for cut in cuts[1:]:
        loudness = loudness * one(*cut)
    return loudness


def routed_block(rng, own, number, rows, amount, top, reach, lean):
    order = jax.random.permutation(rng, amount)
    packed, usual = shares(amount, rows * top, reach, lean, True), shares(amount, rows * top, reach, lean, False)
    places = jnp.arange(amount)

    def named(sizes, offset_by):
        used = int((sizes > 0).sum())
        fixed = max(1, used // 4)
        shifted = fixed + (places - fixed + offset_by * (used - fixed)) % max(1, amount - fixed)
        return jnp.zeros((amount,), jnp.int32).at[order[jnp.where(places < fixed, places, shifted)]].set(jnp.asarray(sizes, jnp.int32))

    sizes = jnp.where(number % 4 == 0, named(packed, number // 4), named(usual, number - number // 4 - 1))
    mixed = jax.random.permutation(jax.random.fold_in(own, 3), amount)
    giver, taker = mixed[0:amount // 2 * 2:2], mixed[1:amount // 2 * 2:2]
    room = jnp.minimum(sizes[giver] - 1, reach - sizes[taker]) // 2
    room = jnp.where((giver == order[0]) | (taker == order[0]) | (sizes[taker] == 0), 0, jnp.maximum(room, 0))
    shifted = jax.random.randint(jax.random.fold_in(own, 4), (amount // 2,), 0, 1 << 20) % (room + 1)
    sizes = sizes.at[giver].add(-shifted).at[taker].add(shifted)
    labels = jnp.searchsorted(jnp.cumsum(sizes), jnp.arange(rows * top), side="right").astype(jnp.int32)
    listing = labels.reshape(top, rows).T
    listing = listing[jax.random.permutation(jax.random.fold_in(own, 1), rows)]
    offset_by = jax.random.randint(jax.random.fold_in(own, 2), (rows, 1), 0, top)
    return jnp.take_along_axis(listing, (jnp.arange(top)[None, :] + offset_by) % top, axis=1)


def shares(count, total, reach, skew, full):
    loads = [(1 << 20) // math.isqrt(rank ** skew) + 1 for rank in range(1, count + 1)]
    largest = reach if full else min(reach, max(-(-total // count), total * loads[0] // sum(loads)))
    least = 1 if total - largest >= count - 1 else 0
    given, spare = [largest] + [least] * (count - 1), total - largest - least * (count - 1)
    while spare > 0:
        movable = [i for i in range(1, count) if given[i] < largest] or [i for i in range(1, count) if given[i] < reach]
        pool, budget = sum([loads[i] for i in movable]), spare
        for i in movable:
            more = min(reach - given[i], max(1, budget * loads[i] // pool), spare)
            given[i] = given[i] + more
            spare = spare - more
    return np.array(given)


def noise(rng, dims, deviation, bound, shards=(), dtype=jnp.bfloat16):
    drawn = jax.random.normal(rng, dims, jnp.float32) * deviation
    if len(shards) > 0:
        drawn = level_of(rng, dims, shards, -0.22, 0.18) * drawn
    return jnp.clip(drawn, min=-bound, max=bound).astype(dtype)


def setup_inputs(seed: int = 0) -> dict:
    key_list = jax.random.split(jax.random.key(seed), 6)
    traces = noise(key_list[0], (TRACES, NT), 1.0, 6.0, ((0, 128),))
    dest_tile_keys = jax.random.split(jax.random.fold_in(key_list[1], 1), TRACES // TR_DEV)
    dest_tile_turns = jax.random.permutation(jax.random.fold_in(key_list[1], 3), TRACES // TR_DEV)
    dest_tile = jax.vmap(lambda own, number: routed_block(jax.random.fold_in(key_list[1], 2), own, number, TR_DEV, N_INL * N_XL, 1, CAP, 2))(dest_tile_keys, dest_tile_turns).reshape((TRACES, 1))
    bin_in_tile = plant(jax.random.randint(key_list[2], (TRACES,), 0, IC * XC), jax.random.fold_in(key_list[2], 1), 0, (IC * XC) - 1).astype(jnp.int32)
    fold = plant(jax.random.randint(key_list[3], (INLINES, CROSSLINES), 1, 9), jax.random.fold_in(key_list[3], 1), 1, 8).astype(jnp.int32)
    thresholds = jnp.clip(jnp.exp(jax.random.uniform(key_list[4], (LEVELS, BANDS), jnp.float32, math.log(0.05), math.log(0.8))), 0.05, 0.8)
    return dict(traces=traces, dest_tile=dest_tile, bin_in_tile=bin_in_tile, fold=fold, thresholds=thresholds)


low_taps = [0.0352262918857095, -0.0854412738820267, -0.1350110200102546, 0.4598775021184914, 0.8068915093110924, 0.3326705529500826]
high_taps = [(-1) ** offset * low_taps[5 - offset] for offset in range(6)]

def analyse(extended, dimension):
    half_len = (extended.shape[dimension] - 4) // 2
    low_sum = None
    high_sum = None
    for offset in range(6):
        portion = lax.slice_in_dim(extended, offset, offset + 2 * half_len - 1, 2, dimension)
        if low_sum is None:
            low_sum = low_taps[offset] * portion
            high_sum = high_taps[offset] * portion
        else:
            low_sum = low_sum + low_taps[offset] * portion
            high_sum = high_sum + high_taps[offset] * portion
    return jnp.stack([low_sum, high_sum], 0)

def synthesise(low_ext, high_ext, dimension):
    half_len = low_ext.shape[dimension] - 2
    parts = []
    for phase in range(2):
        total = None
        for shift_at in range(3):
            low_part = lax.slice_in_dim(low_ext, 2 - shift_at, 2 - shift_at + half_len, 1, dimension)
            high_part = lax.slice_in_dim(high_ext, 2 - shift_at, 2 - shift_at + half_len, 1, dimension)
            term = low_taps[2 * shift_at + phase] * low_part + high_taps[2 * shift_at + phase] * high_part
            total = term if total is None else total + term
        parts.append(total)
    stacked = jnp.stack(parts, dimension + 1)
    shape_now = list(parts[0].shape)
    shape_now[dimension] = 2 * half_len
    return stacked.reshape(shape_now)

def right_wrap(values, dimension, margin):
    return jnp.concatenate([values, lax.slice_in_dim(values, 0, margin, 1, dimension)], dimension)

def left_wrap(values, dimension, margin):
    length_now = values.shape[dimension]
    return jnp.concatenate([lax.slice_in_dim(values, length_now - margin, length_now, 1, dimension), values], dimension)

def shrink(bands, limits):
    limit_table = jnp.concatenate([jnp.zeros((1,), jnp.float32), limits]).reshape(2, 2, 2, 1, 1, 1)
    return bands - jnp.clip(bands, -limit_table, limit_table)

def reference(traces, dest_tile, bin_in_tile, fold, thresholds):
    target = dest_tile[:, 0]
    inline_bin = target // N_XL * IC + bin_in_tile // XC
    cross_bin = target % N_XL * XC + bin_in_tile % XC
    global_bin = (inline_bin * CROSSLINES + cross_bin).astype(jnp.int32)
    summed = jax.ops.segment_sum(traces.astype(jnp.float32), global_bin, num_segments=INLINES * CROSSLINES)
    scale_root = jnp.sqrt(fold.astype(jnp.float32))[:, :, None]
    coarse = summed.reshape(INLINES, CROSSLINES, NT) / scale_root
    shrunk = []
    for octave in range(LEVELS):
        timed = analyse(right_wrap(coarse, 2, 4), 2)
        inlined = analyse(right_wrap(timed, 1, 4), 1)
        bands = analyse(right_wrap(inlined, 3, 4), 3)
        shrunk.append(shrink(bands, thresholds[octave]))
        coarse = bands[0, 0, 0]
    for octave in reversed(range(LEVELS)):
        bands = shrunk[octave].at[0, 0, 0].set(coarse)
        crossed_ext = left_wrap(bands, 4, 2)
        crossed = synthesise(crossed_ext[0], crossed_ext[1], 3)
        inlined_ext = left_wrap(crossed, 2, 2)
        timed = synthesise(inlined_ext[0], inlined_ext[1], 1)
        timed_ext = left_wrap(timed, 3, 2)
        coarse = synthesise(timed_ext[0], timed_ext[1], 2)
    return coarse / scale_root
```

```python
import functools

import jax
import jax.numpy as jnp
import ml_dtypes
import numpy as np
from jax import lax
from jax.experimental import pallas as pl
from jax.experimental.pallas import tpu as pltpu
from jax.sharding import PartitionSpec as P

LEVELS = 3
SLOTS = 6
GROUP = 8
LANES = 128
BLOCK = 256

low_taps = [
    0.0352262918857095,
    -0.0854412738820267,
    -0.1350110200102546,
    0.4598775021184914,
    0.8068915093110924,
    0.3326705529500826,
]
high_taps = [(-1) ** offset * low_taps[5 - offset] for offset in range(6)]

bf16 = jnp.bfloat16
f32 = jnp.float32


def halves(matrix):
    top = np.asarray(matrix, np.float32).astype(ml_dtypes.bfloat16)
    rest = (np.asarray(matrix, np.float64) - top.astype(np.float64)).astype(ml_dtypes.bfloat16)
    return top, rest


def triple(matrix, axis):
    top, rest = halves(matrix)
    return np.concatenate([top, top, rest], axis)


def line_parts(length):
    half = length // 2
    whole = np.zeros((length, length + 4))
    for m in range(half):
        for k in range(6):
            whole[m, 2 * m + k] = low_taps[k]
            whole[half + m, 2 * m + k] = high_taps[k]
    left, sizes, right = np.linalg.svd(whole[:, length:])
    assert sizes[2] < 1e-9
    state = np.zeros((2, length))
    state[:, :4] = right[:2]
    return whole[:, :length], left[:, :2] * sizes[:2], state


def tile_parts(rows, cols):
    own_i, edge_i, state_i = line_parts(rows)
    own_c, edge_c, state_c = line_parts(cols)
    half_r, half_c = rows // 2, cols // 2

    def outer(on_rows, on_cols, banded_rows):
        both = np.einsum("ar,bc->abrc", on_rows, on_cols)
        a, b, r, c = both.shape
        if banded_rows:
            both = both.reshape(2, half_r, 2, half_c, r, c).transpose(2, 0, 1, 3, 4, 5)
        return both.reshape(a * b, r * c)

    own = outer(own_i, own_c, True)
    edges = [outer(edge_i, own_c, True), outer(own_i, edge_c, True), outer(edge_i, edge_c, True)]
    states = [
        outer(state_i, np.eye(cols), False),
        outer(np.eye(rows), state_c, False),
        outer(state_i, state_c, False),
    ]
    sizes = [-(-e.shape[1] // 8) * 8 for e in edges]
    if sum(sizes) % 16:
        sizes[2] += 8
    edges = [np.pad(e, ((0, 0), (0, s - e.shape[1]))) for e, s in zip(edges, sizes)]
    states = [np.pad(v, ((0, s - v.shape[0]), (0, 0))) for v, s in zip(states, sizes)]
    return own, np.concatenate(edges, 1), np.concatenate(states, 0), sizes


def time_parts():
    whole = np.zeros((BLOCK + LANES, BLOCK))
    for m in range(LANES):
        for k in range(6):
            whole[2 * m + k, m] = low_taps[k]
            whole[2 * m + k, LANES + m] = high_taps[k]
    return whole[:BLOCK], whole[BLOCK:]


def split(value):
    top = value.astype(bf16)
    return top, (value - top.astype(f32)).astype(bf16)


def dot(left, right):
    return jnp.dot(left, right, preferred_element_type=f32)


def left_dot(matrix, value):
    top, rest = split(value)
    return dot(matrix, jnp.concatenate([top, rest, top], 0))


def time_analysis(blocks, matrix):
    parts = [split(block) for block in blocks]
    lows, highs = [], []
    for b in range(len(blocks)):
        top, rest = parts[b]
        next_top, next_rest = [part[:, :LANES] for part in parts[(b + 1) % len(blocks)]]
        joined = jnp.concatenate([top, rest, top, next_top, next_rest, next_top], 1)
        result = dot(joined, matrix)
        lows.append(result[:, :LANES])
        highs.append(result[:, LANES:])
    return lows, highs


def time_synthesis(blocks, matrix):
    parts = [split(block) for block in blocks]
    results = []
    for b in range(len(blocks)):
        top, rest = parts[b]
        last_top, last_rest = parts[b - 1]
        joined = jnp.concatenate([top, rest, top, last_top, last_rest, last_top], 1)
        results.append(dot(joined, matrix))
    return results


def shrink(value, limit):
    return value - jnp.clip(value, -limit, limit)


def route_kernel(dest_ref, bin_ref, traces_ref, out_ref):
    traces = traces_ref.shape[0]
    tiles = out_ref.shape[0] // GROUP
    rows = out_ref.shape[0]
    dest = dest_ref[...]
    matches = lax.broadcasted_iota(jnp.int32, (tiles, traces), 0) == dest
    before = lax.broadcasted_iota(jnp.int32, (traces, traces), 0) <= lax.broadcasted_iota(
        jnp.int32, (traces, traces), 1
    )
    counts = dot(matches.astype(f32).astype(bf16), before.astype(f32).astype(bf16))
    place = jnp.sum(jnp.where(matches, counts, 0.0), 0, keepdims=True).astype(jnp.int32) - 1
    row_at = lax.broadcasted_iota(jnp.int32, (rows, traces), 0)
    main = (row_at == dest * GROUP + place).astype(f32).astype(bf16)
    span = out_ref.shape[1] // 3 // LANES * LANES
    samples = traces_ref.shape[1]
    tail = traces_ref[:, 3 * span : samples]
    for j in range(3):
        tail_row = jnp.where(place == j, SLOTS, jnp.where(place == 3 + j, SLOTS + 1, -rows * GROUP))
        extra = (row_at == dest * GROUP + tail_row).astype(f32).astype(bf16)
        at = slice(j * span, (j + 1) * span)
        out_ref[:, at] = (dot(main, traces_ref[:, at]) + dot(extra, tail)).astype(bf16)
    code = bin_ref[...] + 1
    lane = lax.broadcasted_iota(jnp.int32, (LANES, traces), 0)
    digits = jnp.where(lane == 0, code // 2, jnp.where(lane == 1, code % 2, 0))
    labels = lax.dot_general(
        main,
        digits.astype(f32).astype(bf16),
        (((1,), (1,)), ((), ())),
        preferred_element_type=f32,
    )
    out_ref[:, 3 * span :] = labels.astype(bf16)


def bin_kernel(arrived_ref, scale_ref, time_ref, state_ref, timed_ref, *state_outs):
    rows = arrived_ref.shape[0]
    bins, samples = timed_ref.shape
    span = samples // 4
    labels = arrived_ref[:, 3 * span :]
    lane = lax.broadcasted_iota(jnp.int32, (GROUP, LANES), 1)
    weights = jnp.where(lane == 0, 2.0, jnp.where(lane == 1, 1.0, 0.0)).astype(bf16)
    code = lax.dot_general(
        weights, labels, (((1,), (1,)), ((), ())), preferred_element_type=f32
    ).astype(jnp.int32)
    at = lax.broadcasted_iota(jnp.int32, (GROUP, rows), 1) % GROUP
    code = jnp.where(at < SLOTS, code, 0) - 1
    bin_at = lax.broadcasted_iota(jnp.int32, (bins, rows), 0)
    main = (bin_at == code[:1]).astype(f32).astype(bf16)
    scale = scale_ref[...]
    pieces = [dot(main, arrived_ref[:, j * span : (j + 1) * span]) for j in range(3)]
    last = None
    for j in range(3):
        first = pltpu.roll(code, SLOTS - j, 1)
        second = pltpu.roll(code, SLOTS + 1 - 3 - j, 1)
        tail_code = jnp.where(at == SLOTS, first, jnp.where(at == SLOTS + 1, second, -1))
        onehot = (bin_at == tail_code[:1]).astype(f32).astype(bf16)
        term = dot(onehot, arrived_ref[:, j * span : (j + 1) * span])
        last = term if last is None else last + term
    pieces.append(last)
    blocks = []
    for piece in pieces:
        piece = piece * scale
        blocks += [piece[:, b : b + BLOCK] for b in range(0, span, BLOCK)]
    lows, highs = time_analysis(blocks, time_ref[...])
    half = samples // 2
    for b in range(len(blocks)):
        for base, piece in ((0, lows[b]), (half, highs[b])):
            where = slice(base + b * LANES, base + (b + 1) * LANES)
            timed_ref[:, where] = piece
    put_states(timed_ref, state_ref, state_outs, BLOCK)


def put_states(value_ref, state_ref, state_outs, step):
    matrix = state_ref[...]
    for start in range(0, value_ref.shape[1], step):
        where = slice(start, start + step)
        result = left_dot(matrix, value_ref[:, where])
        top = 0
        for out in state_outs:
            out[:, where] = result[top : top + out.shape[0]]
            top += out.shape[0]


def own_kernel(timed_ref, own_ref, bands_ref):
    matrix = own_ref[...]
    for start in range(0, timed_ref.shape[1], BLOCK):
        where = slice(start, start + BLOCK)
        bands_ref[:, where] = left_dot(matrix, timed_ref[:, where])


def forward_kernel(level, thr_ref, bands_in, edge_ref, s0, s1, s2, time_ref, state_ref, *outs):
    shrunk_ref, timed_ref = outs[0], outs[1]
    state_outs = outs[2:]
    quarter = bands_in.shape[0] // 4
    half = bands_in.shape[1] // 2
    matrix = edge_ref[...]
    coarse = []
    for start in range(0, 2 * half, BLOCK):
        where = slice(start, start + BLOCK)
        states = jnp.concatenate([s0[:, where], s1[:, where], s2[:, where]], 0)
        bands = bands_in[:, where] + left_dot(matrix, states)
        high = start >= half
        for q in range(4):
            piece = bands[q * quarter : (q + 1) * quarter]
            if q or high:
                piece = shrink(piece, thr_ref[level, 2 * q + int(high) - 1])
            else:
                coarse.append(piece)
            shrunk_ref[q * quarter : (q + 1) * quarter, where] = piece
    lows, highs = time_analysis(coarse, time_ref[...])
    for b in range(len(coarse)):
        for base, piece in ((0, lows[b]), (half // 2, highs[b])):
            timed_ref[:, base + b * LANES : base + (b + 1) * LANES] = piece
    put_states(timed_ref, state_ref, state_outs, BLOCK)


def last_kernel(level, thr_ref, timed_ref, own_ref, edge_ref, s0, s1, s2, back_ref, shrunk_ref, *state_outs):
    quarter = timed_ref.shape[0] // 4
    half = timed_ref.shape[1] // 2
    for start in range(0, 2 * half, BLOCK):
        where = slice(start, start + BLOCK)
        states = jnp.concatenate([s0[:, where], s1[:, where], s2[:, where]], 0)
        bands = left_dot(own_ref[...], timed_ref[:, where]) + left_dot(edge_ref[...], states)
        high = start >= half
        row = lax.broadcasted_iota(jnp.int32, bands.shape, 0)
        limit = jnp.full(bands.shape, thr_ref[level, 0] if high else 0.0, f32)
        for q in range(1, 4):
            limit = jnp.where(row >= q * quarter, thr_ref[level, 2 * q + int(high) - 1], limit)
        shrunk_ref[:, where] = shrink(bands, limit)
    put_states(shrunk_ref, back_ref, state_outs, BLOCK)


def own_forward_kernel(level, thr_ref, timed_in, own_ref, edge_ref, s0, s1, s2, time_ref, state_ref, *outs):
    own_bands = outs[-1]
    own_kernel(timed_in, own_ref, own_bands)
    forward_kernel(level, thr_ref, own_bands, edge_ref, s0, s1, s2, time_ref, state_ref, *outs[:-1])


def rebuilt_blocks(shrunk, own_t, state_t, s0, s1, s2, time_t):
    half = shrunk.shape[1] // 2
    blocks = []
    for start in range(0, half, LANES):
        pair = []
        for base in (0, half):
            where = slice(base + start, base + start + LANES)
            pair.append((shrunk[:, where], jnp.concatenate([s0[:, where], s1[:, where], s2[:, where]], 0)))
        bands = jnp.concatenate([pair[0][0], pair[1][0]], 1)
        states = jnp.concatenate([pair[0][1], pair[1][1]], 1)
        blocks.append(left_dot(own_t[...], bands) + left_dot(state_t[...], states))
    return time_synthesis(blocks, time_t[...])


def inverse_kernel(shrunk, own_t, state_t, s0, s1, s2, time_t, above_in, back_ref, above_out, *state_outs):
    blocks = rebuilt_blocks(shrunk, own_t, state_t, s0, s1, s2, time_t)
    rows = blocks[0].shape[0]
    half = above_in.shape[1] // 2
    above_out[rows:, :] = above_in[rows:, :]
    above_out[:rows, half:] = above_in[:rows, half:]
    for b, block in enumerate(blocks):
        above_out[:rows, b * BLOCK : (b + 1) * BLOCK] = block
    put_states(above_out, back_ref, state_outs, BLOCK)


def final_kernel(shrunk, own_t, state_t, s0, s1, s2, time_t, scale_ref, out_ref):
    blocks = rebuilt_blocks(shrunk, own_t, state_t, s0, s1, s2, time_t)
    scale = scale_ref[...]
    for b, block in enumerate(blocks):
        out_ref[:, b * BLOCK : (b + 1) * BLOCK] = block * scale


def call(kernel, outs, *args, smem=(), scratch=(), aliases=None):
    in_specs = [
        pl.BlockSpec(memory_space=pltpu.SMEM if i in smem else pltpu.VMEM) for i in range(len(args))
    ]
    return pl.pallas_call(
        kernel,
        out_shape=[jax.ShapeDtypeStruct(shape, dtype) for shape, dtype in outs],
        in_specs=in_specs,
        out_specs=[pl.BlockSpec(memory_space=pltpu.VMEM)] * len(outs),
        scratch_shapes=list(scratch),
        input_output_aliases=aliases or {},
        compiler_params=pltpu.CompilerParams(vmem_limit_bytes=48 * 1024 * 1024),
    )(*args)


def shift(block, inline_by, cross_by):
    inline_devs, cross_devs = lax.axis_size("inl"), lax.axis_size("xl")
    if not cross_by:
        return lax.ppermute(block, "inl", [((i + inline_by) % inline_devs, i) for i in range(inline_devs)])
    if not inline_by:
        return lax.ppermute(block, "xl", [((j + cross_by) % cross_devs, j) for j in range(cross_devs)])
    route = [
        ((i + inline_by) % inline_devs * cross_devs + (j + cross_by) % cross_devs, i * cross_devs + j)
        for i in range(inline_devs)
        for j in range(cross_devs)
    ]
    return lax.ppermute(block, ("inl", "xl"), route)


def exchange(states, ahead):
    return [shift(states[0], ahead, 0), shift(states[1], 0, ahead), shift(states[2], ahead, ahead)]


def on_device(traces, dest_tile, bin_in_tile, fold, thresholds):
    devices = lax.axis_size("inl") * lax.axis_size("xl")
    trace_count, samples = traces.shape
    tile_rows, tile_cols = fold.shape
    bins = tile_rows * tile_cols
    width = SLOTS * samples // GROUP + LANES
    (outgoing,) = call(
        route_kernel,
        [((devices * GROUP, width), bf16)],
        dest_tile.reshape(1, trace_count),
        bin_in_tile.reshape(1, trace_count),
        traces,
    )
    arrived = lax.all_to_all(
        outgoing.reshape(devices, GROUP, width), ("inl", "xl"), split_axis=0, concat_axis=0, tiled=True
    ).reshape(devices * GROUP, width)
    scale = (1.0 / jnp.sqrt(fold.astype(f32))).reshape(bins, 1)

    main, following = time_parts()
    time_matrix = np.concatenate([triple(main, 0), triple(following, 0)], 0)
    time_back = np.concatenate(
        [triple(main.T, 0), triple(np.pad(following.T, ((0, 0), (0, BLOCK - LANES))), 0)], 0
    )
    sizes, own, edge, state = [], [], [], []
    for level in range(LEVELS):
        own_l, edge_l, state_l, sizes_l = tile_parts(tile_rows >> level, tile_cols >> level)
        sizes.append(sizes_l)
        own.append(own_l)
        edge.append(edge_l)
        state.append(state_l)
    counts = [bins >> (2 * level) for level in range(LEVELS)]
    lengths = [samples >> level for level in range(LEVELS)]

    def state_shapes(level):
        return [((size, lengths[level]), f32) for size in sizes[level]]

    timed, *states = call(
        bin_kernel,
        [((bins, samples), f32)] + state_shapes(0),
        arrived,
        scale,
        time_matrix,
        triple(state[0], 1),
    )
    states = exchange(states, 1)
    (bands,) = call(own_kernel, [((bins, samples), f32)], timed, triple(own[0], 1))
    shrunk = [None] * LEVELS
    shrunk[0], timed, *states = call(
        functools.partial(forward_kernel, 0),
        [((bins, samples), f32), ((counts[1], lengths[1]), f32)] + state_shapes(1),
        thresholds,
        bands,
        triple(edge[0], 1),
        *states,
        time_matrix,
        triple(state[1], 1),
        smem=(0,),
    )
    states = exchange(states, 1)
    shrunk[1], timed, *states = call(
        functools.partial(own_forward_kernel, 1),
        [((counts[1], lengths[1]), f32), ((counts[2], lengths[2]), f32)] + state_shapes(2),
        thresholds,
        timed,
        triple(own[1], 1),
        triple(edge[1], 1),
        *states,
        time_matrix,
        triple(state[2], 1),
        smem=(0,),
        scratch=[pltpu.VMEM((counts[1], lengths[1]), f32)],
    )
    states = exchange(states, 1)
    shrunk[2], *states = call(
        functools.partial(last_kernel, 2),
        [((counts[2], lengths[2]), f32)] + state_shapes(2),
        thresholds,
        timed,
        triple(own[2], 1),
        triple(edge[2], 1),
        *states,
        triple(edge[2].T, 1),
        smem=(0,),
    )
    states = exchange(states, -1)
    for level in (2, 1):
        shrunk[level - 1], *states = call(
            inverse_kernel,
            [((counts[level - 1], lengths[level - 1]), f32)] + state_shapes(level - 1),
            shrunk[level],
            triple(own[level].T, 1),
            triple(state[level].T, 1),
            *states,
            time_back,
            shrunk[level - 1],
            triple(edge[level - 1].T, 1),
        )
        states = exchange(states, -1)
    (denoised,) = call(
        final_kernel,
        [((bins, samples), f32)],
        shrunk[0],
        triple(own[0].T, 1),
        triple(state[0].T, 1),
        *states,
        time_back,
        scale,
    )
    return denoised.reshape(tile_rows, tile_cols, samples)


def solution(mesh):
    placed = (P(("inl", "xl"), None), P(("inl", "xl"), None), P(("inl", "xl")), P("inl", "xl"), P())
    return jax.shard_map(
        on_device, mesh=mesh, in_specs=placed, out_specs=P("inl", "xl", None), check_vma=False
    )
```

```python
import functools

import jax
import jax.numpy as jnp
import ml_dtypes
import numpy as np
from jax import lax
from jax.experimental import pallas as pl
from jax.experimental.pallas import tpu as pltpu
from jax.sharding import PartitionSpec as P

LEVELS = 3
SLOTS = 6
GROUP = 8
LANES = 128
BLOCK = 256
VMEM_LIMIT = 32 * 1024 * 1024

low_taps = [
    0.0352262918857095,
    -0.0854412738820267,
    -0.1350110200102546,
    0.4598775021184914,
    0.8068915093110924,
    0.3326705529500826,
]
high_taps = [(-1) ** offset * low_taps[5 - offset] for offset in range(6)]

bf16 = jnp.bfloat16
f32 = jnp.float32


def halves(matrix):
    top = np.asarray(matrix, np.float32).astype(ml_dtypes.bfloat16)
    rest = (np.asarray(matrix, np.float64) - top.astype(np.float64)).astype(ml_dtypes.bfloat16)
    return top, rest


def triple(matrix, axis):
    top, rest = halves(matrix)
    return np.concatenate([top, top, rest], axis)


def line_parts(length):
    half = length // 2
    whole = np.zeros((length, length + 4))
    for m in range(half):
        for k in range(6):
            whole[m, 2 * m + k] = low_taps[k]
            whole[half + m, 2 * m + k] = high_taps[k]
    left, sizes, right = np.linalg.svd(whole[:, length:])
    assert sizes[2] < 1e-9
    state = np.zeros((2, length))
    state[:, :4] = right[:2]
    return whole[:, :length], left[:, :2] * sizes[:2], state


def outer(on_rows, on_cols, banded):
    both = np.einsum("ar,bc->abrc", on_rows, on_cols)
    a, b, r, c = both.shape
    if banded:
        both = both.reshape(2, a // 2, 2, b // 2, r, c).transpose(2, 0, 1, 3, 4, 5)
    return both.reshape(a * b, r * c)


def two_levels(length):
    own0, edge0, state0 = line_parts(length)
    own1, edge1, state1 = line_parts(length // 2)
    low = slice(0, length // 2)
    assert np.abs(state1 @ edge0[low]).max() < 1e-9
    further = state1 @ own0[low]
    return dict(
        own0=own0,
        edge0=edge0,
        state0=state0,
        own1=own1 @ own0[low],
        far1=own1 @ edge0[low],
        edge1=edge1,
        further=further,
        states=np.concatenate([state0, further]),
    )


def joint_matrices(rows, cols):
    i, c = two_levels(rows), two_levels(cols)
    wide = [np.concatenate([d["edge0"], np.zeros_like(d["edge0"])], 1) for d in (i, c)]
    both = [np.concatenate([d["far1"], d["edge1"]], 1) for d in (i, c)]
    own0 = outer(i["own0"], c["own0"], True)
    edge0 = [outer(i["edge0"], c["own0"], True), outer(i["own0"], c["edge0"], True), outer(*wide, True)]
    own1 = outer(i["own1"], c["own1"], True)
    edge1 = [
        outer(i["far1"], c["own1"], True),
        outer(i["own1"], c["far1"], True),
        outer(*both, True),
        outer(i["edge1"], np.eye(cols // 2), True),
        outer(np.eye(rows // 2), c["edge1"], True),
    ]
    states = [
        outer(i["state0"], np.eye(cols), False),
        outer(np.eye(rows), c["state0"], False),
        outer(i["states"], c["states"], False),
        outer(i["further"], c["own1"], False),
        outer(i["own1"], c["further"], False),
    ]
    sizes = [len(part) for part in states]
    return own0, np.concatenate(edge0, 1), own1, np.concatenate(edge1, 1), np.concatenate(states, 0), sizes


def tile_parts(rows, cols):
    own_i, edge_i, state_i = line_parts(rows)
    own_c, edge_c, state_c = line_parts(cols)
    own = outer(own_i, own_c, True)
    edges = [outer(edge_i, own_c, True), outer(own_i, edge_c, True), outer(edge_i, edge_c, True)]
    states = [
        outer(state_i, np.eye(cols), False),
        outer(np.eye(rows), state_c, False),
        outer(state_i, state_c, False),
    ]
    sizes = [-(-e.shape[1] // 8) * 8 for e in edges]
    if sum(sizes) % 16:
        sizes[2] += 8
    edges = [np.pad(e, ((0, 0), (0, s - e.shape[1]))) for e, s in zip(edges, sizes)]
    states = [np.pad(v, ((0, s - v.shape[0]), (0, 0))) for v, s in zip(states, sizes)]
    return own, np.concatenate(edges, 1), np.concatenate(states, 0), sizes


def time_parts():
    whole = np.zeros((BLOCK + LANES, BLOCK))
    for m in range(LANES):
        for k in range(6):
            whole[2 * m + k, m] = low_taps[k]
            whole[2 * m + k, LANES + m] = high_taps[k]
    return whole[:BLOCK], whole[BLOCK:]


def split(value):
    top = value.astype(bf16)
    return top, (value - top.astype(f32)).astype(bf16)


def dot(left, right):
    return jnp.dot(left, right, preferred_element_type=f32)


def left_dot(matrix, value):
    top, rest = split(value)
    return dot(matrix, jnp.concatenate([top, rest, top], 0))


def time_analysis(blocks, matrix):
    parts = [split(block) for block in blocks]
    lows, highs = [], []
    for b in range(len(blocks)):
        top, rest = parts[b]
        next_top, next_rest = [part[:, :LANES] for part in parts[(b + 1) % len(blocks)]]
        joined = jnp.concatenate([top, rest, top, next_top, next_rest, next_top], 1)
        result = dot(joined, matrix)
        lows.append(result[:, :LANES])
        highs.append(result[:, LANES:])
    return lows, highs


def time_synthesis(blocks, matrix):
    parts = [split(block) for block in blocks]
    results = []
    for b in range(len(blocks)):
        top, rest = parts[b]
        last_top, last_rest = parts[b - 1]
        joined = jnp.concatenate([top, rest, top, last_top, last_rest, last_top], 1)
        results.append(dot(joined, matrix))
    return results


def synthesis_from_low(lows, matrix):
    parts = [split(low) for low in lows]
    results = []
    for b in range(len(lows)):
        top, rest = parts[b]
        last_top, last_rest = parts[b - 1]
        joined = jnp.concatenate([top, rest, top, last_top, last_rest, last_top], 1)
        results.append(dot(joined, matrix))
    return results


def shrink(value, limit):
    return value - jnp.clip(value, -limit, limit)


def route_kernel(dest_far, bin_far, traces_far, out_far, dest_ref, bin_ref, traces_ref, out_ref, in_sems, out_sems):
    traces, samples = traces_ref.shape
    rows = out_ref.shape[0]
    tiles = rows // GROUP
    span = samples // 4
    coming = [
        pltpu.make_async_copy(dest_far, dest_ref, in_sems.at[4]),
        pltpu.make_async_copy(bin_far, bin_ref, in_sems.at[5]),
    ]
    for j in (3, 0, 1, 2):
        at = pl.ds(j * span, span)
        coming.append(pltpu.make_async_copy(traces_far.at[:, at], traces_ref.at[:, at], in_sems.at[j]))
    for copy in coming:
        copy.start()
    before = lax.broadcasted_iota(jnp.int32, (traces, traces), 0) <= lax.broadcasted_iota(
        jnp.int32, (traces, traces), 1
    )
    before = before.astype(f32).astype(bf16)
    coming[0].wait()
    coming[1].wait()
    dest = dest_ref[...]
    matches = lax.broadcasted_iota(jnp.int32, (tiles, traces), 0) == dest
    counts = dot(matches.astype(f32).astype(bf16), before)
    place = jnp.sum(jnp.where(matches, counts, 0.0), 0, keepdims=True).astype(jnp.int32) - 1
    row_at = lax.broadcasted_iota(jnp.int32, (rows, traces), 0)
    main = (row_at == dest * GROUP + place).astype(f32).astype(bf16)
    going = []

    def send(number, first, width):
        at = pl.ds(first, width)
        going.append(pltpu.make_async_copy(out_ref.at[:, at], out_far.at[:, at], out_sems.at[number]))
        going[-1].start()

    code = bin_ref[...] + 1
    lane = lax.broadcasted_iota(jnp.int32, (LANES, traces), 0)
    digits = jnp.where(lane == 0, code // 2, jnp.where(lane == 1, code % 2, 0))
    labels = lax.dot_general(
        main,
        digits.astype(f32).astype(bf16),
        (((1,), (1,)), ((), ())),
        preferred_element_type=f32,
    )
    out_ref[:, 3 * span :] = labels.astype(bf16)
    send(3, 3 * span, LANES)
    coming[2].wait()
    tail = traces_ref[:, 3 * span : samples]
    for j in range(3):
        tail_row = jnp.where(place == j, SLOTS, jnp.where(place == 3 + j, SLOTS + 1, -rows * GROUP))
        extra = (row_at == dest * GROUP + tail_row).astype(f32).astype(bf16)
        at = slice(j * span, (j + 1) * span)
        coming[3 + j].wait()
        out_ref[:, at] = (dot(main, traces_ref[:, at]) + dot(extra, tail)).astype(bf16)
        send(j, j * span, span)
    for copy in going:
        copy.wait()


def bin_kernel(
    arrived_far, scale_ref, time_far, state_far, summed_ref, s0, s1, s2, arrived_ref, time_ref, state_ref, sems
):
    outs = (s0, s1, s2)
    width = summed_ref.shape[1] // 4
    coming = []
    for j, (first, size) in enumerate([(3 * width, LANES)] + [(j * width, width) for j in range(3)]):
        at = pl.ds(first, size)
        coming.append(pltpu.make_async_copy(arrived_far.at[:, at], arrived_ref.at[:, at], sems.at[j]))
    coming.append(pltpu.make_async_copy(state_far, state_ref, sems.at[4]))
    coming.append(pltpu.make_async_copy(time_far, time_ref, sems.at[5]))
    for copy in coming:
        copy.start()
    coming[0].wait()
    rows = arrived_ref.shape[0]
    bins, samples = summed_ref.shape
    span = samples // 4
    labels = arrived_ref[:, 3 * span :]
    lane = lax.broadcasted_iota(jnp.int32, (GROUP, LANES), 1)
    weights = jnp.where(lane == 0, 2.0, jnp.where(lane == 1, 1.0, 0.0)).astype(bf16)
    code = lax.dot_general(
        weights, labels, (((1,), (1,)), ((), ())), preferred_element_type=f32
    ).astype(jnp.int32)
    at = lax.broadcasted_iota(jnp.int32, (GROUP, rows), 1) % GROUP
    code = jnp.where(at < SLOTS, code, 0) - 1
    bin_at = lax.broadcasted_iota(jnp.int32, (bins, rows), 0)
    main = (bin_at == code[:1]).astype(f32).astype(bf16)
    scale = scale_ref[...]
    pieces = []
    for j in range(3):
        coming[1 + j].wait()
        pieces.append(dot(main, arrived_ref[:, j * span : (j + 1) * span]))
    last = None
    for j in range(3):
        first = pltpu.roll(code, SLOTS - j, 1)
        second = pltpu.roll(code, SLOTS + 1 - 3 - j, 1)
        tail_code = jnp.where(at == SLOTS, first, jnp.where(at == SLOTS + 1, second, -1))
        onehot = (bin_at == tail_code[:1]).astype(f32).astype(bf16)
        term = dot(onehot, arrived_ref[:, j * span : (j + 1) * span])
        last = term if last is None else last + term
    pieces.append(last)
    coming[4].wait()
    coming[5].wait()
    matrix = state_ref[...]
    blocks = []
    for p, piece in enumerate(pieces):
        piece = piece * scale
        summed_ref[:, p * span : (p + 1) * span] = piece
        states = left_dot(matrix, piece)
        blocks += [states[:, b : b + BLOCK] for b in range(0, span, BLOCK)]
    lows, highs = time_analysis(blocks, time_ref[...])
    for b in range(len(blocks)):
        put_joint(outs, slice(b * LANES, (b + 1) * LANES), lows[b], highs[b])


def put_joint(outs, where, low, high):
    rows, cols, corner = [out.shape[0] for out in outs]
    ends = [0]
    for size in (rows * 2 // 5, cols * 2 // 5, corner // 2, rows // 5, cols // 5):
        ends.append(ends[-1] + size)
    part = [slice(ends[k], ends[k + 1]) for k in range(5)]
    put_rows([outs[0]], where, jnp.concatenate([low[part[0]], high[part[0]], low[part[3]]], 0))
    put_rows([outs[1]], where, jnp.concatenate([low[part[1]], high[part[1]], low[part[4]]], 0))
    put_rows([outs[2]], where, jnp.concatenate([low[part[2]], high[part[2]]], 0))


def take_joint(refs, where):
    rows, cols, corner = [ref.shape[0] for ref in refs]
    r, c, d = rows * 2 // 5, cols * 2 // 5, corner // 2
    m0, m1, m2 = [ref[:, where] for ref in refs]
    low = jnp.concatenate([m0[:r], m1[:c], m2[:d], m0[2 * r :], m1[2 * c :]], 0)
    high = jnp.concatenate([m0[r : 2 * r], m1[c : 2 * c], m2[d:]], 0)
    return low, high


def put_rows(outs, where, value):
    top = 0
    for out in outs:
        out[:, where] = value[top : top + out.shape[0]]
        top += out.shape[0]


def join_rows(refs, where):
    return jnp.concatenate([ref[:, where] for ref in refs], 0)


def put_states(value_ref, state_ref, state_outs, step):
    matrix = state_ref[...]
    for start in range(0, value_ref.shape[1], step):
        where = slice(start, start + step)
        result = left_dot(matrix, value_ref[:, where])
        put_rows(state_outs, where, result)


def steps(ref):
    return [slice(start, start + BLOCK) for start in range(0, ref.shape[1], BLOCK)]


def own_kernel(summed_ref, time_ref, own_ref, next_ref, low_ref, high_ref, next_out):
    blocks = [summed_ref[:, where] for where in steps(summed_ref)]
    lows, highs = time_analysis(blocks, time_ref[...])
    for b in range(0, len(blocks), 2):
        where = slice(b * LANES, (b + 2) * LANES)
        low = jnp.concatenate([lows[b], lows[b + 1]], 1)
        next_out[:, where] = left_dot(next_ref[...], low)
        low_ref[:, where] = left_dot(own_ref[...], low)
        high_ref[:, where] = left_dot(own_ref[...], jnp.concatenate([highs[b], highs[b + 1]], 1))


def middle_kernel(thr_ref, own_ref, edge_ref, s0, s1, s2, time_ref, state_ref, shrunk_ref, timed_ref, *state_outs):
    quarter = shrunk_ref.shape[0] // 4
    half = shrunk_ref.shape[1] // 2
    matrix = edge_ref[...]
    blocks = []
    for where in steps(own_ref):
        low, _ = take_joint((s0, s1, s2), where)
        blocks.append(own_ref[:, where] + left_dot(matrix, low))
    lows, highs = time_analysis(blocks, time_ref[...])
    for b in range(len(blocks)):
        for base, piece, high in ((0, lows[b], 0), (half, highs[b], 1)):
            where = slice(base + b * LANES, base + (b + 1) * LANES)
            for q in range(4):
                at = slice(q * quarter, (q + 1) * quarter)
                if q or high:
                    shrunk_ref[at, where] = shrink(piece[at], thr_ref[1, 2 * q + high - 1])
                else:
                    shrunk_ref[at, where] = jnp.zeros_like(piece[at])
    coarse = [jnp.concatenate([lows[b][:quarter], lows[b + 1][:quarter]], 1) for b in range(0, len(lows), 2)]
    lows, highs = time_analysis(coarse, time_ref[...])
    for b in range(len(coarse)):
        for base, piece in ((0, lows[b]), (half // 2, highs[b])):
            timed_ref[:, base + b * LANES : base + (b + 1) * LANES] = piece
    put_states(timed_ref, state_ref, state_outs, BLOCK)


def details_kernel(thr_ref, low_in, high_in, edge_ref, s0, s1, s2, back_low, back_ref, low_out, high_out, *state_outs):
    quarter = low_in.shape[0] // 4
    for where in steps(low_in):
        low, high = take_joint((s0, s1, s2), where)
        bands = low_in[quarter:, where] + left_dot(edge_ref[quarter:], low[: high.shape[0]])
        bands = [shrink(bands[(q - 1) * quarter : q * quarter], thr_ref[0, 2 * q - 1]) for q in range(1, 4)]
        bands = jnp.concatenate(bands, 0)
        low_out[:, where] = bands
        state_outs[0][:, where] = left_dot(back_low[...], bands)
        bands = high_in[:, where] + left_dot(edge_ref[...], high)
        bands = [shrink(bands[q * quarter : (q + 1) * quarter], thr_ref[0, 2 * q]) for q in range(4)]
        bands = jnp.concatenate(bands, 0)
        high_out[:, where] = bands
        state_outs[1][:, where] = left_dot(back_ref[...], bands)


def spread_kernel(low_in, high_in, low_matrix, own_matrix, shrunk_in, time_t, low_out, high_out, next_out):
    for where in steps(low_in):
        low_out[:, where] = left_dot(low_matrix[...], low_in[:, where])
        high_out[:, where] = left_dot(own_matrix[...], high_in[:, where])
    half = shrunk_in.shape[1] // 2
    blocks = []
    for b in range(0, half, LANES):
        blocks.append(jnp.concatenate([shrunk_in[:, b : b + LANES], shrunk_in[:, half + b : half + b + LANES]], 1))
    for b, block in enumerate(time_synthesis(blocks, time_t[...])):
        next_out[:, b * BLOCK : (b + 1) * BLOCK] = block


def rejoin_kernel(
    shrunk, own_t, state_t, s0, s1, s2, time_t, time_low, next_in, low_states, high_states, back_ref, next_out, *outs
):
    coarse = rebuilt_blocks(shrunk, own_t, state_t, s0, s1, s2, time_t)
    rows = coarse[0].shape[0]
    lows = []
    for block in coarse:
        lows += [block[:, b : b + LANES] for b in range(0, BLOCK, LANES)]
    count = low_states.shape[0]
    for b, block in enumerate(synthesis_from_low(lows, time_low[...])):
        where = slice(b * BLOCK, (b + 1) * BLOCK)
        bands = jnp.concatenate([next_in[:rows, where] + block, next_in[rows:, where]], 0)
        next_out[:, where] = bands
        states = left_dot(back_ref[...], bands)
        low = jnp.concatenate([states[:count] + low_states[:, where], states[count:]], 0)
        put_joint(outs, where, low, high_states[:, where])


def own_back_kernel(low_in, high_in, next_in, next_t, time_t, out_ref):
    blocks = []
    for where in steps(low_in):
        low = low_in[:, where] + left_dot(next_t[...], next_in[:, where])
        high = high_in[:, where]
        for b in range(0, BLOCK, LANES):
            blocks.append(jnp.concatenate([low[:, b : b + LANES], high[:, b : b + LANES]], 1))
    for b, block in enumerate(time_synthesis(blocks, time_t[...])):
        out_ref[:, b * BLOCK : (b + 1) * BLOCK] = block


def final_kernel(own_ref, s0, s1, s2, time_t, state_t, scale_ref, out_ref):
    pairs, lows = [], []
    for start in range(0, s0.shape[1], LANES):
        low, high = take_joint((s0, s1, s2), slice(start, start + LANES))
        count = high.shape[0]
        pairs.append(jnp.concatenate([low[:count], high], 1))
        lows.append(low[count:])
    level0 = time_synthesis(pairs, time_t[...])
    level1 = synthesis_from_low(lows, low_rows(time_t))
    scale = scale_ref[...]
    for b in range(len(pairs)):
        where = slice(b * BLOCK, (b + 1) * BLOCK)
        states = jnp.concatenate([level0[b], level1[b]], 0)
        out_ref[:, where] = (own_ref[:, where] + left_dot(state_t[...], states)) * scale


def low_rows(time_t):
    count = time_t.shape[0] // BLOCK
    return jnp.concatenate([time_t[k * BLOCK : k * BLOCK + LANES] for k in range(count)], 0)


def last_kernel(level, thr_ref, timed_ref, own_ref, edge_ref, s0, s1, s2, back_ref, shrunk_ref, *state_outs):
    quarter = timed_ref.shape[0] // 4
    half = timed_ref.shape[1] // 2
    for start in range(0, 2 * half, BLOCK):
        where = slice(start, start + BLOCK)
        states = join_rows((s0, s1, s2), where)
        bands = left_dot(own_ref[...], timed_ref[:, where]) + left_dot(edge_ref[...], states)
        high = start >= half
        row = lax.broadcasted_iota(jnp.int32, bands.shape, 0)
        limit = jnp.full(bands.shape, thr_ref[level, 0] if high else 0.0, f32)
        for q in range(1, 4):
            limit = jnp.where(row >= q * quarter, thr_ref[level, 2 * q + int(high) - 1], limit)
        shrunk_ref[:, where] = shrink(bands, limit)
    put_states(shrunk_ref, back_ref, state_outs, BLOCK)


def rebuilt_blocks(shrunk, own_t, state_t, s0, s1, s2, time_t):
    half = shrunk.shape[1] // 2
    blocks = []
    for start in range(0, half, LANES):
        pair = []
        for base in (0, half):
            where = slice(base + start, base + start + LANES)
            pair.append((shrunk[:, where], join_rows((s0, s1, s2), where)))
        bands = jnp.concatenate([pair[0][0], pair[1][0]], 1)
        states = jnp.concatenate([pair[0][1], pair[1][1]], 1)
        blocks.append(left_dot(own_t[...], bands) + left_dot(state_t[...], states))
    return time_synthesis(blocks, time_t[...])


def call(kernel, outs, *args, smem=(), far=(), far_outs=(), scratch=(), after=(), cost=None):
    spaces = [pltpu.SMEM if i in smem else pltpu.HBM if i in far else pltpu.VMEM for i in range(len(args))]
    spaces += [pl.ANY] * len(after)
    count = len(args)

    def body(*refs):
        kernel(*refs[:count], *refs[count + len(after) :])

    return pl.pallas_call(
        body,
        out_shape=[jax.ShapeDtypeStruct(shape, dtype) for shape, dtype in outs],
        in_specs=[pl.BlockSpec(memory_space=space) for space in spaces],
        out_specs=[
            pl.BlockSpec(memory_space=pltpu.HBM if i in far_outs else pltpu.VMEM) for i in range(len(outs))
        ],
        scratch_shapes=list(scratch),
        compiler_params=pltpu.CompilerParams(vmem_limit_bytes=VMEM_LIMIT),
        cost_estimate=None
        if cost is None
        else pl.CostEstimate(flops=int(cost), bytes_accessed=0, transcendentals=0),
    )(*args, *after)


def shift(block, inline_by, cross_by):
    inline_devs, cross_devs = lax.axis_size("inl"), lax.axis_size("xl")
    if not cross_by:
        return lax.ppermute(block, "inl", [((i + inline_by) % inline_devs, i) for i in range(inline_devs)])
    if not inline_by:
        return lax.ppermute(block, "xl", [((j + cross_by) % cross_devs, j) for j in range(cross_devs)])
    route = [
        ((i + inline_by) % inline_devs * cross_devs + (j + cross_by) % cross_devs, i * cross_devs + j)
        for i in range(inline_devs)
        for j in range(cross_devs)
    ]
    return lax.ppermute(block, ("inl", "xl"), route)


def exchange(states, ahead):
    return [shift(states[0], ahead, 0), shift(states[1], 0, ahead), shift(states[2], ahead, ahead)]


def on_device(traces, dest_tile, bin_in_tile, fold, thresholds):
    devices = lax.axis_size("inl") * lax.axis_size("xl")
    trace_count, samples = traces.shape
    tile_rows, tile_cols = fold.shape
    bins = tile_rows * tile_cols
    width = SLOTS * samples // GROUP + LANES
    (outgoing,) = call(
        route_kernel,
        [((devices * GROUP, width), bf16)],
        dest_tile.reshape(1, trace_count),
        bin_in_tile.reshape(1, trace_count),
        traces,
        far=(0, 1, 2),
        far_outs=(0,),
        scratch=[
            pltpu.VMEM((1, trace_count), jnp.int32),
            pltpu.VMEM((1, trace_count), jnp.int32),
            pltpu.VMEM((trace_count, samples), bf16),
            pltpu.VMEM((devices * GROUP, width), bf16),
            pltpu.SemaphoreType.DMA((6,)),
            pltpu.SemaphoreType.DMA((4,)),
        ],
    )
    arrived = lax.all_to_all(
        outgoing.reshape(devices, GROUP, width), ("inl", "xl"), split_axis=0, concat_axis=0, tiled=True
    ).reshape(devices * GROUP, width)
    scale = (1.0 / jnp.sqrt(fold.astype(f32))).reshape(bins, 1)

    main, following = time_parts()
    time_matrix = np.concatenate([triple(main, 0), triple(following, 0)], 0)
    back_main, back_last = main.T, np.pad(following.T, ((0, 0), (0, BLOCK - LANES)))
    time_back = np.concatenate([triple(back_main, 0), triple(back_last, 0)], 0)
    time_back_low = np.concatenate([triple(back_main[:LANES], 0), triple(back_last[:LANES], 0)], 0)
    half, rows2, cols2 = samples // 2, tile_rows // 4, tile_cols // 4
    quarter, last = bins // 4, bins // 16
    own0, edge0, own1, edge1, states01, sizes = joint_matrices(tile_rows, tile_cols)
    own2, edge2, states2, sizes2 = tile_parts(rows2, cols2)
    count0 = sum(sizes[:3])
    joint_shapes = [
        ((2 * sizes[0] + sizes[3], half), f32),
        ((2 * sizes[1] + sizes[4], half), f32),
        ((2 * sizes[2], half), f32),
    ]
    shapes2 = [((size, samples // 4), f32) for size in sizes2]

    summed, *states = call(
        bin_kernel,
        [((bins, samples), f32)] + joint_shapes,
        arrived,
        scale,
        time_matrix,
        triple(states01, 1),
        far=(0, 2, 3),
        scratch=[
            pltpu.VMEM((devices * GROUP, width), bf16),
            pltpu.VMEM(time_matrix.shape, bf16),
            pltpu.VMEM((sum(sizes), 3 * bins), bf16),
            pltpu.SemaphoreType.DMA((6,)),
        ],
    )
    states = exchange(states, 1)
    own_low, own_high, own_next = call(
        own_kernel,
        [((bins, half), f32)] * 2 + [((quarter, half), f32)],
        summed,
        time_matrix,
        triple(own0, 1),
        triple(own1, 1),
        cost=8e9,
    )
    shrunk1, timed, *states2_out = call(
        middle_kernel,
        [((quarter, half), f32), ((last, half // 2), f32)] + shapes2,
        thresholds,
        own_next,
        triple(edge1, 1),
        *states,
        time_matrix,
        triple(states2, 1),
        smem=(0,),
    )
    ahead = exchange(states2_out, 1)
    low_details, high_details, low_states, high_states = call(
        details_kernel,
        [((bins - quarter, half), f32), ((bins, half), f32)] + [((count0, half), f32)] * 2,
        thresholds,
        own_low,
        own_high,
        triple(edge0, 1),
        *states,
        triple(edge0[quarter:].T, 1),
        triple(edge0.T, 1),
        smem=(0,),
        after=(timed,),
        cost=6e9,
    )
    shrunk2, *states2_out = call(
        functools.partial(last_kernel, 2),
        [((last, half // 2), f32)] + shapes2,
        thresholds,
        timed,
        triple(own2, 1),
        triple(edge2, 1),
        *ahead,
        triple(edge2.T, 1),
        smem=(0,),
        after=(low_details,),
    )
    behind = exchange(states2_out, -1)
    spread_low, spread_high, spread_next = call(
        spread_kernel,
        [((bins, half), f32)] * 2 + [((quarter, half), f32)],
        low_details,
        high_details,
        triple(own0[quarter:].T, 1),
        triple(own0.T, 1),
        shrunk1,
        time_back,
        after=(shrunk2,),
        cost=6e9,
    )
    bands1, *states = call(
        rejoin_kernel,
        [((quarter, half), f32)] + joint_shapes,
        shrunk2,
        triple(own2.T, 1),
        triple(states2.T, 1),
        *behind,
        time_back,
        time_back_low,
        spread_next,
        low_states,
        high_states,
        triple(edge1.T, 1),
    )
    states = exchange(states, -1)
    (own_back,) = call(
        own_back_kernel,
        [((bins, samples), f32)],
        spread_low,
        spread_high,
        bands1,
        triple(own1.T, 1),
        time_back,
        cost=6e9,
    )
    (denoised,) = call(
        final_kernel,
        [((bins, samples), f32)],
        own_back,
        *states,
        time_back,
        triple(states01.T, 1),
        scale,
    )
    return denoised.reshape(tile_rows, tile_cols, samples)


def solution(mesh):
    placed = (P(("inl", "xl"), None), P(("inl", "xl"), None), P(("inl", "xl")), P("inl", "xl"), P())
    return jax.shard_map(
        on_device, mesh=mesh, in_specs=placed, out_specs=P("inl", "xl", None), check_vma=False
    )
```

```python
import functools

import jax
import jax.numpy as jnp
import ml_dtypes
import numpy as np
from jax import lax
from jax.experimental import pallas as pl
from jax.experimental.pallas import tpu as pltpu
from jax.sharding import PartitionSpec as P

LEVELS = 3
SLOTS = 6
GROUP = 8
LANES = 128
BLOCK = 256
VMEM_LIMIT = 32 * 1024 * 1024
LARGE_LIMIT = 62 * 1024 * 1024
MIDDLE_LIMIT = 48 * 1024 * 1024
SIDE = 4

low_taps = [
    0.0352262918857095,
    -0.0854412738820267,
    -0.1350110200102546,
    0.4598775021184914,
    0.8068915093110924,
    0.3326705529500826,
]
high_taps = [(-1) ** offset * low_taps[5 - offset] for offset in range(6)]

bf16 = jnp.bfloat16
f32 = jnp.float32


def halves(matrix):
    top = np.asarray(matrix, np.float32).astype(ml_dtypes.bfloat16)
    rest = (np.asarray(matrix, np.float64) - top.astype(np.float64)).astype(ml_dtypes.bfloat16)
    return top, rest


def triple(matrix, axis):
    top, rest = halves(matrix)
    return np.concatenate([top, top, rest], axis)


def line_parts(length):
    half = length // 2
    whole = np.zeros((length, length + 4))
    for m in range(half):
        for k in range(6):
            whole[m, 2 * m + k] = low_taps[k]
            whole[half + m, 2 * m + k] = high_taps[k]
    left, sizes, right = np.linalg.svd(whole[:, length:])
    assert sizes[2] < 1e-9
    state = np.zeros((2, length))
    state[:, :4] = right[:2]
    return whole[:, :length], left[:, :2] * sizes[:2], state


def outer(on_rows, on_cols, banded):
    both = np.einsum("ar,bc->abrc", on_rows, on_cols)
    a, b, r, c = both.shape
    if banded:
        both = both.reshape(2, a // 2, 2, b // 2, r, c).transpose(2, 0, 1, 3, 4, 5)
    return both.reshape(a * b, r * c)


def two_levels(length):
    own0, edge0, state0 = line_parts(length)
    own1, edge1, state1 = line_parts(length // 2)
    low = slice(0, length // 2)
    assert np.abs(state1 @ edge0[low]).max() < 1e-9
    further = state1 @ own0[low]
    return dict(
        own0=own0,
        edge0=edge0,
        state0=state0,
        own1=own1 @ own0[low],
        far1=own1 @ edge0[low],
        edge1=edge1,
        further=further,
        states=np.concatenate([state0, further]),
    )


def joint_matrices(rows, cols):
    i, c = two_levels(rows), two_levels(cols)
    wide = [np.concatenate([d["edge0"], np.zeros_like(d["edge0"])], 1) for d in (i, c)]
    both = [np.concatenate([d["far1"], d["edge1"]], 1) for d in (i, c)]
    first = [0, 1, 4, 5] + [k for k in range(16) if k not in (0, 1, 4, 5)]
    own0 = outer(i["own0"], c["own0"], True)
    edge0 = [outer(i["edge0"], c["own0"], True), outer(i["own0"], c["edge0"], True), outer(*wide, True)[:, first]]
    own1 = outer(i["own1"], c["own1"], True)
    edge1 = [
        outer(i["far1"], c["own1"], True),
        outer(i["own1"], c["far1"], True),
        outer(*both, True)[:, first],
        outer(i["edge1"], np.eye(cols // 2), True),
        outer(np.eye(rows // 2), c["edge1"], True),
    ]
    states = [
        outer(i["state0"], np.eye(cols), False),
        outer(np.eye(rows), c["state0"], False),
        outer(i["states"], c["states"], False)[first],
        outer(i["further"], c["own1"], False),
        outer(i["own1"], c["further"], False),
    ]
    sizes = [len(part) for part in states]
    return own0, np.concatenate(edge0, 1), own1, np.concatenate(edge1, 1), np.concatenate(states, 0), sizes


def side_parts(length):
    firsts = range(-SIDE // 2, length // 2)
    count = len(firsts)
    bands = np.zeros((2 * count, length + 2 * SIDE))
    back = np.zeros((length, 2 * count))
    for m, first in enumerate(firsts):
        for k in range(6):
            for part, taps in ((0, low_taps), (count, high_taps)):
                bands[part + m, SIDE + 2 * first + k] = taps[k]
                if 0 <= 2 * first + k < length:
                    back[2 * first + k, part + m] = taps[k]
    return bands, back


def side_matrices(rows, cols):
    bands_i, back_i = side_parts(rows)
    bands_c, back_c = side_parts(cols)
    bands = outer(bands_i, bands_c, True)
    wide = cols + 2 * SIDE
    order = []
    for block in range(3):
        for first, size in ((0, SIDE), (SIDE, cols), (SIDE + cols, SIDE)):
            order += [(block * rows + r) * wide + first + c for r in range(rows) for c in range(size)]
    back = outer(back_i.T, back_c.T, True).T
    return bands[:, order], back


def time_parts():
    whole = np.zeros((BLOCK + LANES, BLOCK))
    for m in range(LANES):
        for k in range(6):
            whole[2 * m + k, m] = low_taps[k]
            whole[2 * m + k, LANES + m] = high_taps[k]
    return whole[:BLOCK], whole[BLOCK:]


def split(value):
    top = value.astype(bf16)
    return top, (value - top.astype(f32)).astype(bf16)


def dot(left, right):
    return jnp.dot(left, right, preferred_element_type=f32)


def left_dot(matrix, value):
    top, rest = split(value)
    return dot(matrix, jnp.concatenate([top, rest, top], 0))


def time_analysis(blocks, matrix):
    parts = [split(block) for block in blocks]
    lows, highs = [], []
    for b in range(len(blocks)):
        top, rest = parts[b]
        next_top, next_rest = [part[:, :LANES] for part in parts[(b + 1) % len(blocks)]]
        joined = jnp.concatenate([top, rest, top, next_top, next_rest, next_top], 1)
        result = dot(joined, matrix)
        lows.append(result[:, :LANES])
        highs.append(result[:, LANES:])
    return lows, highs


def time_synthesis(blocks, matrix):
    parts = [split(block) for block in blocks]
    results = []
    for b in range(len(blocks)):
        top, rest = parts[b]
        last_top, last_rest = parts[b - 1]
        joined = jnp.concatenate([top, rest, top, last_top, last_rest, last_top], 1)
        results.append(dot(joined, matrix))
    return results


def synthesis_from_low(lows, matrix):
    parts = [split(low) for low in lows]
    results = []
    for b in range(len(lows)):
        top, rest = parts[b]
        last_top, last_rest = parts[b - 1]
        joined = jnp.concatenate([top, rest, top, last_top, last_rest, last_top], 1)
        results.append(dot(joined, matrix))
    return results


def shrink(value, limit):
    return value - jnp.clip(value, -limit, limit)


def route_kernel(dest_far, bin_far, traces_far, out_far, dest_ref, bin_ref, traces_ref, out_ref, in_sems, out_sems):
    traces, samples = traces_ref.shape
    rows = out_ref.shape[0]
    tiles = rows // GROUP
    span = samples // 4
    coming = [
        pltpu.make_async_copy(dest_far, dest_ref, in_sems.at[4]),
        pltpu.make_async_copy(bin_far, bin_ref, in_sems.at[5]),
    ]
    for j in (3, 0, 1, 2):
        at = pl.ds(j * span, span)
        coming.append(pltpu.make_async_copy(traces_far.at[:, at], traces_ref.at[:, at], in_sems.at[j]))
    for copy in coming:
        copy.start()
    before = lax.broadcasted_iota(jnp.int32, (traces, traces), 0) <= lax.broadcasted_iota(
        jnp.int32, (traces, traces), 1
    )
    before = before.astype(f32).astype(bf16)
    coming[0].wait()
    coming[1].wait()
    dest = dest_ref[...]
    matches = lax.broadcasted_iota(jnp.int32, (tiles, traces), 0) == dest
    counts = dot(matches.astype(f32).astype(bf16), before)
    place = jnp.sum(jnp.where(matches, counts, 0.0), 0, keepdims=True).astype(jnp.int32) - 1
    row_at = lax.broadcasted_iota(jnp.int32, (rows, traces), 0)
    main = (row_at == dest * GROUP + place).astype(f32).astype(bf16)
    going = []

    def send(number, first, width):
        at = pl.ds(first, width)
        going.append(pltpu.make_async_copy(out_ref.at[:, at], out_far.at[:, at], out_sems.at[number]))
        going[-1].start()

    code = bin_ref[...] + 1
    lane = lax.broadcasted_iota(jnp.int32, (LANES, traces), 0)
    digits = jnp.where(lane == 0, code // 2, jnp.where(lane == 1, code % 2, 0))
    labels = lax.dot_general(
        main,
        digits.astype(f32).astype(bf16),
        (((1,), (1,)), ((), ())),
        preferred_element_type=f32,
    )
    out_ref[:, 3 * span :] = labels.astype(bf16)
    send(3, 3 * span, LANES)
    coming[2].wait()
    tail = traces_ref[:, 3 * span : samples]
    for j in range(3):
        tail_row = jnp.where(place == j, SLOTS, jnp.where(place == 3 + j, SLOTS + 1, -rows * GROUP))
        extra = (row_at == dest * GROUP + tail_row).astype(f32).astype(bf16)
        at = slice(j * span, (j + 1) * span)
        coming[3 + j].wait()
        both = jnp.concatenate([traces_ref[:, at], tail], 0)
        out_ref[:, at] = dot(jnp.concatenate([main, extra], 1), both).astype(bf16)
        send(j, j * span, span)
    for copy in going:
        copy.wait()


def bin_kernel(arrived_far, scale_ref, time_ref, state_ref, summed_ref, s0, s1, s2, arrived_ref, sems):
    outs = (s0, s1, s2)
    width = summed_ref.shape[1] // 4
    coming = []
    for j, (first, size) in enumerate([(3 * width, LANES)] + [(j * width, width) for j in range(3)]):
        at = pl.ds(first, size)
        coming.append(pltpu.make_async_copy(arrived_far.at[:, at], arrived_ref.at[:, at], sems.at[j]))
        coming[-1].start()
    coming[0].wait()
    rows = arrived_ref.shape[0]
    bins, samples = summed_ref.shape
    span = samples // 4
    labels = arrived_ref[:, 3 * span :]
    lane = lax.broadcasted_iota(jnp.int32, (GROUP, LANES), 1)
    weights = jnp.where(lane == 0, 2.0, jnp.where(lane == 1, 1.0, 0.0)).astype(bf16)
    code = lax.dot_general(
        weights, labels, (((1,), (1,)), ((), ())), preferred_element_type=f32
    ).astype(jnp.int32)
    at = lax.broadcasted_iota(jnp.int32, (GROUP, rows), 1) % GROUP
    code = jnp.where(at < SLOTS, code, 0) - 1
    bin_at = lax.broadcasted_iota(jnp.int32, (bins, rows), 0)
    main = (bin_at == code[:1]).astype(f32).astype(bf16)
    scale = scale_ref[...]
    pieces = []
    for j in range(3):
        coming[1 + j].wait()
        pieces.append(dot(main, arrived_ref[:, j * span : (j + 1) * span]))
    last = None
    for j in range(3):
        first = pltpu.roll(code, SLOTS - j, 1)
        second = pltpu.roll(code, SLOTS + 1 - 3 - j, 1)
        tail_code = jnp.where(at == SLOTS, first, jnp.where(at == SLOTS + 1, second, -1))
        onehot = (bin_at == tail_code[:1]).astype(f32).astype(bf16)
        term = dot(onehot, arrived_ref[:, j * span : (j + 1) * span])
        last = term if last is None else last + term
    pieces.append(last)
    matrix = state_ref[...]
    blocks = []
    for p, piece in enumerate(pieces):
        piece = piece * scale
        summed_ref[:, p * span : (p + 1) * span] = piece
        states = left_dot(matrix, piece)
        blocks += [states[:, b : b + BLOCK] for b in range(0, span, BLOCK)]
    lows, highs = time_analysis(blocks, time_ref[...])
    for b in range(len(blocks)):
        put_joint(outs, slice(b * LANES, (b + 1) * LANES), lows[b], highs[b])


def put_joint(outs, where, low, high):
    part = joint_parts(outs)
    outs[0][:, where] = jnp.concatenate([low[part[0]], high[part[0]], low[part[3]]], 0)
    outs[1][:, where] = jnp.concatenate([low[part[1]], high[part[1]], low[part[4]]], 0)
    outs[2][:, where] = jnp.concatenate([low[part[2]], high[part[2]][:8]], 0)


def joint_parts(refs):
    rows, cols, corner = [ref.shape[0] for ref in refs]
    ends = [0]
    for size in (rows * 2 // 5, cols * 2 // 5, corner - 8, rows // 5, cols // 5):
        ends.append(ends[-1] + size)
    return [slice(ends[k], ends[k + 1]) for k in range(5)]


def take_joint(refs, where):
    rows, cols, corner = [ref.shape[0] for ref in refs]
    r, c, d = rows * 2 // 5, cols * 2 // 5, corner - 8
    m0, m1, m2 = [ref[:, where] for ref in refs]
    low = jnp.concatenate([m0[:r], m1[:c], m2[:d], m0[2 * r :], m1[2 * c :]], 0)
    high = jnp.concatenate([m0[r : 2 * r], m1[c : 2 * c], m2[d:], jnp.zeros((d - 8, m2.shape[1]), f32)], 0)
    return low, high


def join_rows(refs, where):
    return jnp.concatenate([ref[:, where] for ref in refs], 0)


def steps(ref):
    return [slice(start, start + BLOCK) for start in range(0, ref.shape[1], BLOCK)]


def own_kernel(summed_ref, time_ref, own_ref, next_ref, low_ref, high_ref, next_out):
    blocks = [summed_ref[:, where] for where in steps(summed_ref)]
    lows, highs = time_analysis(blocks, time_ref[...])
    for b in range(0, len(blocks), 2):
        where = slice(b * LANES, (b + 2) * LANES)
        low = jnp.concatenate([lows[b], lows[b + 1]], 1)
        next_out[:, where] = left_dot(next_ref[...], low)
        low_ref[:, where] = left_dot(own_ref[...], low)
        high_ref[:, where] = left_dot(own_ref[...], jnp.concatenate([highs[b], highs[b + 1]], 1))


def middle_kernel(cols, thr_ref, own_ref, edge_ref, s0, s1, s2, time_ref, shrunk_ref, timed_ref, first_out, last_out):
    quarter = shrunk_ref.shape[0] // 4
    half = shrunk_ref.shape[1] // 2
    matrix = edge_ref[...]
    blocks = []
    for where in steps(own_ref):
        low, _ = take_joint((s0, s1, s2), where)
        blocks.append(own_ref[:, where] + left_dot(matrix, low))
    lows, highs = time_analysis(blocks, time_ref[...])
    for b in range(len(blocks)):
        for base, piece, high in ((0, lows[b], 0), (half, highs[b], 1)):
            where = slice(base + b * LANES, base + (b + 1) * LANES)
            for q in range(4):
                at = slice(q * quarter, (q + 1) * quarter)
                if q or high:
                    shrunk_ref[at, where] = shrink(piece[at], thr_ref[1, 2 * q + high - 1])
                else:
                    shrunk_ref[at, where] = jnp.zeros_like(piece[at])
    coarse = [jnp.concatenate([lows[b][:quarter], lows[b + 1][:quarter]], 1) for b in range(0, len(lows), 2)]
    lows, highs = time_analysis(coarse, time_ref[...])
    for b in range(len(coarse)):
        for base, piece in ((0, lows[b]), (half // 2, highs[b])):
            timed_ref[:, base + b * LANES : base + (b + 1) * LANES] = piece
    starts = range(0, timed_ref.shape[0], cols)
    first_out[...] = jnp.concatenate([timed_ref[at : at + SIDE] for at in starts], 0)
    last_out[...] = jnp.concatenate([timed_ref[at + cols - SIDE : at + cols] for at in starts], 0)


def join_kernel(left_ref, own_ref, right_ref, out_ref):
    out_ref[...] = jnp.concatenate([left_ref[...], own_ref[...], right_ref[...]], 0)


def details_kernel(
    thr_ref, low_in, high_in, edge_ref, s0, s1, s2, back_low, back_ref, low_out, high_out, low_states, high_states
):
    quarter = low_in.shape[0] // 4
    for where in steps(low_in):
        low, high = take_joint((s0, s1, s2), where)
        bands = low_in[quarter:, where] + left_dot(edge_ref[quarter:], low[: high.shape[0]])
        bands = [shrink(bands[(q - 1) * quarter : q * quarter], thr_ref[0, 2 * q - 1]) for q in range(1, 4)]
        bands = jnp.concatenate(bands, 0)
        low_out[:, where] = bands
        low_states[:, where] = left_dot(back_low[...], bands)
        bands = high_in[:, where] + left_dot(edge_ref[...], high)
        bands = [shrink(bands[q * quarter : (q + 1) * quarter], thr_ref[0, 2 * q]) for q in range(4)]
        bands = jnp.concatenate(bands, 0)
        high_out[:, where] = bands
        high_states[:, where] = left_dot(back_ref[...], bands)


def time_pairs(bands, matrix):
    half = bands.shape[1] // 2
    pairs = []
    for b in range(0, half, LANES):
        pairs.append(jnp.concatenate([bands[:, b : b + LANES], bands[:, half + b : half + b + LANES]], 1))
    return time_synthesis(pairs, matrix)


def deepest_kernel(
    thr_ref, before, own, after, bands_m, back_m, time_t, time_low, next_in, low_states, high_states, back_ref, next_out, *outs
):
    stack = jnp.concatenate([before[...], own[...], after[...]], 0)
    bands = left_dot(bands_m[...], stack)
    row = lax.broadcasted_iota(jnp.int32, bands.shape, 0)
    high = lax.broadcasted_iota(jnp.int32, bands.shape, 1) >= bands.shape[1] // 2
    limit = jnp.where(high, thr_ref[2, 0], 0.0)
    quarter = bands.shape[0] // 4
    for q in range(1, 4):
        limit = jnp.where(row >= q * quarter, jnp.where(high, thr_ref[2, 2 * q], thr_ref[2, 2 * q - 1]), limit)
    rebuilt = left_dot(back_m[...], shrink(bands, limit))
    details = time_pairs(next_in[...], time_t[...])
    lows = []
    for block in time_pairs(rebuilt, time_t[...]):
        lows += [block[:, b : b + LANES] for b in range(0, BLOCK, LANES)]
    rows = rebuilt.shape[0]
    count = low_states.shape[0]
    for b, block in enumerate(synthesis_from_low(lows, time_low[...])):
        where = slice(b * BLOCK, (b + 1) * BLOCK)
        bands = jnp.concatenate([details[b][:rows] + block, details[b][rows:]], 0)
        next_out[:, where] = bands
        states = left_dot(back_ref[...], bands)
        low = jnp.concatenate([states[:count] + low_states[:, where], states[count:]], 0)
        put_joint(outs, where, low, high_states[:, where])


def own_back_kernel(low_in, high_in, next_in, low_t, high_t, next_t, time_t, scale_ref, out_ref):
    blocks = []
    for where in steps(low_in):
        low = left_dot(low_t[...], low_in[:, where]) + left_dot(next_t[...], next_in[:, where])
        high = left_dot(high_t[...], high_in[:, where])
        for b in range(0, BLOCK, LANES):
            blocks.append(jnp.concatenate([low[:, b : b + LANES], high[:, b : b + LANES]], 1))
    scale = scale_ref[...]
    for b, block in enumerate(time_synthesis(blocks, time_t[...])):
        out_ref[:, b * BLOCK : (b + 1) * BLOCK] = block * scale


def final_kernel(own_ref, s0, s1, s2, time_t, time_low, state_t, scale_ref, out_far, out_ref, sems):
    pairs, lows = [], []
    for start in range(0, s0.shape[1], LANES):
        low, high = take_joint((s0, s1, s2), slice(start, start + LANES))
        count = high.shape[0]
        pairs.append(jnp.concatenate([low[:count], high], 1))
        lows.append(low[count:])
    level0 = time_synthesis(pairs, time_t[...])
    level1 = synthesis_from_low(lows, time_low[...])
    scale = scale_ref[...]
    going = []
    for b in range(len(pairs)):
        where = slice(b * BLOCK, (b + 1) * BLOCK)
        states = jnp.concatenate([level0[b], level1[b]], 0)
        out_ref[:, where] = own_ref[:, where] + left_dot(state_t[...], states) * scale
        going.append(pltpu.make_async_copy(out_ref.at[:, where], out_far.at[:, where], sems.at[b]))
        going[-1].start()
    for copy in going:
        copy.wait()


def call(kernel, outs, *args, smem=(), far=(), far_outs=(), scratch=(), after=(), cost=None, limit=VMEM_LIMIT):
    spaces = [pltpu.SMEM if i in smem else pltpu.HBM if i in far else pltpu.VMEM for i in range(len(args))]
    spaces += [pl.ANY] * len(after)
    count = len(args)

    def body(*refs):
        kernel(*refs[:count], *refs[count + len(after) :])

    return pl.pallas_call(
        body,
        out_shape=[jax.ShapeDtypeStruct(shape, dtype) for shape, dtype in outs],
        in_specs=[pl.BlockSpec(memory_space=space) for space in spaces],
        out_specs=[
            pl.BlockSpec(memory_space=pltpu.HBM if i in far_outs else pltpu.VMEM) for i in range(len(outs))
        ],
        scratch_shapes=list(scratch),
        compiler_params=pltpu.CompilerParams(vmem_limit_bytes=limit),
        cost_estimate=None
        if cost is None
        else pl.CostEstimate(flops=int(cost), bytes_accessed=0, transcendentals=0),
    )(*args, *after)


def shift(block, inline_by, cross_by):
    inline_devs, cross_devs = lax.axis_size("inl"), lax.axis_size("xl")
    if not cross_by:
        return lax.ppermute(block, "inl", [((i + inline_by) % inline_devs, i) for i in range(inline_devs)])
    if not inline_by:
        return lax.ppermute(block, "xl", [((j + cross_by) % cross_devs, j) for j in range(cross_devs)])
    route = [
        ((i + inline_by) % inline_devs * cross_devs + (j + cross_by) % cross_devs, i * cross_devs + j)
        for i in range(inline_devs)
        for j in range(cross_devs)
    ]
    return lax.ppermute(block, ("inl", "xl"), route)


def exchange(states, ahead):
    return [shift(states[0], ahead, 0), shift(states[1], 0, ahead), shift(states[2], ahead, ahead)]


def on_device(traces, dest_tile, bin_in_tile, fold, thresholds):
    devices = lax.axis_size("inl") * lax.axis_size("xl")
    trace_count, samples = traces.shape
    tile_rows, tile_cols = fold.shape
    bins = tile_rows * tile_cols
    width = SLOTS * samples // GROUP + LANES
    (outgoing,) = call(
        route_kernel,
        [((devices * GROUP, width), bf16)],
        dest_tile.reshape(1, trace_count),
        bin_in_tile.reshape(1, trace_count),
        traces,
        far=(0, 1, 2),
        far_outs=(0,),
        limit=LARGE_LIMIT,
        scratch=[
            pltpu.VMEM((1, trace_count), jnp.int32),
            pltpu.VMEM((1, trace_count), jnp.int32),
            pltpu.VMEM((trace_count, samples), bf16),
            pltpu.VMEM((devices * GROUP, width), bf16),
            pltpu.SemaphoreType.DMA((6,)),
            pltpu.SemaphoreType.DMA((4,)),
        ],
    )
    arrived = lax.all_to_all(
        outgoing.reshape(devices, GROUP, width), ("inl", "xl"), split_axis=0, concat_axis=0, tiled=True
    ).reshape(devices * GROUP, width)
    scale = (1.0 / jnp.sqrt(fold.astype(f32))).reshape(bins, 1)

    main, following = time_parts()
    time_matrix = np.concatenate([triple(main, 0), triple(following, 0)], 0)
    back_main, back_last = main.T, np.pad(following.T, ((0, 0), (0, BLOCK - LANES)))
    time_back = np.concatenate([triple(back_main, 0), triple(back_last, 0)], 0)
    time_back_low = np.concatenate([triple(back_main[:LANES], 0), triple(back_last[:LANES], 0)], 0)
    half, rows2, cols2 = samples // 2, tile_rows // 4, tile_cols // 4
    quarter, last = bins // 4, bins // 16
    own0, edge0, own1, edge1, states01, sizes = joint_matrices(tile_rows, tile_cols)
    assert rows2 == SIDE and cols2 >= SIDE
    bands2, back2 = side_matrices(rows2, cols2)
    count0 = sum(sizes[:3])
    joint_shapes = [
        ((2 * sizes[0] + sizes[3], half), f32),
        ((2 * sizes[1] + sizes[4], half), f32),
        ((sizes[2] + 8, half), f32),
    ]

    summed, *states = call(
        bin_kernel,
        [((bins, samples), f32)] + joint_shapes,
        arrived,
        scale,
        time_matrix,
        triple(states01, 1),
        far=(0,),
        limit=MIDDLE_LIMIT,
        scratch=[pltpu.VMEM((devices * GROUP, width), bf16), pltpu.SemaphoreType.DMA((4,))],
    )
    states = exchange(states, 1)
    own_low, own_high, own_next = call(
        own_kernel,
        [((bins, half), f32)] * 2 + [((quarter, half), f32)],
        summed,
        time_matrix,
        triple(own0, 1),
        triple(own1, 1),
        cost=8e9,
    )
    side_shape = ((rows2 * SIDE, samples // 4), f32)
    shrunk1, timed, firsts, lasts = call(
        functools.partial(middle_kernel, cols2),
        [((quarter, half), f32), ((last, half // 2), f32), side_shape, side_shape],
        thresholds,
        own_next,
        triple(edge1, 1),
        *states,
        time_matrix,
        smem=(0,),
    )
    sides = shift(lasts, 0, -1), shift(firsts, 0, 1)
    (wide,) = call(
        join_kernel,
        [((last + 2 * rows2 * SIDE, samples // 4), f32)],
        sides[0],
        timed,
        sides[1],
    )
    before, behind = shift(wide, -1, 0), shift(wide, 1, 0)
    low_details, high_details, low_states, high_states = call(
        details_kernel,
        [((bins - quarter, half), f32), ((bins, half), f32)] + [((count0, half), f32)] * 2,
        thresholds,
        own_low,
        own_high,
        triple(edge0, 1),
        *states,
        triple(edge0[quarter:].T, 1),
        triple(edge0.T, 1),
        smem=(0,),
        after=(wide,),
        cost=6e9,
    )
    bands1, *states = call(
        deepest_kernel,
        [((quarter, half), f32)] + joint_shapes,
        thresholds,
        before,
        wide,
        behind,
        triple(bands2, 1),
        triple(back2, 1),
        time_back,
        time_back_low,
        shrunk1,
        low_states,
        high_states,
        triple(edge1.T, 1),
        smem=(0,),
    )
    states = exchange(states, -1)
    (own_back,) = call(
        own_back_kernel,
        [((bins, samples), f32)],
        low_details,
        high_details,
        bands1,
        triple(own0[quarter:].T, 1),
        triple(own0.T, 1),
        triple(own1.T, 1),
        time_back,
        scale,
        cost=6e9,
    )
    (denoised,) = call(
        final_kernel,
        [((bins, samples), f32)],
        own_back,
        *states,
        time_back,
        time_back_low,
        triple(states01.T, 1),
        scale,
        far_outs=(0,),
        scratch=[pltpu.VMEM((bins, samples), f32), pltpu.SemaphoreType.DMA((samples // BLOCK,))],
    )
    return denoised.reshape(tile_rows, tile_cols, samples)


def solution(mesh):
    placed = (P(("inl", "xl"), None), P(("inl", "xl"), None), P(("inl", "xl")), P("inl", "xl"), P())
    return jax.shard_map(
        on_device, mesh=mesh, in_specs=placed, out_specs=P("inl", "xl", None), check_vma=False
    )
```

```python
import functools

import jax
import jax.numpy as jnp
import ml_dtypes
import numpy as np
from jax import lax
from jax.experimental import pallas as pl
from jax.experimental.pallas import tpu as pltpu
from jax.sharding import PartitionSpec as P

LEVELS = 3
SLOTS = 6
GROUP = 8
LANES = 128
BLOCK = 256
VMEM_LIMIT = 32 * 1024 * 1024
LARGE_LIMIT = 62 * 1024 * 1024
MIDDLE_LIMIT = 48 * 1024 * 1024
SIDE = 4

low_taps = [
    0.0352262918857095,
    -0.0854412738820267,
    -0.1350110200102546,
    0.4598775021184914,
    0.8068915093110924,
    0.3326705529500826,
]
high_taps = [(-1) ** offset * low_taps[5 - offset] for offset in range(6)]

bf16 = jnp.bfloat16
f32 = jnp.float32


def halves(matrix):
    top = np.asarray(matrix, np.float32).astype(ml_dtypes.bfloat16)
    rest = (np.asarray(matrix, np.float64) - top.astype(np.float64)).astype(ml_dtypes.bfloat16)
    return top, rest


def triple(matrix, axis):
    top, rest = halves(matrix)
    return np.concatenate([top, top, rest], axis)


def line_parts(length):
    half = length // 2
    whole = np.zeros((length, length + 4))
    for m in range(half):
        for k in range(6):
            whole[m, 2 * m + k] = low_taps[k]
            whole[half + m, 2 * m + k] = high_taps[k]
    left, sizes, right = np.linalg.svd(whole[:, length:])
    assert sizes[2] < 1e-9
    state = np.zeros((2, length))
    state[:, :4] = right[:2]
    return whole[:, :length], left[:, :2] * sizes[:2], state


def outer(on_rows, on_cols, banded):
    both = np.einsum("ar,bc->abrc", on_rows, on_cols)
    a, b, r, c = both.shape
    if banded:
        both = both.reshape(2, a // 2, 2, b // 2, r, c).transpose(2, 0, 1, 3, 4, 5)
    return both.reshape(a * b, r * c)


def two_levels(length):
    own0, edge0, state0 = line_parts(length)
    own1, edge1, state1 = line_parts(length // 2)
    low = slice(0, length // 2)
    assert np.abs(state1 @ edge0[low]).max() < 1e-9
    further = state1 @ own0[low]
    return dict(
        own0=own0,
        edge0=edge0,
        state0=state0,
        own1=own1 @ own0[low],
        far1=own1 @ edge0[low],
        edge1=edge1,
        further=further,
        states=np.concatenate([state0, further]),
    )


def joint_matrices(rows, cols):
    i, c = two_levels(rows), two_levels(cols)
    wide = [np.concatenate([d["edge0"], np.zeros_like(d["edge0"])], 1) for d in (i, c)]
    both = [np.concatenate([d["far1"], d["edge1"]], 1) for d in (i, c)]
    first = [0, 1, 4, 5] + [k for k in range(16) if k not in (0, 1, 4, 5)]
    own0 = outer(i["own0"], c["own0"], True)
    edge0 = [outer(i["edge0"], c["own0"], True), outer(i["own0"], c["edge0"], True), outer(*wide, True)[:, first]]
    own1 = outer(i["own1"], c["own1"], True)
    edge1 = [
        outer(i["far1"], c["own1"], True),
        outer(i["own1"], c["far1"], True),
        outer(*both, True)[:, first],
        outer(i["edge1"], np.eye(cols // 2), True),
        outer(np.eye(rows // 2), c["edge1"], True),
    ]
    states = [
        outer(i["state0"], np.eye(cols), False),
        outer(np.eye(rows), c["state0"], False),
        outer(i["states"], c["states"], False)[first],
        outer(i["further"], c["own1"], False),
        outer(i["own1"], c["further"], False),
    ]
    sizes = [len(part) for part in states]
    return own0, np.concatenate(edge0, 1), own1, np.concatenate(edge1, 1), np.concatenate(states, 0), sizes


def side_parts(length):
    firsts = range(-SIDE // 2, length // 2)
    count = len(firsts)
    bands = np.zeros((2 * count, length + 2 * SIDE))
    back = np.zeros((length, 2 * count))
    for m, first in enumerate(firsts):
        for k in range(6):
            for part, taps in ((0, low_taps), (count, high_taps)):
                bands[part + m, SIDE + 2 * first + k] = taps[k]
                if 0 <= 2 * first + k < length:
                    back[2 * first + k, part + m] = taps[k]
    return bands, back


def side_matrices(rows, cols):
    bands_i, back_i = side_parts(rows)
    bands_c, back_c = side_parts(cols)
    bands = outer(bands_i, bands_c, True)
    wide = cols + 2 * SIDE
    order = []
    for first, size in ((0, SIDE), (SIDE, cols), (SIDE + cols, SIDE)):
        order += [r * wide + first + c for r in range(rows + 2 * SIDE) for c in range(size)]
    back = outer(back_i.T, back_c.T, True).T
    return bands[:, order], back


def time_parts():
    whole = np.zeros((BLOCK + LANES, BLOCK))
    for m in range(LANES):
        for k in range(6):
            whole[2 * m + k, m] = low_taps[k]
            whole[2 * m + k, LANES + m] = high_taps[k]
    return whole[:BLOCK], whole[BLOCK:]


def split(value):
    top = value.astype(bf16)
    return top, (value - top.astype(f32)).astype(bf16)


def dot(left, right):
    return jnp.dot(left, right, preferred_element_type=f32)


def left_dot(matrix, value):
    top, rest = split(value)
    return dot(matrix, jnp.concatenate([top, rest, top], 0))


def time_analysis(blocks, matrix):
    parts = [split(block) for block in blocks]
    lows, highs = [], []
    for b in range(len(blocks)):
        top, rest = parts[b]
        next_top, next_rest = [part[:, :LANES] for part in parts[(b + 1) % len(blocks)]]
        joined = jnp.concatenate([top, rest, top, next_top, next_rest, next_top], 1)
        result = dot(joined, matrix)
        lows.append(result[:, :LANES])
        highs.append(result[:, LANES:])
    return lows, highs


def time_synthesis(blocks, matrix):
    parts = [split(block) for block in blocks]
    results = []
    for b in range(len(blocks)):
        top, rest = parts[b]
        last_top, last_rest = parts[b - 1]
        joined = jnp.concatenate([top, rest, top, last_top, last_rest, last_top], 1)
        results.append(dot(joined, matrix))
    return results


def synthesis_from_low(lows, matrix):
    parts = [split(low) for low in lows]
    results = []
    for b in range(len(lows)):
        top, rest = parts[b]
        last_top, last_rest = parts[b - 1]
        joined = jnp.concatenate([top, rest, top, last_top, last_rest, last_top], 1)
        results.append(dot(joined, matrix))
    return results


def shrink(value, limit):
    return value - jnp.clip(value, -limit, limit)


def tail_rows(rows, count):
    row = lax.broadcasted_iota(jnp.int32, (rows, count), 0)
    tail = lax.broadcasted_iota(jnp.int32, (rows, count), 1)
    each = GROUP - SLOTS
    return (row == tail // each * GROUP + SLOTS + tail % each).astype(f32).astype(bf16)


def route_kernel(dest_far, bin_far, traces_far, out_far, dest_ref, bin_ref, traces_ref, out_ref, in_sems, out_sems):
    traces, samples = traces_ref.shape
    rows = out_ref.shape[0]
    tiles = rows // GROUP
    span = samples // 4
    coming = [
        pltpu.make_async_copy(dest_far, dest_ref, in_sems.at[4]),
        pltpu.make_async_copy(bin_far, bin_ref, in_sems.at[5]),
    ]
    for j in (3, 0, 1, 2):
        at = pl.ds(j * span, span)
        coming.append(pltpu.make_async_copy(traces_far.at[:, at], traces_ref.at[:, at], in_sems.at[j]))
    for copy in coming:
        copy.start()
    before = lax.broadcasted_iota(jnp.int32, (traces, traces), 0) <= lax.broadcasted_iota(
        jnp.int32, (traces, traces), 1
    )
    before = before.astype(f32).astype(bf16)
    coming[0].wait()
    coming[1].wait()
    dest = dest_ref[...]
    matches = lax.broadcasted_iota(jnp.int32, (tiles, traces), 0) == dest
    counts = dot(matches.astype(f32).astype(bf16), before)
    place = jnp.sum(jnp.where(matches, counts, 0.0), 0, keepdims=True).astype(jnp.int32) - 1
    row_at = lax.broadcasted_iota(jnp.int32, (rows, traces), 0)
    main = (row_at == dest * GROUP + place).astype(f32).astype(bf16)
    going = []

    def send(number, first, width):
        at = pl.ds(first, width)
        going.append(pltpu.make_async_copy(out_ref.at[:, at], out_far.at[:, at], out_sems.at[number]))
        going[-1].start()

    code = bin_ref[...] + 1
    lane = lax.broadcasted_iota(jnp.int32, (LANES, traces), 0)
    digits = jnp.where(lane == 0, code // 2, jnp.where(lane == 1, code % 2, 0))
    labels = lax.dot_general(
        main,
        digits.astype(f32).astype(bf16),
        (((1,), (1,)), ((), ())),
        preferred_element_type=f32,
    )
    out_ref[:, 3 * span :] = labels.astype(bf16)
    send(3, 3 * span, LANES)
    count = GROUP - SLOTS
    tail_at = lax.broadcasted_iota(jnp.int32, (count * tiles, traces), 0)
    put = tail_rows(rows, count * tiles)
    coming[2].wait()
    tail = traces_ref[:, 3 * span : samples]
    for j in range(3):
        tail_row = jnp.where(place == j, 0, jnp.where(place == 3 + j, 1, -rows))
        extra = (tail_at == dest * count + tail_row).astype(f32).astype(bf16)
        rest = dot(extra, tail).astype(bf16)
        at = slice(j * span, (j + 1) * span)
        coming[3 + j].wait()
        both = jnp.concatenate([traces_ref[:, at], rest], 0)
        out_ref[:, at] = dot(jnp.concatenate([main, put], 1), both).astype(bf16)
        send(j, j * span, span)
    for copy in going:
        copy.wait()


def bin_kernel(arrived_far, scale_ref, time_ref, state_ref, summed_ref, s0, s1, s2, arrived_ref, sems):
    outs = (s0, s1, s2)
    width = summed_ref.shape[1] // 4
    coming = []
    for j, (first, size) in enumerate([(3 * width, LANES)] + [(j * width, width) for j in range(3)]):
        at = pl.ds(first, size)
        coming.append(pltpu.make_async_copy(arrived_far.at[:, at], arrived_ref.at[:, at], sems.at[j]))
        coming[-1].start()
    coming[0].wait()
    rows = arrived_ref.shape[0]
    bins, samples = summed_ref.shape
    span = samples // 4
    labels = arrived_ref[:, 3 * span :]
    lane = lax.broadcasted_iota(jnp.int32, (GROUP, LANES), 1)
    weights = jnp.where(lane == 0, 2.0, jnp.where(lane == 1, 1.0, 0.0)).astype(bf16)
    code = lax.dot_general(
        weights, labels, (((1,), (1,)), ((), ())), preferred_element_type=f32
    ).astype(jnp.int32)
    at = lax.broadcasted_iota(jnp.int32, (GROUP, rows), 1) % GROUP
    code = jnp.where(at < SLOTS, code, 0) - 1
    bin_at = lax.broadcasted_iota(jnp.int32, (bins, rows), 0)
    main = (bin_at == code[:1]).astype(f32).astype(bf16)
    scale = scale_ref[...]
    pieces = []
    for j in range(3):
        coming[1 + j].wait()
        pieces.append(dot(main, arrived_ref[:, j * span : (j + 1) * span]))
    last = None
    for j in range(3):
        first = pltpu.roll(code, SLOTS - j, 1)
        second = pltpu.roll(code, SLOTS + 1 - 3 - j, 1)
        tail_code = jnp.where(at == SLOTS, first, jnp.where(at == SLOTS + 1, second, -1))
        onehot = (bin_at == tail_code[:1]).astype(f32).astype(bf16)
        term = dot(onehot, arrived_ref[:, j * span : (j + 1) * span])
        last = term if last is None else last + term
    pieces.append(last)
    matrix = state_ref[...]
    blocks = []
    for p, piece in enumerate(pieces):
        piece = piece * scale
        summed_ref[:, p * span : (p + 1) * span] = piece
        states = left_dot(matrix, piece)
        blocks += [states[:, b : b + BLOCK] for b in range(0, span, BLOCK)]
    lows, highs = time_analysis(blocks, time_ref[...])
    for b in range(len(blocks)):
        put_joint(outs, slice(b * LANES, (b + 1) * LANES), lows[b], highs[b])


def put_joint(outs, where, low, high):
    part = joint_parts(outs)
    outs[0][:, where] = jnp.concatenate([low[part[0]], high[part[0]], low[part[3]]], 0)
    outs[1][:, where] = jnp.concatenate([low[part[1]], high[part[1]], low[part[4]]], 0)
    outs[2][:, where] = jnp.concatenate([low[part[2]], high[part[2]][:8]], 0)


def joint_parts(refs):
    rows, cols, corner = [ref.shape[0] for ref in refs]
    ends = [0]
    for size in (rows * 2 // 5, cols * 2 // 5, corner - 8, rows // 5, cols // 5):
        ends.append(ends[-1] + size)
    return [slice(ends[k], ends[k + 1]) for k in range(5)]


def take_joint(refs, where):
    rows, cols, corner = [ref.shape[0] for ref in refs]
    r, c, d = rows * 2 // 5, cols * 2 // 5, corner - 8
    m0, m1, m2 = [ref[:, where] for ref in refs]
    low = jnp.concatenate([m0[:r], m1[:c], m2[:d], m0[2 * r :], m1[2 * c :]], 0)
    high = jnp.concatenate([m0[r : 2 * r], m1[c : 2 * c], m2[d:], jnp.zeros((d - 8, m2.shape[1]), f32)], 0)
    return low, high


def join_rows(refs, where):
    return jnp.concatenate([ref[:, where] for ref in refs], 0)


def steps(ref):
    return [slice(start, start + BLOCK) for start in range(0, ref.shape[1], BLOCK)]


def own_kernel(summed_ref, time_ref, own_ref, next_ref, low_ref, high_ref, next_out):
    blocks = [summed_ref[:, where] for where in steps(summed_ref)]
    lows, highs = time_analysis(blocks, time_ref[...])
    for b in range(0, len(blocks), 2):
        where = slice(b * LANES, (b + 2) * LANES)
        low = jnp.concatenate([lows[b], lows[b + 1]], 1)
        next_out[:, where] = left_dot(next_ref[...], low)
        low_ref[:, where] = left_dot(own_ref[...], low)
        high_ref[:, where] = left_dot(own_ref[...], jnp.concatenate([highs[b], highs[b + 1]], 1))


def middle_kernel(thr_ref, own_ref, edge_ref, s0, s1, s2, time_ref, shrunk_ref, timed_ref):
    quarter = shrunk_ref.shape[0] // 4
    half = shrunk_ref.shape[1] // 2
    matrix = edge_ref[...]
    blocks = []
    for where in steps(own_ref):
        low, _ = take_joint((s0, s1, s2), where)
        blocks.append(own_ref[:, where] + left_dot(matrix, low))
    lows, highs = time_analysis(blocks, time_ref[...])
    for b in range(len(blocks)):
        for base, piece, high in ((0, lows[b], 0), (half, highs[b], 1)):
            where = slice(base + b * LANES, base + (b + 1) * LANES)
            for q in range(4):
                at = slice(q * quarter, (q + 1) * quarter)
                if q or high:
                    shrunk_ref[at, where] = shrink(piece[at], thr_ref[1, 2 * q + high - 1])
                else:
                    shrunk_ref[at, where] = jnp.zeros_like(piece[at])
    coarse = [jnp.concatenate([lows[b][:quarter], lows[b + 1][:quarter]], 1) for b in range(0, len(lows), 2)]
    lows, highs = time_analysis(coarse, time_ref[...])
    for b in range(len(coarse)):
        for base, piece in ((0, lows[b]), (half // 2, highs[b])):
            timed_ref[:, base + b * LANES : base + (b + 1) * LANES] = piece


def sides_kernel(cols, before, own, after, stack_out, first_out, last_out):
    stack_out[...] = jnp.concatenate([before[...], own[...], after[...]], 0)
    starts = range(0, stack_out.shape[0], cols)
    first_out[...] = jnp.concatenate([stack_out[at : at + SIDE] for at in starts], 0)
    last_out[...] = jnp.concatenate([stack_out[at + cols - SIDE : at + cols] for at in starts], 0)


def details_kernel(
    thr_ref,
    low_in,
    high_in,
    edge_ref,
    s0,
    s1,
    s2,
    back_low,
    back_ref,
    next_in,
    time_t,
    low_out,
    high_out,
    low_states,
    high_states,
    next_out,
):
    for b, block in enumerate(time_pairs(next_in[...], time_t[...])):
        next_out[:, b * BLOCK : (b + 1) * BLOCK] = block
    quarter = low_in.shape[0] // 4
    for where in steps(low_in):
        low, high = take_joint((s0, s1, s2), where)
        bands = low_in[quarter:, where] + left_dot(edge_ref[quarter:], low[: high.shape[0]])
        bands = [shrink(bands[(q - 1) * quarter : q * quarter], thr_ref[0, 2 * q - 1]) for q in range(1, 4)]
        bands = jnp.concatenate(bands, 0)
        low_out[:, where] = bands
        low_states[:, where] = left_dot(back_low[...], bands)
        bands = high_in[:, where] + left_dot(edge_ref[...], high)
        bands = [shrink(bands[q * quarter : (q + 1) * quarter], thr_ref[0, 2 * q]) for q in range(4)]
        bands = jnp.concatenate(bands, 0)
        high_out[:, where] = bands
        high_states[:, where] = left_dot(back_ref[...], bands)


def time_pairs(bands, matrix):
    half = bands.shape[1] // 2
    pairs = []
    for b in range(0, half, LANES):
        pairs.append(jnp.concatenate([bands[:, b : b + LANES], bands[:, half + b : half + b + LANES]], 1))
    return time_synthesis(pairs, matrix)


def deepest_kernel(
    thr_ref, before, own, after, bands_m, back_m, time_t, time_low, next_in, low_states, high_states, back_ref, next_out, *outs
):
    stack = jnp.concatenate([before[...], own[...], after[...]], 0)
    bands = left_dot(bands_m[...], stack)
    row = lax.broadcasted_iota(jnp.int32, bands.shape, 0)
    high = lax.broadcasted_iota(jnp.int32, bands.shape, 1) >= bands.shape[1] // 2
    limit = jnp.where(high, thr_ref[2, 0], 0.0)
    quarter = bands.shape[0] // 4
    for q in range(1, 4):
        limit = jnp.where(row >= q * quarter, jnp.where(high, thr_ref[2, 2 * q], thr_ref[2, 2 * q - 1]), limit)
    rebuilt = left_dot(back_m[...], shrink(bands, limit))
    lows = []
    for block in time_pairs(rebuilt, time_t[...]):
        lows += [block[:, b : b + LANES] for b in range(0, BLOCK, LANES)]
    rows = rebuilt.shape[0]
    count = low_states.shape[0]
    for b, block in enumerate(synthesis_from_low(lows, time_low[...])):
        where = slice(b * BLOCK, (b + 1) * BLOCK)
        bands = jnp.concatenate([next_in[:rows, where] + block, next_in[rows:, where]], 0)
        next_out[:, where] = bands
        states = left_dot(back_ref[...], bands)
        low = jnp.concatenate([states[:count] + low_states[:, where], states[count:]], 0)
        put_joint(outs, where, low, high_states[:, where])


def own_back_kernel(low_in, high_in, next_in, low_t, high_t, next_t, time_t, scale_ref, out_ref):
    blocks = []
    for where in steps(low_in):
        low = left_dot(low_t[...], low_in[:, where]) + left_dot(next_t[...], next_in[:, where])
        high = left_dot(high_t[...], high_in[:, where])
        for b in range(0, BLOCK, LANES):
            blocks.append(jnp.concatenate([low[:, b : b + LANES], high[:, b : b + LANES]], 1))
    scale = scale_ref[...]
    for b, block in enumerate(time_synthesis(blocks, time_t[...])):
        out_ref[:, b * BLOCK : (b + 1) * BLOCK] = block * scale


def final_kernel(own_ref, s0, s1, s2, time_t, time_low, state_t, scale_ref, out_far, out_ref, sems):
    pairs, lows = [], []
    for start in range(0, s0.shape[1], LANES):
        low, high = take_joint((s0, s1, s2), slice(start, start + LANES))
        count = high.shape[0]
        pairs.append(jnp.concatenate([low[:count], high], 1))
        lows.append(low[count:])
    level0 = time_synthesis(pairs, time_t[...])
    level1 = synthesis_from_low(lows, time_low[...])
    scale = scale_ref[...]
    going = []
    for b in range(len(pairs)):
        where = slice(b * BLOCK, (b + 1) * BLOCK)
        states = jnp.concatenate([level0[b], level1[b]], 0)
        out_ref[:, where] = own_ref[:, where] + left_dot(state_t[...], states) * scale
        going.append(pltpu.make_async_copy(out_ref.at[:, where], out_far.at[:, where], sems.at[b]))
        going[-1].start()
    for copy in going:
        copy.wait()


def call(kernel, outs, *args, smem=(), far=(), far_outs=(), scratch=(), after=(), cost=None, limit=VMEM_LIMIT):
    spaces = [pltpu.SMEM if i in smem else pltpu.HBM if i in far else pltpu.VMEM for i in range(len(args))]
    spaces += [pl.ANY] * len(after)
    count = len(args)

    def body(*refs):
        kernel(*refs[:count], *refs[count + len(after) :])

    return pl.pallas_call(
        body,
        out_shape=[jax.ShapeDtypeStruct(shape, dtype) for shape, dtype in outs],
        in_specs=[pl.BlockSpec(memory_space=space) for space in spaces],
        out_specs=[
            pl.BlockSpec(memory_space=pltpu.HBM if i in far_outs else pltpu.VMEM) for i in range(len(outs))
        ],
        scratch_shapes=list(scratch),
        compiler_params=pltpu.CompilerParams(vmem_limit_bytes=limit),
        cost_estimate=None
        if cost is None
        else pl.CostEstimate(flops=int(cost), bytes_accessed=0, transcendentals=0),
    )(*args, *after)


def shift(block, inline_by, cross_by):
    inline_devs, cross_devs = lax.axis_size("inl"), lax.axis_size("xl")
    if not cross_by:
        return lax.ppermute(block, "inl", [((i + inline_by) % inline_devs, i) for i in range(inline_devs)])
    if not inline_by:
        return lax.ppermute(block, "xl", [((j + cross_by) % cross_devs, j) for j in range(cross_devs)])
    route = [
        ((i + inline_by) % inline_devs * cross_devs + (j + cross_by) % cross_devs, i * cross_devs + j)
        for i in range(inline_devs)
        for j in range(cross_devs)
    ]
    return lax.ppermute(block, ("inl", "xl"), route)


def exchange(states, ahead):
    corner = shift(states[2], ahead, ahead)
    column = shift(states[1], 0, ahead)
    return [shift(states[0], ahead, 0), column, corner]


def on_device(traces, dest_tile, bin_in_tile, fold, thresholds):
    devices = lax.axis_size("inl") * lax.axis_size("xl")
    trace_count, samples = traces.shape
    tile_rows, tile_cols = fold.shape
    bins = tile_rows * tile_cols
    width = SLOTS * samples // GROUP + LANES
    (outgoing,) = call(
        route_kernel,
        [((devices * GROUP, width), bf16)],
        dest_tile.reshape(1, trace_count),
        bin_in_tile.reshape(1, trace_count),
        traces,
        far=(0, 1, 2),
        far_outs=(0,),
        limit=LARGE_LIMIT,
        scratch=[
            pltpu.VMEM((1, trace_count), jnp.int32),
            pltpu.VMEM((1, trace_count), jnp.int32),
            pltpu.VMEM((trace_count, samples), bf16),
            pltpu.VMEM((devices * GROUP, width), bf16),
            pltpu.SemaphoreType.DMA((6,)),
            pltpu.SemaphoreType.DMA((4,)),
        ],
    )
    arrived = lax.all_to_all(
        outgoing.reshape(devices, GROUP, width), ("inl", "xl"), split_axis=0, concat_axis=0, tiled=True
    ).reshape(devices * GROUP, width)
    scale = (1.0 / jnp.sqrt(fold.astype(f32))).reshape(bins, 1)

    main, following = time_parts()
    time_matrix = np.concatenate([triple(main, 0), triple(following, 0)], 0)
    back_main, back_last = main.T, np.pad(following.T, ((0, 0), (0, BLOCK - LANES)))
    time_back = np.concatenate([triple(back_main, 0), triple(back_last, 0)], 0)
    time_back_low = np.concatenate([triple(back_main[:LANES], 0), triple(back_last[:LANES], 0)], 0)
    half, rows2, cols2 = samples // 2, tile_rows // 4, tile_cols // 4
    quarter, last = bins // 4, bins // 16
    own0, edge0, own1, edge1, states01, sizes = joint_matrices(tile_rows, tile_cols)
    assert rows2 == SIDE and cols2 >= SIDE
    bands2, back2 = side_matrices(rows2, cols2)
    count0 = sum(sizes[:3])
    joint_shapes = [
        ((2 * sizes[0] + sizes[3], half), f32),
        ((2 * sizes[1] + sizes[4], half), f32),
        ((sizes[2] + 8, half), f32),
    ]

    summed, *states = call(
        bin_kernel,
        [((bins, samples), f32)] + joint_shapes,
        arrived,
        scale,
        time_matrix,
        triple(states01, 1),
        far=(0,),
        limit=MIDDLE_LIMIT,
        scratch=[pltpu.VMEM((devices * GROUP, width), bf16), pltpu.SemaphoreType.DMA((4,))],
    )
    states = exchange(states, 1)
    own_low, own_high, own_next = call(
        own_kernel,
        [((bins, half), f32)] * 2 + [((quarter, half), f32)],
        summed,
        time_matrix,
        triple(own0, 1),
        triple(own1, 1),
        cost=1e9,
    )
    rows_all = rows2 + 2 * SIDE
    shrunk1, timed = call(
        middle_kernel,
        [((quarter, half), f32), ((last, half // 2), f32)],
        thresholds,
        own_next,
        triple(edge1, 1),
        *states,
        time_matrix,
        smem=(0,),
    )
    before, behind = shift(timed, -1, 0), shift(timed, 1, 0)
    low_details, high_details, low_states, high_states, next_details = call(
        details_kernel,
        [((bins - quarter, half), f32), ((bins, half), f32)]
        + [((count0, half), f32)] * 2
        + [((quarter, half), f32)],
        thresholds,
        own_low,
        own_high,
        triple(edge0, 1),
        *states,
        triple(edge0[quarter:].T, 1),
        triple(edge0.T, 1),
        shrunk1,
        time_back,
        smem=(0,),
        after=(timed,),
        cost=1e9,
    )
    stack, firsts, lasts = call(
        functools.partial(sides_kernel, cols2),
        [((rows_all * size, samples // 4), f32) for size in (cols2, SIDE, SIDE)],
        before,
        timed,
        behind,
        after=(low_details,),
    )
    left, right = shift(lasts, 0, -1), shift(firsts, 0, 1)
    bands1, *states = call(
        deepest_kernel,
        [((quarter, half), f32)] + joint_shapes,
        thresholds,
        left,
        stack,
        right,
        triple(bands2, 1),
        triple(back2, 1),
        time_back,
        time_back_low,
        next_details,
        low_states,
        high_states,
        triple(edge1.T, 1),
        smem=(0,),
    )
    states = exchange(states, -1)
    (own_back,) = call(
        own_back_kernel,
        [((bins, samples), f32)],
        low_details,
        high_details,
        bands1,
        triple(own0[quarter:].T, 1),
        triple(own0.T, 1),
        triple(own1.T, 1),
        time_back,
        scale,
        cost=1e9,
    )
    (denoised,) = call(
        final_kernel,
        [((bins, samples), f32)],
        own_back,
        *states,
        time_back,
        time_back_low,
        triple(states01.T, 1),
        scale,
        far_outs=(0,),
        scratch=[pltpu.VMEM((bins, samples), f32), pltpu.SemaphoreType.DMA((samples // BLOCK,))],
    )
    return denoised.reshape(tile_rows, tile_cols, samples)


def solution(mesh):
    placed = (P(("inl", "xl"), None), P(("inl", "xl"), None), P(("inl", "xl")), P("inl", "xl"), P())
    return jax.shard_map(
        on_device, mesh=mesh, in_specs=placed, out_specs=P("inl", "xl", None), check_vma=False
    )
```

```python
import functools

import jax
import jax.numpy as jnp
import ml_dtypes
import numpy as np
from jax import lax
from jax.experimental import pallas as pl
from jax.experimental.pallas import tpu as pltpu
from jax.sharding import PartitionSpec as P

LEVELS = 3
SLOTS = 6
GROUP = 8
LANES = 128
BLOCK = 256
VMEM_LIMIT = 32 * 1024 * 1024
LARGE_LIMIT = 62 * 1024 * 1024
MIDDLE_LIMIT = 48 * 1024 * 1024
TOP_CODE = 32767.0
LAST_MARK = 880.0
SIDE = 4

low_taps = [
    0.0352262918857095,
    -0.0854412738820267,
    -0.1350110200102546,
    0.4598775021184914,
    0.8068915093110924,
    0.3326705529500826,
]
high_taps = [(-1) ** offset * low_taps[5 - offset] for offset in range(6)]

bf16 = jnp.bfloat16
f32 = jnp.float32


def halves(matrix):
    top = np.asarray(matrix, np.float32).astype(ml_dtypes.bfloat16)
    rest = (np.asarray(matrix, np.float64) - top.astype(np.float64)).astype(ml_dtypes.bfloat16)
    return top, rest


def triple(matrix, axis):
    top, rest = halves(matrix)
    return np.concatenate([top, top, rest], axis)


def line_parts(length):
    half = length // 2
    whole = np.zeros((length, length + 4))
    for m in range(half):
        for k in range(6):
            whole[m, 2 * m + k] = low_taps[k]
            whole[half + m, 2 * m + k] = high_taps[k]
    left, sizes, right = np.linalg.svd(whole[:, length:])
    assert sizes[2] < 1e-9
    state = np.zeros((2, length))
    state[:, :4] = right[:2]
    return whole[:, :length], left[:, :2] * sizes[:2], state


def outer(on_rows, on_cols, banded):
    both = np.einsum("ar,bc->abrc", on_rows, on_cols)
    a, b, r, c = both.shape
    if banded:
        both = both.reshape(2, a // 2, 2, b // 2, r, c).transpose(2, 0, 1, 3, 4, 5)
    return both.reshape(a * b, r * c)


def two_levels(length):
    own0, edge0, state0 = line_parts(length)
    own1, edge1, state1 = line_parts(length // 2)
    low = slice(0, length // 2)
    assert np.abs(state1 @ edge0[low]).max() < 1e-9
    further = state1 @ own0[low]
    return dict(
        own0=own0,
        edge0=edge0,
        state0=state0,
        own1=own1 @ own0[low],
        far1=own1 @ edge0[low],
        edge1=edge1,
        further=further,
        states=np.concatenate([state0, further]),
    )


def joint_matrices(rows, cols):
    i, c = two_levels(rows), two_levels(cols)
    wide = [np.concatenate([d["edge0"], np.zeros_like(d["edge0"])], 1) for d in (i, c)]
    both = [np.concatenate([d["far1"], d["edge1"]], 1) for d in (i, c)]
    first = [0, 1, 4, 5] + [k for k in range(16) if k not in (0, 1, 4, 5)]
    own0 = outer(i["own0"], c["own0"], True)
    edge0 = [outer(i["edge0"], c["own0"], True), outer(i["own0"], c["edge0"], True), outer(*wide, True)[:, first]]
    own1 = outer(i["own1"], c["own1"], True)
    edge1 = [
        outer(i["far1"], c["own1"], True),
        outer(i["own1"], c["far1"], True),
        outer(*both, True)[:, first],
        outer(i["edge1"], np.eye(cols // 2), True),
        outer(np.eye(rows // 2), c["edge1"], True),
    ]
    states = [
        outer(i["state0"], np.eye(cols), False),
        outer(np.eye(rows), c["state0"], False),
        outer(i["states"], c["states"], False)[first],
        outer(i["further"], c["own1"], False),
        outer(i["own1"], c["further"], False),
    ]
    sizes = [len(part) for part in states]
    return own0, np.concatenate(edge0, 1), own1, np.concatenate(edge1, 1), np.concatenate(states, 0), sizes


def side_parts(length):
    firsts = range(-SIDE // 2, length // 2)
    count = len(firsts)
    bands = np.zeros((2 * count, length + 2 * SIDE))
    back = np.zeros((length, 2 * count))
    for m, first in enumerate(firsts):
        for k in range(6):
            for part, taps in ((0, low_taps), (count, high_taps)):
                bands[part + m, SIDE + 2 * first + k] = taps[k]
                if 0 <= 2 * first + k < length:
                    back[2 * first + k, part + m] = taps[k]
    return bands, back


def side_matrices(rows, cols):
    bands_i, back_i = side_parts(rows)
    bands_c, back_c = side_parts(cols)
    bands = outer(bands_i, bands_c, True)
    wide = cols + 2 * SIDE
    order = []
    for first, size in ((0, SIDE), (SIDE, cols), (SIDE + cols, SIDE)):
        order += [r * wide + first + c for r in range(rows + 2 * SIDE) for c in range(size)]
    back = outer(back_i.T, back_c.T, True).T
    return bands[:, order], back


def time_parts():
    whole = np.zeros((BLOCK + LANES, BLOCK))
    for m in range(LANES):
        for k in range(6):
            whole[2 * m + k, m] = low_taps[k]
            whole[2 * m + k, LANES + m] = high_taps[k]
    return whole[:BLOCK], whole[BLOCK:]


def split(value):
    top = value.astype(bf16)
    return top, (value - top.astype(f32)).astype(bf16)


def dot(left, right):
    return jnp.dot(left, right, preferred_element_type=f32)


def left_dot(matrix, value):
    top, rest = split(value)
    return dot(matrix, jnp.concatenate([top, rest, top], 0))


def time_analysis(blocks, matrix):
    parts = [split(block) for block in blocks]
    lows, highs = [], []
    for b in range(len(blocks)):
        top, rest = parts[b]
        next_top, next_rest = [part[:, :LANES] for part in parts[(b + 1) % len(blocks)]]
        joined = jnp.concatenate([top, rest, top, next_top, next_rest, next_top], 1)
        result = dot(joined, matrix)
        lows.append(result[:, :LANES])
        highs.append(result[:, LANES:])
    return lows, highs


def time_synthesis(blocks, matrix):
    parts = [split(block) for block in blocks]
    results = []
    for b in range(len(blocks)):
        top, rest = parts[b]
        last_top, last_rest = parts[b - 1]
        joined = jnp.concatenate([top, rest, top, last_top, last_rest, last_top], 1)
        results.append(dot(joined, matrix))
    return results


def synthesis_from_low(lows, matrix):
    parts = [split(low) for low in lows]
    results = []
    for b in range(len(lows)):
        top, rest = parts[b]
        last_top, last_rest = parts[b - 1]
        joined = jnp.concatenate([top, rest, top, last_top, last_rest, last_top], 1)
        results.append(dot(joined, matrix))
    return results


def shrink(value, limit):
    return value - jnp.clip(value, -limit, limit)


def tail_rows(rows, count):
    row = lax.broadcasted_iota(jnp.int32, (rows, count), 0)
    tail = lax.broadcasted_iota(jnp.int32, (rows, count), 1)
    each = GROUP - SLOTS
    return (row == tail // each * GROUP + SLOTS + tail % each).astype(f32).astype(bf16)


def route_kernel(dest_far, bin_far, traces_far, out_far, dest_ref, bin_ref, traces_ref, out_ref, in_sems, out_sems):
    traces, samples = traces_ref.shape
    rows = out_ref.shape[0]
    tiles = rows // GROUP
    span = samples // 4
    coming = [
        pltpu.make_async_copy(dest_far, dest_ref, in_sems.at[4]),
        pltpu.make_async_copy(bin_far, bin_ref, in_sems.at[5]),
    ]
    for j in (3, 0, 1, 2):
        at = pl.ds(j * span, span)
        coming.append(pltpu.make_async_copy(traces_far.at[:, at], traces_ref.at[:, at], in_sems.at[j]))
    for copy in coming:
        copy.start()
    before = lax.broadcasted_iota(jnp.int32, (traces, traces), 0) <= lax.broadcasted_iota(
        jnp.int32, (traces, traces), 1
    )
    before = before.astype(f32).astype(bf16)
    coming[0].wait()
    coming[1].wait()
    dest = dest_ref[...]
    matches = lax.broadcasted_iota(jnp.int32, (tiles, traces), 0) == dest
    counts = dot(matches.astype(f32).astype(bf16), before)
    place = jnp.sum(jnp.where(matches, counts, 0.0), 0, keepdims=True).astype(jnp.int32) - 1
    row_at = lax.broadcasted_iota(jnp.int32, (rows, traces), 0)
    main = (row_at == dest * GROUP + place).astype(f32).astype(bf16)
    going = []

    def send(number, first, width):
        at = pl.ds(first, width)
        going.append(pltpu.make_async_copy(out_ref.at[:, at], out_far.at[:, at], out_sems.at[number]))
        going[-1].start()

    code = bin_ref[...] + 1
    lane = lax.broadcasted_iota(jnp.int32, (LANES, traces), 0)
    digits = jnp.where(lane == 0, code // 2, jnp.where(lane == 1, code % 2, 0))
    labels = lax.dot_general(
        main,
        digits.astype(f32).astype(bf16),
        (((1,), (1,)), ((), ())),
        preferred_element_type=f32,
    )
    out_ref[:, 3 * span :] = labels.astype(bf16)
    send(3, 3 * span, LANES)
    count = GROUP - SLOTS
    tail_at = lax.broadcasted_iota(jnp.int32, (count * tiles, traces), 0)
    put = tail_rows(rows, count * tiles)
    coming[2].wait()
    tail = traces_ref[:, 3 * span : samples]
    for j in range(3):
        tail_row = jnp.where(place == j, 0, jnp.where(place == 3 + j, 1, -rows))
        extra = (tail_at == dest * count + tail_row).astype(f32).astype(bf16)
        rest = dot(extra, tail).astype(bf16)
        at = slice(j * span, (j + 1) * span)
        coming[3 + j].wait()
        both = jnp.concatenate([traces_ref[:, at], rest], 0)
        out_ref[:, at] = dot(jnp.concatenate([main, put], 1), both).astype(bf16)
        send(j, j * span, span)
    for copy in going:
        copy.wait()


def bin_kernel(sizes, arrived_far, scale_ref, time_ref, state_ref, summed_ref, s0, s1, s2, arrived_ref, sems):
    outs = (s0, s1, s2)
    width = summed_ref.shape[1] // 4
    coming = []
    for j, (first, size) in enumerate([(3 * width, LANES)] + [(j * width, width) for j in range(3)]):
        at = pl.ds(first, size)
        coming.append(pltpu.make_async_copy(arrived_far.at[:, at], arrived_ref.at[:, at], sems.at[j]))
        coming[-1].start()
    coming[0].wait()
    rows = arrived_ref.shape[0]
    bins, samples = summed_ref.shape
    span = samples // 4
    labels = arrived_ref[:, 3 * span :]
    lane = lax.broadcasted_iota(jnp.int32, (GROUP, LANES), 1)
    weights = jnp.where(lane == 0, 2.0, jnp.where(lane == 1, 1.0, 0.0)).astype(bf16)
    code = lax.dot_general(
        weights, labels, (((1,), (1,)), ((), ())), preferred_element_type=f32
    ).astype(jnp.int32)
    at = lax.broadcasted_iota(jnp.int32, (GROUP, rows), 1) % GROUP
    code = jnp.where(at < SLOTS, code, 0) - 1
    bin_at = lax.broadcasted_iota(jnp.int32, (bins, rows), 0)
    main = (bin_at == code[:1]).astype(f32).astype(bf16)
    scale = scale_ref[...]
    pieces = []
    for j in range(3):
        coming[1 + j].wait()
        pieces.append(dot(main, arrived_ref[:, j * span : (j + 1) * span]))
    last = None
    for j in range(3):
        first = pltpu.roll(code, SLOTS - j, 1)
        second = pltpu.roll(code, SLOTS + 1 - 3 - j, 1)
        tail_code = jnp.where(at == SLOTS, first, jnp.where(at == SLOTS + 1, second, -1))
        onehot = (bin_at == tail_code[:1]).astype(f32).astype(bf16)
        term = dot(onehot, arrived_ref[:, j * span : (j + 1) * span])
        last = term if last is None else last + term
    pieces.append(last)
    matrix = state_ref[...]
    blocks = []
    for p, piece in enumerate(pieces):
        piece = piece * scale
        summed_ref[:, p * span : (p + 1) * span] = piece
        states = left_dot(matrix, piece)
        blocks += [states[:, b : b + BLOCK] for b in range(0, span, BLOCK)]
    lows, highs = time_analysis(blocks, time_ref[...])
    put_joint(sizes, outs, lows, highs)


def encode(pieces, out):
    lane = lax.broadcasted_iota(jnp.int32, (out.shape[0], LANES), 1)
    marks = jnp.zeros((out.shape[0], LANES), f32)
    for b, piece in enumerate(pieces):
        largest = jnp.max(jnp.abs(piece), 1, keepdims=True)
        mark = jnp.clip(jnp.ceil(jnp.log2(largest) * 8.0), -LAST_MARK, LAST_MARK)
        code = jnp.clip(jnp.round(piece * (jnp.exp2(mark * -0.125) * TOP_CODE)), -TOP_CODE, TOP_CODE)
        out[:, b * LANES : (b + 1) * LANES] = code.astype(jnp.int32).astype(jnp.int16)
        marks = jnp.where(lane == b, mark, marks)
    out[:, len(pieces) * LANES :] = marks.astype(jnp.int32).astype(jnp.int16)


def scales_of(refs):
    marks = [ref[:, ref.shape[1] - LANES :].astype(jnp.int32).astype(f32) for ref in refs]
    return [jnp.exp2(mark * 0.125) * (1.0 / TOP_CODE) for mark in marks]


def decode(ref, scale, where):
    pieces = []
    for start in range(where.start, where.stop, LANES):
        b = start // LANES
        code = ref[:, start : start + LANES].astype(jnp.int32).astype(f32)
        pieces.append(code * scale[:, b : b + 1])
    return jnp.concatenate(pieces, 1)


def put_joint(sizes, outs, lows, highs):
    ends = np.cumsum([0] + sizes)
    part = [slice(int(ends[k]), int(ends[k + 1])) for k in range(5)]

    def message(rows, *pieces):
        spare = rows - sum(piece.shape[0] for piece in pieces)
        if spare:
            pieces += (jnp.zeros((spare, LANES), f32),)
        return jnp.concatenate(pieces, 0)

    rows = [out.shape[0] for out in outs]
    pairs = list(zip(lows, highs))
    encode([message(rows[0], low[part[0]], high[part[0]], low[part[3]]) for low, high in pairs], outs[0])
    encode([message(rows[1], low[part[1]], high[part[1]], low[part[4]]) for low, high in pairs], outs[1])
    encode([message(rows[2], low[part[2]], high[part[2]][:8]) for low, high in pairs], outs[2])


def take_joint(sizes, refs, scales, where):
    r, c, d, further_r, further_c = sizes
    m0, m1, m2 = [decode(ref, scale, where) for ref, scale in zip(refs, scales)]
    low = [m0[:r], m1[:c], m2[:d], m0[2 * r : 2 * r + further_r], m1[2 * c : 2 * c + further_c]]
    high = [m0[r : 2 * r], m1[c : 2 * c], m2[d : d + 8], jnp.zeros((d - 8, m2.shape[1]), f32)]
    return jnp.concatenate(low, 0), jnp.concatenate(high, 0)


def join_rows(refs, where):
    return jnp.concatenate([ref[:, where] for ref in refs], 0)


def steps(ref):
    return [slice(start, start + BLOCK) for start in range(0, ref.shape[1], BLOCK)]


def own_kernel(summed_ref, time_ref, own_ref, next_ref, low_ref, high_ref, next_out):
    blocks = [summed_ref[:, where] for where in steps(summed_ref)]
    lows, highs = time_analysis(blocks, time_ref[...])
    for b in range(0, len(blocks), 2):
        where = slice(b * LANES, (b + 2) * LANES)
        low = jnp.concatenate([lows[b], lows[b + 1]], 1)
        next_out[:, where] = left_dot(next_ref[...], low)
        low_ref[:, where] = left_dot(own_ref[...], low)
        high_ref[:, where] = left_dot(own_ref[...], jnp.concatenate([highs[b], highs[b + 1]], 1))


def middle_kernel(sizes, thr_ref, own_ref, edge_ref, s0, s1, s2, time_ref, shrunk_ref, timed_ref):
    quarter = shrunk_ref.shape[0] // 4
    half = shrunk_ref.shape[1] // 2
    matrix = edge_ref[...]
    blocks = []
    refs = (s0, s1, s2)
    scales = scales_of(refs)
    for where in steps(own_ref):
        low, _ = take_joint(sizes, refs, scales, where)
        blocks.append(own_ref[:, where] + left_dot(matrix, low))
    lows, highs = time_analysis(blocks, time_ref[...])
    for b in range(len(blocks)):
        for base, piece, high in ((0, lows[b], 0), (half, highs[b], 1)):
            where = slice(base + b * LANES, base + (b + 1) * LANES)
            for q in range(4):
                at = slice(q * quarter, (q + 1) * quarter)
                if q or high:
                    shrunk_ref[at, where] = shrink(piece[at], thr_ref[1, 2 * q + high - 1])
                else:
                    shrunk_ref[at, where] = jnp.zeros_like(piece[at])
    coarse = [jnp.concatenate([lows[b][:quarter], lows[b + 1][:quarter]], 1) for b in range(0, len(lows), 2)]
    lows, highs = time_analysis(coarse, time_ref[...])
    for b in range(len(coarse)):
        for base, piece in ((0, lows[b]), (half // 2, highs[b])):
            timed_ref[:, base + b * LANES : base + (b + 1) * LANES] = piece


def sides_kernel(cols, before, own, after, stack_out, first_out, last_out):
    stack_out[...] = jnp.concatenate([before[...], own[...], after[...]], 0)
    starts = range(0, stack_out.shape[0], cols)
    first_out[...] = jnp.concatenate([stack_out[at : at + SIDE] for at in starts], 0)
    last_out[...] = jnp.concatenate([stack_out[at + cols - SIDE : at + cols] for at in starts], 0)


def details_kernel(
    sizes,
    thr_ref,
    low_in,
    high_in,
    edge_ref,
    s0,
    s1,
    s2,
    back_low,
    back_ref,
    next_in,
    time_t,
    low_out,
    high_out,
    low_states,
    high_states,
    next_out,
):
    for b, block in enumerate(time_pairs(next_in[...], time_t[...])):
        next_out[:, b * BLOCK : (b + 1) * BLOCK] = block
    quarter = low_in.shape[0] // 4
    refs = (s0, s1, s2)
    scales = scales_of(refs)
    for where in steps(low_in):
        low, high = take_joint(sizes, refs, scales, where)
        bands = low_in[quarter:, where] + left_dot(edge_ref[quarter:], low[: high.shape[0]])
        bands = [shrink(bands[(q - 1) * quarter : q * quarter], thr_ref[0, 2 * q - 1]) for q in range(1, 4)]
        bands = jnp.concatenate(bands, 0)
        low_out[:, where] = bands
        low_states[:, where] = left_dot(back_low[...], bands)
        bands = high_in[:, where] + left_dot(edge_ref[...], high)
        bands = [shrink(bands[q * quarter : (q + 1) * quarter], thr_ref[0, 2 * q]) for q in range(4)]
        bands = jnp.concatenate(bands, 0)
        high_out[:, where] = bands
        high_states[:, where] = left_dot(back_ref[...], bands)


def time_pairs(bands, matrix):
    half = bands.shape[1] // 2
    pairs = []
    for b in range(0, half, LANES):
        pairs.append(jnp.concatenate([bands[:, b : b + LANES], bands[:, half + b : half + b + LANES]], 1))
    return time_synthesis(pairs, matrix)


def deepest_kernel(
    sizes, thr_ref, before, own, after, bands_m, back_m, time_t, time_low, next_in, low_states, high_states, back_ref, next_out, *outs
):
    stack = jnp.concatenate([before[...], own[...], after[...]], 0)
    bands = left_dot(bands_m[...], stack)
    row = lax.broadcasted_iota(jnp.int32, bands.shape, 0)
    high = lax.broadcasted_iota(jnp.int32, bands.shape, 1) >= bands.shape[1] // 2
    limit = jnp.where(high, thr_ref[2, 0], 0.0)
    quarter = bands.shape[0] // 4
    for q in range(1, 4):
        limit = jnp.where(row >= q * quarter, jnp.where(high, thr_ref[2, 2 * q], thr_ref[2, 2 * q - 1]), limit)
    rebuilt = left_dot(back_m[...], shrink(bands, limit))
    lows = []
    for block in time_pairs(rebuilt, time_t[...]):
        lows += [block[:, b : b + LANES] for b in range(0, BLOCK, LANES)]
    rows = rebuilt.shape[0]
    count = low_states.shape[0]
    state_lows, state_highs = [], []
    for b, block in enumerate(synthesis_from_low(lows, time_low[...])):
        where = slice(b * BLOCK, (b + 1) * BLOCK)
        bands = jnp.concatenate([next_in[:rows, where] + block, next_in[rows:, where]], 0)
        next_out[:, where] = bands
        states = left_dot(back_ref[...], bands)
        low = jnp.concatenate([states[:count] + low_states[:, where], states[count:]], 0)
        for at in range(0, BLOCK, LANES):
            state_lows.append(low[:, at : at + LANES])
            state_highs.append(high_states[:, where.start + at : where.start + at + LANES])
    put_joint(sizes, outs, state_lows, state_highs)


def own_back_kernel(low_in, high_in, next_in, low_t, high_t, next_t, time_t, scale_ref, out_ref):
    blocks = []
    for where in steps(low_in):
        low = left_dot(low_t[...], low_in[:, where]) + left_dot(next_t[...], next_in[:, where])
        high = left_dot(high_t[...], high_in[:, where])
        for b in range(0, BLOCK, LANES):
            blocks.append(jnp.concatenate([low[:, b : b + LANES], high[:, b : b + LANES]], 1))
    scale = scale_ref[...]
    for b, block in enumerate(time_synthesis(blocks, time_t[...])):
        out_ref[:, b * BLOCK : (b + 1) * BLOCK] = block * scale


def final_kernel(sizes, own_ref, s0, s1, s2, time_t, time_low, state_t, scale_ref, out_far, out_ref, sems):
    pairs, lows = [], []
    refs = (s0, s1, s2)
    scales = scales_of(refs)
    for start in range(0, own_ref.shape[1] // 2, LANES):
        low, high = take_joint(sizes, refs, scales, slice(start, start + LANES))
        count = high.shape[0]
        pairs.append(jnp.concatenate([low[:count], high], 1))
        lows.append(low[count:])
    level0 = time_synthesis(pairs, time_t[...])
    level1 = synthesis_from_low(lows, time_low[...])
    scale = scale_ref[...]
    going = []
    for b in range(len(pairs)):
        where = slice(b * BLOCK, (b + 1) * BLOCK)
        states = jnp.concatenate([level0[b], level1[b]], 0)
        out_ref[:, where] = own_ref[:, where] + left_dot(state_t[...], states) * scale
        going.append(pltpu.make_async_copy(out_ref.at[:, where], out_far.at[:, where], sems.at[b]))
        going[-1].start()
    for copy in going:
        copy.wait()


def call(kernel, outs, *args, smem=(), far=(), far_outs=(), scratch=(), after=(), cost=None, limit=VMEM_LIMIT):
    spaces = [pltpu.SMEM if i in smem else pltpu.HBM if i in far else pltpu.VMEM for i in range(len(args))]
    spaces += [pl.ANY] * len(after)
    count = len(args)

    def body(*refs):
        kernel(*refs[:count], *refs[count + len(after) :])

    return pl.pallas_call(
        body,
        out_shape=[jax.ShapeDtypeStruct(shape, dtype) for shape, dtype in outs],
        in_specs=[pl.BlockSpec(memory_space=space) for space in spaces],
        out_specs=[
            pl.BlockSpec(memory_space=pltpu.HBM if i in far_outs else pltpu.VMEM) for i in range(len(outs))
        ],
        scratch_shapes=list(scratch),
        compiler_params=pltpu.CompilerParams(vmem_limit_bytes=limit),
        cost_estimate=None
        if cost is None
        else pl.CostEstimate(flops=int(cost), bytes_accessed=0, transcendentals=0),
    )(*args, *after)


def shift(block, inline_by, cross_by):
    inline_devs, cross_devs = lax.axis_size("inl"), lax.axis_size("xl")
    if not cross_by:
        return lax.ppermute(block, "inl", [((i + inline_by) % inline_devs, i) for i in range(inline_devs)])
    if not inline_by:
        return lax.ppermute(block, "xl", [((j + cross_by) % cross_devs, j) for j in range(cross_devs)])
    route = [
        ((i + inline_by) % inline_devs * cross_devs + (j + cross_by) % cross_devs, i * cross_devs + j)
        for i in range(inline_devs)
        for j in range(cross_devs)
    ]
    return lax.ppermute(block, ("inl", "xl"), route)


def exchange(states, ahead):
    corner = shift(states[2], ahead, ahead)
    column = shift(states[1], 0, ahead)
    return [shift(states[0], ahead, 0), column, corner]


def on_device(traces, dest_tile, bin_in_tile, fold, thresholds):
    devices = lax.axis_size("inl") * lax.axis_size("xl")
    trace_count, samples = traces.shape
    tile_rows, tile_cols = fold.shape
    bins = tile_rows * tile_cols
    width = SLOTS * samples // GROUP + LANES
    (outgoing,) = call(
        route_kernel,
        [((devices * GROUP, width), bf16)],
        dest_tile.reshape(1, trace_count),
        bin_in_tile.reshape(1, trace_count),
        traces,
        far=(0, 1, 2),
        far_outs=(0,),
        limit=LARGE_LIMIT,
        scratch=[
            pltpu.VMEM((1, trace_count), jnp.int32),
            pltpu.VMEM((1, trace_count), jnp.int32),
            pltpu.VMEM((trace_count, samples), bf16),
            pltpu.VMEM((devices * GROUP, width), bf16),
            pltpu.SemaphoreType.DMA((6,)),
            pltpu.SemaphoreType.DMA((4,)),
        ],
    )
    arrived = lax.all_to_all(
        outgoing.reshape(devices, GROUP, width), ("inl", "xl"), split_axis=0, concat_axis=0, tiled=True
    ).reshape(devices * GROUP, width)
    scale = (1.0 / jnp.sqrt(fold.astype(f32))).reshape(bins, 1)

    main, following = time_parts()
    time_matrix = np.concatenate([triple(main, 0), triple(following, 0)], 0)
    back_main, back_last = main.T, np.pad(following.T, ((0, 0), (0, BLOCK - LANES)))
    time_back = np.concatenate([triple(back_main, 0), triple(back_last, 0)], 0)
    time_back_low = np.concatenate([triple(back_main[:LANES], 0), triple(back_last[:LANES], 0)], 0)
    half, rows2, cols2 = samples // 2, tile_rows // 4, tile_cols // 4
    quarter, last = bins // 4, bins // 16
    own0, edge0, own1, edge1, states01, sizes = joint_matrices(tile_rows, tile_cols)
    assert rows2 == SIDE and cols2 >= SIDE
    bands2, back2 = side_matrices(rows2, cols2)
    count0 = sum(sizes[:3])
    joint_rows = [2 * sizes[0] + sizes[3], 2 * sizes[1] + sizes[4], sizes[2] + 8]
    joint_shapes = [((-(-rows // 16) * 16, half + LANES), jnp.int16) for rows in joint_rows]

    summed, *states = call(
        functools.partial(bin_kernel, sizes),
        [((bins, samples), f32)] + joint_shapes,
        arrived,
        scale,
        time_matrix,
        triple(states01, 1),
        far=(0,),
        limit=MIDDLE_LIMIT,
        scratch=[pltpu.VMEM((devices * GROUP, width), bf16), pltpu.SemaphoreType.DMA((4,))],
    )
    states = exchange(states, 1)
    own_low, own_high, own_next = call(
        own_kernel,
        [((bins, half), f32)] * 2 + [((quarter, half), f32)],
        summed,
        time_matrix,
        triple(own0, 1),
        triple(own1, 1),
        cost=1e9,
    )
    rows_all = rows2 + 2 * SIDE
    shrunk1, timed = call(
        functools.partial(middle_kernel, sizes),
        [((quarter, half), f32), ((last, half // 2), f32)],
        thresholds,
        own_next,
        triple(edge1, 1),
        *states,
        time_matrix,
        smem=(0,),
    )
    before, behind = shift(timed, -1, 0), shift(timed, 1, 0)
    low_details, high_details, low_states, high_states, next_details = call(
        functools.partial(details_kernel, sizes),
        [((bins - quarter, half), f32), ((bins, half), f32)]
        + [((count0, half), f32)] * 2
        + [((quarter, half), f32)],
        thresholds,
        own_low,
        own_high,
        triple(edge0, 1),
        *states,
        triple(edge0[quarter:].T, 1),
        triple(edge0.T, 1),
        shrunk1,
        time_back,
        smem=(0,),
        after=(timed,),
        cost=1e9,
    )
    stack, firsts, lasts = call(
        functools.partial(sides_kernel, cols2),
        [((rows_all * size, samples // 4), f32) for size in (cols2, SIDE, SIDE)],
        before,
        timed,
        behind,
        after=(low_details,),
    )
    left, right = shift(lasts, 0, -1), shift(firsts, 0, 1)
    bands1, *states = call(
        functools.partial(deepest_kernel, sizes),
        [((quarter, half), f32)] + joint_shapes,
        thresholds,
        left,
        stack,
        right,
        triple(bands2, 1),
        triple(back2, 1),
        time_back,
        time_back_low,
        next_details,
        low_states,
        high_states,
        triple(edge1.T, 1),
        smem=(0,),
    )
    states = exchange(states, -1)
    (own_back,) = call(
        own_back_kernel,
        [((bins, samples), f32)],
        low_details,
        high_details,
        bands1,
        triple(own0[quarter:].T, 1),
        triple(own0.T, 1),
        triple(own1.T, 1),
        time_back,
        scale,
        cost=1e9,
    )
    (denoised,) = call(
        functools.partial(final_kernel, sizes),
        [((bins, samples), f32)],
        own_back,
        *states,
        time_back,
        time_back_low,
        triple(states01.T, 1),
        scale,
        far_outs=(0,),
        scratch=[pltpu.VMEM((bins, samples), f32), pltpu.SemaphoreType.DMA((samples // BLOCK,))],
    )
    return denoised.reshape(tile_rows, tile_cols, samples)


def solution(mesh):
    placed = (P(("inl", "xl"), None), P(("inl", "xl"), None), P(("inl", "xl")), P("inl", "xl"), P())
    return jax.shard_map(
        on_device, mesh=mesh, in_specs=placed, out_specs=P("inl", "xl", None), check_vma=False
    )
```

```python
import functools

import jax
import jax.numpy as jnp
import ml_dtypes
import numpy as np
from jax import lax
from jax.experimental import pallas as pl
from jax.experimental.pallas import tpu as pltpu
from jax.sharding import PartitionSpec as P

LEVELS = 3
SLOTS = 6
GROUP = 8
LANES = 128
BLOCK = 256
VMEM_LIMIT = 32 * 1024 * 1024
LARGE_LIMIT = 62 * 1024 * 1024
MIDDLE_LIMIT = 48 * 1024 * 1024
TOP_CODE = 32767.0
LAST_MARK = 880.0
SIDE = 4

low_taps = [
    0.0352262918857095,
    -0.0854412738820267,
    -0.1350110200102546,
    0.4598775021184914,
    0.8068915093110924,
    0.3326705529500826,
]
high_taps = [(-1) ** offset * low_taps[5 - offset] for offset in range(6)]

bf16 = jnp.bfloat16
f32 = jnp.float32


def halves(matrix):
    top = np.asarray(matrix, np.float32).astype(ml_dtypes.bfloat16)
    rest = (np.asarray(matrix, np.float64) - top.astype(np.float64)).astype(ml_dtypes.bfloat16)
    return top, rest


def triple(matrix, axis):
    top, rest = halves(matrix)
    return np.concatenate([top, top, rest], axis)


def line_parts(length):
    half = length // 2
    whole = np.zeros((length, length + 4))
    for m in range(half):
        for k in range(6):
            whole[m, 2 * m + k] = low_taps[k]
            whole[half + m, 2 * m + k] = high_taps[k]
    left, sizes, right = np.linalg.svd(whole[:, length:])
    assert sizes[2] < 1e-9
    state = np.zeros((2, length))
    state[:, :4] = right[:2]
    return whole[:, :length], left[:, :2] * sizes[:2], state


def outer(on_rows, on_cols, banded):
    both = np.einsum("ar,bc->abrc", on_rows, on_cols)
    a, b, r, c = both.shape
    if banded:
        both = both.reshape(2, a // 2, 2, b // 2, r, c).transpose(2, 0, 1, 3, 4, 5)
    return both.reshape(a * b, r * c)


def two_levels(length):
    own0, edge0, state0 = line_parts(length)
    own1, edge1, state1 = line_parts(length // 2)
    low = slice(0, length // 2)
    assert np.abs(state1 @ edge0[low]).max() < 1e-9
    further = state1 @ own0[low]
    return dict(
        own0=own0,
        edge0=edge0,
        state0=state0,
        own1=own1 @ own0[low],
        far1=own1 @ edge0[low],
        edge1=edge1,
        further=further,
        states=np.concatenate([state0, further]),
    )


def joint_matrices(rows, cols):
    i, c = two_levels(rows), two_levels(cols)
    wide = [np.concatenate([d["edge0"], np.zeros_like(d["edge0"])], 1) for d in (i, c)]
    both = [np.concatenate([d["far1"], d["edge1"]], 1) for d in (i, c)]
    first = [0, 1, 4, 5] + [k for k in range(16) if k not in (0, 1, 4, 5)]
    own0 = outer(i["own0"], c["own0"], True)
    edge0 = [outer(i["edge0"], c["own0"], True), outer(i["own0"], c["edge0"], True), outer(*wide, True)[:, first]]
    own1 = outer(i["own1"], c["own1"], True)
    edge1 = [
        outer(i["far1"], c["own1"], True),
        outer(i["own1"], c["far1"], True),
        outer(*both, True)[:, first],
        outer(i["edge1"], np.eye(cols // 2), True),
        outer(np.eye(rows // 2), c["edge1"], True),
    ]
    states = [
        outer(i["state0"], np.eye(cols), False),
        outer(np.eye(rows), c["state0"], False),
        outer(i["states"], c["states"], False)[first],
        outer(i["further"], c["own1"], False),
        outer(i["own1"], c["further"], False),
    ]
    sizes = [len(part) for part in states]
    return own0, np.concatenate(edge0, 1), own1, np.concatenate(edge1, 1), np.concatenate(states, 0), sizes


def side_parts(length):
    firsts = range(-SIDE // 2, length // 2)
    count = len(firsts)
    bands = np.zeros((2 * count, length + 2 * SIDE))
    back = np.zeros((length, 2 * count))
    for m, first in enumerate(firsts):
        for k in range(6):
            for part, taps in ((0, low_taps), (count, high_taps)):
                bands[part + m, SIDE + 2 * first + k] = taps[k]
                if 0 <= 2 * first + k < length:
                    back[2 * first + k, part + m] = taps[k]
    return bands, back


def side_matrices(rows, cols):
    bands_i, back_i = side_parts(rows)
    bands_c, back_c = side_parts(cols)
    bands = outer(bands_i, bands_c, True)
    wide = cols + 2 * SIDE
    order = []
    for first, size in ((0, SIDE), (SIDE, cols), (SIDE + cols, SIDE)):
        order += [r * wide + first + c for r in range(rows + 2 * SIDE) for c in range(size)]
    back = outer(back_i.T, back_c.T, True).T
    return bands[:, order], back


def time_parts():
    whole = np.zeros((BLOCK + LANES, BLOCK))
    for m in range(LANES):
        for k in range(6):
            whole[2 * m + k, m] = low_taps[k]
            whole[2 * m + k, LANES + m] = high_taps[k]
    return whole[:BLOCK], whole[BLOCK:]


def split(value):
    top = value.astype(bf16)
    return top, (value - top.astype(f32)).astype(bf16)


def dot(left, right):
    return jnp.dot(left, right, preferred_element_type=f32)


def left_dot(matrix, value):
    top, rest = split(value)
    return dot(matrix, jnp.concatenate([top, rest, top], 0))


def time_analysis(blocks, matrix):
    parts = [split(block) for block in blocks]
    lows, highs = [], []
    for b in range(len(blocks)):
        top, rest = parts[b]
        next_top, next_rest = [part[:, :LANES] for part in parts[(b + 1) % len(blocks)]]
        joined = jnp.concatenate([top, rest, top, next_top, next_rest, next_top], 1)
        result = dot(joined, matrix)
        lows.append(result[:, :LANES])
        highs.append(result[:, LANES:])
    return lows, highs


def time_synthesis(blocks, matrix):
    parts = [split(block) for block in blocks]
    results = []
    for b in range(len(blocks)):
        top, rest = parts[b]
        last_top, last_rest = parts[b - 1]
        joined = jnp.concatenate([top, rest, top, last_top, last_rest, last_top], 1)
        results.append(dot(joined, matrix))
    return results


def synthesis_from_low(lows, matrix):
    parts = [split(low) for low in lows]
    results = []
    for b in range(len(lows)):
        top, rest = parts[b]
        last_top, last_rest = parts[b - 1]
        joined = jnp.concatenate([top, rest, top, last_top, last_rest, last_top], 1)
        results.append(dot(joined, matrix))
    return results


def shrink(value, limit):
    return value - jnp.clip(value, -limit, limit)


def tail_rows(rows, count):
    row = lax.broadcasted_iota(jnp.int32, (rows, count), 0)
    tail = lax.broadcasted_iota(jnp.int32, (rows, count), 1)
    each = GROUP - SLOTS
    return (row == tail // each * GROUP + SLOTS + tail % each).astype(f32).astype(bf16)


def route_kernel(dest_far, bin_far, traces_far, out_far, dest_ref, bin_ref, traces_ref, out_ref, in_sems, out_sems):
    traces, samples = traces_ref.shape
    rows = out_ref.shape[0]
    tiles = rows // GROUP
    span = samples // 4
    coming = [
        pltpu.make_async_copy(dest_far, dest_ref, in_sems.at[4]),
        pltpu.make_async_copy(bin_far, bin_ref, in_sems.at[5]),
    ]
    for j in (3, 0, 1, 2):
        at = pl.ds(j * span, span)
        coming.append(pltpu.make_async_copy(traces_far.at[:, at], traces_ref.at[:, at], in_sems.at[j]))
    for copy in coming:
        copy.start()
    before = lax.broadcasted_iota(jnp.int32, (traces, traces), 0) <= lax.broadcasted_iota(
        jnp.int32, (traces, traces), 1
    )
    before = before.astype(f32).astype(bf16)
    coming[0].wait()
    coming[1].wait()
    dest = dest_ref[...]
    matches = lax.broadcasted_iota(jnp.int32, (tiles, traces), 0) == dest
    counts = dot(matches.astype(f32).astype(bf16), before)
    place = jnp.sum(jnp.where(matches, counts, 0.0), 0, keepdims=True).astype(jnp.int32) - 1
    row_at = lax.broadcasted_iota(jnp.int32, (rows, traces), 0)
    main = (row_at == dest * GROUP + place).astype(f32).astype(bf16)
    going = []

    def send(number, first, width):
        at = pl.ds(first, width)
        going.append(pltpu.make_async_copy(out_ref.at[:, at], out_far.at[:, at], out_sems.at[number]))
        going[-1].start()

    code = bin_ref[...] + 1
    lane = lax.broadcasted_iota(jnp.int32, (LANES, traces), 0)
    digits = jnp.where(lane == 0, code // 2, jnp.where(lane == 1, code % 2, 0))
    labels = lax.dot_general(
        main,
        digits.astype(f32).astype(bf16),
        (((1,), (1,)), ((), ())),
        preferred_element_type=f32,
    )
    out_ref[:, 3 * span :] = labels.astype(bf16)
    send(3, 3 * span, LANES)
    count = GROUP - SLOTS
    tail_at = lax.broadcasted_iota(jnp.int32, (count * tiles, traces), 0)
    put = tail_rows(rows, count * tiles)
    coming[2].wait()
    tail = traces_ref[:, 3 * span : samples]
    for j in range(3):
        tail_row = jnp.where(place == j, 0, jnp.where(place == 3 + j, 1, -rows))
        extra = (tail_at == dest * count + tail_row).astype(f32).astype(bf16)
        rest = dot(extra, tail).astype(bf16)
        at = slice(j * span, (j + 1) * span)
        coming[3 + j].wait()
        both = jnp.concatenate([traces_ref[:, at], rest], 0)
        out_ref[:, at] = dot(jnp.concatenate([main, put], 1), both).astype(bf16)
        send(j, j * span, span)
    for copy in going:
        copy.wait()


def bin_kernel(sizes, arrived_far, scale_ref, time_ref, state_ref, summed_ref, s0, s1, s2, arrived_ref, sems):
    outs = (s0, s1, s2)
    width = summed_ref.shape[1] // 4
    coming = []
    for j, (first, size) in enumerate([(3 * width, LANES)] + [(j * width, width) for j in range(3)]):
        at = pl.ds(first, size)
        coming.append(pltpu.make_async_copy(arrived_far.at[:, at], arrived_ref.at[:, at], sems.at[j]))
        coming[-1].start()
    coming[0].wait()
    rows = arrived_ref.shape[0]
    bins, samples = summed_ref.shape
    span = samples // 4
    labels = arrived_ref[:, 3 * span :]
    lane = lax.broadcasted_iota(jnp.int32, (GROUP, LANES), 1)
    weights = jnp.where(lane == 0, 2.0, jnp.where(lane == 1, 1.0, 0.0)).astype(bf16)
    code = lax.dot_general(
        weights, labels, (((1,), (1,)), ((), ())), preferred_element_type=f32
    ).astype(jnp.int32)
    at = lax.broadcasted_iota(jnp.int32, (GROUP, rows), 1) % GROUP
    code = jnp.where(at < SLOTS, code, 0) - 1
    bin_at = lax.broadcasted_iota(jnp.int32, (bins, rows), 0)
    main = (bin_at == code[:1]).astype(f32).astype(bf16)
    scale = scale_ref[...]
    pieces = []
    for j in range(3):
        coming[1 + j].wait()
        pieces.append(dot(main, arrived_ref[:, j * span : (j + 1) * span]))
    last = None
    for j in range(3):
        first = pltpu.roll(code, SLOTS - j, 1)
        second = pltpu.roll(code, SLOTS + 1 - 3 - j, 1)
        tail_code = jnp.where(at == SLOTS, first, jnp.where(at == SLOTS + 1, second, -1))
        onehot = (bin_at == tail_code[:1]).astype(f32).astype(bf16)
        term = dot(onehot, arrived_ref[:, j * span : (j + 1) * span])
        last = term if last is None else last + term
    pieces.append(last)
    matrix = state_ref[...]
    blocks = []
    for p, piece in enumerate(pieces):
        piece = piece * scale
        summed_ref[:, p * span : (p + 1) * span] = piece
        states = left_dot(matrix, piece)
        blocks += [states[:, b : b + BLOCK] for b in range(0, span, BLOCK)]
    lows, highs = time_analysis(blocks, time_ref[...])
    put_joint(sizes, outs, lows, highs)


def encode(pieces, out):
    lane = lax.broadcasted_iota(jnp.int32, (out.shape[0], LANES), 1)
    marks = jnp.zeros((out.shape[0], LANES), f32)
    for b, piece in enumerate(pieces):
        largest = jnp.max(jnp.abs(piece), 1, keepdims=True)
        mark = jnp.clip(jnp.ceil(jnp.log2(largest) * 8.0), -LAST_MARK, LAST_MARK)
        code = jnp.clip(jnp.round(piece * (jnp.exp2(mark * -0.125) * TOP_CODE)), -TOP_CODE, TOP_CODE)
        out[:, b * LANES : (b + 1) * LANES] = code.astype(jnp.int32).astype(jnp.int16)
        marks = jnp.where(lane == b, mark, marks)
    out[:, len(pieces) * LANES :] = marks.astype(jnp.int32).astype(jnp.int16)


def scales_of(refs):
    marks = [ref[:, ref.shape[1] - LANES :].astype(jnp.int32).astype(f32) for ref in refs]
    return [jnp.exp2(mark * 0.125) * (1.0 / TOP_CODE) for mark in marks]


def decode(ref, scale, where):
    pieces = []
    for start in range(where.start, where.stop, LANES):
        b = start // LANES
        code = ref[:, start : start + LANES].astype(jnp.int32).astype(f32)
        pieces.append(code * scale[:, b : b + 1])
    return jnp.concatenate(pieces, 1)


def put_joint(sizes, outs, lows, highs):
    ends = np.cumsum([0] + sizes)
    part = [slice(int(ends[k]), int(ends[k + 1])) for k in range(5)]

    def message(rows, *pieces):
        spare = rows - sum(piece.shape[0] for piece in pieces)
        if spare:
            pieces += (jnp.zeros((spare, LANES), f32),)
        return jnp.concatenate(pieces, 0)

    rows = [out.shape[0] for out in outs]
    pairs = list(zip(lows, highs))
    encode([message(rows[0], low[part[0]], high[part[0]], low[part[3]]) for low, high in pairs], outs[0])
    encode([message(rows[1], low[part[1]], high[part[1]], low[part[4]]) for low, high in pairs], outs[1])
    encode([message(rows[2], low[part[2]], high[part[2]][:8]) for low, high in pairs], outs[2])


def take_joint(sizes, refs, scales, where):
    r, c, d, further_r, further_c = sizes
    m0, m1, m2 = [decode(ref, scale, where) for ref, scale in zip(refs, scales)]
    low = [m0[:r], m1[:c], m2[:d], m0[2 * r : 2 * r + further_r], m1[2 * c : 2 * c + further_c]]
    high = [m0[r : 2 * r], m1[c : 2 * c], m2[d : d + 8], jnp.zeros((d - 8, m2.shape[1]), f32)]
    return jnp.concatenate(low, 0), jnp.concatenate(high, 0)


def join_rows(refs, where):
    return jnp.concatenate([ref[:, where] for ref in refs], 0)


def steps(ref):
    return [slice(start, start + BLOCK) for start in range(0, ref.shape[1], BLOCK)]


def own_kernel(summed_ref, time_ref, own_ref, next_ref, low_ref, high_ref, next_out):
    blocks = [summed_ref[:, where] for where in steps(summed_ref)]
    lows, highs = time_analysis(blocks, time_ref[...])
    for b in range(0, len(blocks), 2):
        where = slice(b * LANES, (b + 2) * LANES)
        low = jnp.concatenate([lows[b], lows[b + 1]], 1)
        next_out[:, where] = left_dot(next_ref[...], low)
        low_ref[:, where] = left_dot(own_ref[...], low)
        high_ref[:, where] = left_dot(own_ref[...], jnp.concatenate([highs[b], highs[b + 1]], 1))


def middle_kernel(sizes, own_ref, edge_ref, s0, s1, s2, time_ref, timed_ref):
    rows, length = timed_ref.shape
    matrix = edge_ref[:rows]
    refs = (s0, s1, s2)
    scales = scales_of(refs)
    blocks = []
    for where in steps(own_ref):
        low, _ = take_joint(sizes, refs, scales, where)
        blocks.append(own_ref[:rows, where] + left_dot(matrix, low))
    lows, _ = time_analysis(blocks, time_ref[...])
    coarse = [jnp.concatenate([lows[b], lows[b + 1]], 1) for b in range(0, len(lows), 2)]
    lows, highs = time_analysis(coarse, time_ref[...])
    for b in range(len(coarse)):
        for base, piece in ((0, lows[b]), (length // 2, highs[b])):
            timed_ref[:, base + b * LANES : base + (b + 1) * LANES] = piece


def middle_details(thr_ref, blocks, time_matrix, time_t):
    lows, highs = time_analysis(blocks, time_matrix)
    quarter = blocks[0].shape[0] // 4
    pairs = []
    for b in range(len(blocks)):
        sides = []
        for piece, high in ((lows[b], 0), (highs[b], 1)):
            bands = [piece[q * quarter : (q + 1) * quarter] for q in range(4)]
            for q in range(4):
                bands[q] = shrink(bands[q], thr_ref[1, 2 * q + high - 1]) if q or high else jnp.zeros_like(bands[q])
            sides.append(jnp.concatenate(bands, 0))
        pairs.append(jnp.concatenate(sides, 1))
    return time_synthesis(pairs, time_t)


def sides_kernel(cols, before, own, after, stack_out, first_out, last_out):
    stack_out[...] = jnp.concatenate([before[...], own[...], after[...]], 0)
    starts = range(0, stack_out.shape[0], cols)
    first_out[...] = jnp.concatenate([stack_out[at : at + SIDE] for at in starts], 0)
    last_out[...] = jnp.concatenate([stack_out[at + cols - SIDE : at + cols] for at in starts], 0)


def details_kernel(
    sizes,
    thr_ref,
    low_in,
    high_in,
    edge_ref,
    s0,
    s1,
    s2,
    back_low,
    back_ref,
    next_in,
    next_edge,
    time_ref,
    time_t,
    next_back,
    low_out,
    high_out,
    low_states,
    high_states,
    next_out,
):
    quarter = low_in.shape[0] // 4
    refs = (s0, s1, s2)
    scales = scales_of(refs)
    blocks = []
    for where in steps(next_in):
        low, _ = take_joint(sizes, refs, scales, where)
        blocks.append(next_in[:, where] + left_dot(next_edge[...], low))
    next_states = []
    for b, block in enumerate(middle_details(thr_ref, blocks, time_ref[...], time_t[...])):
        next_out[:, b * BLOCK : (b + 1) * BLOCK] = block
        next_states.append(left_dot(next_back[...], block))
    for where in steps(low_in):
        low, high = take_joint(sizes, refs, scales, where)
        bands = low_in[quarter:, where] + left_dot(edge_ref[quarter:], low[: high.shape[0]])
        bands = [shrink(bands[(q - 1) * quarter : q * quarter], thr_ref[0, 2 * q - 1]) for q in range(1, 4)]
        bands = jnp.concatenate(bands, 0)
        low_out[:, where] = bands
        states = left_dot(back_low[...], bands)
        count = states.shape[0]
        more = next_states[where.start // BLOCK]
        low_states[:, where] = jnp.concatenate([states + more[:count], more[count:]], 0)
        bands = high_in[:, where] + left_dot(edge_ref[...], high)
        bands = [shrink(bands[q * quarter : (q + 1) * quarter], thr_ref[0, 2 * q]) for q in range(4)]
        bands = jnp.concatenate(bands, 0)
        high_out[:, where] = bands
        high_states[:, where] = left_dot(back_ref[...], bands)


def time_pairs(bands, matrix):
    half = bands.shape[1] // 2
    pairs = []
    for b in range(0, half, LANES):
        pairs.append(jnp.concatenate([bands[:, b : b + LANES], bands[:, half + b : half + b + LANES]], 1))
    return time_synthesis(pairs, matrix)


def deepest_kernel(
    sizes, thr_ref, before, own, after, bands_m, both_m, time_two, low_states, high_states, coarse_out, *outs
):
    stack = jnp.concatenate([before[...], own[...], after[...]], 0)
    bands = left_dot(bands_m[...], stack)
    row = lax.broadcasted_iota(jnp.int32, bands.shape, 0)
    high = lax.broadcasted_iota(jnp.int32, bands.shape, 1) >= bands.shape[1] // 2
    limit = jnp.where(high, thr_ref[2, 0], 0.0)
    quarter = bands.shape[0] // 4
    for q in range(1, 4):
        limit = jnp.where(row >= q * quarter, jnp.where(high, thr_ref[2, 2 * q], thr_ref[2, 2 * q - 1]), limit)
    state_lows, state_highs = [], []
    rows = coarse_out.shape[0]
    for b, block in enumerate(time_pairs(shrink(bands, limit), time_two[...])):
        where = slice(b * block.shape[1], (b + 1) * block.shape[1])
        both = left_dot(both_m[...], block)
        coarse_out[:, where] = both[:rows]
        low = both[rows:] + low_states[:, where]
        for at in range(0, block.shape[1], LANES):
            state_lows.append(low[:, at : at + LANES])
            state_highs.append(high_states[:, where.start + at : where.start + at + LANES])
    put_joint(sizes, outs, state_lows, state_highs)


def own_back_kernel(low_in, high_in, next_in, coarse_in, low_t, high_t, next_t, time_t, scale_ref, out_ref):
    blocks = []
    for where in steps(low_in):
        rows = coarse_in.shape[0]
        bands = jnp.concatenate([next_in[:rows, where] + coarse_in[:, where], next_in[rows:, where]], 0)
        low = left_dot(low_t[...], low_in[:, where]) + left_dot(next_t[...], bands)
        high = left_dot(high_t[...], high_in[:, where])
        for b in range(0, BLOCK, LANES):
            blocks.append(jnp.concatenate([low[:, b : b + LANES], high[:, b : b + LANES]], 1))
    scale = scale_ref[...]
    for b, block in enumerate(time_synthesis(blocks, time_t[...])):
        out_ref[:, b * BLOCK : (b + 1) * BLOCK] = block * scale


def final_kernel(sizes, own_ref, s0, s1, s2, time_t, time_low, state_t, scale_ref, out_far, out_ref, sems):
    pairs, lows = [], []
    refs = (s0, s1, s2)
    scales = scales_of(refs)
    for start in range(0, own_ref.shape[1] // 2, LANES):
        low, high = take_joint(sizes, refs, scales, slice(start, start + LANES))
        count = high.shape[0]
        pairs.append(jnp.concatenate([low[:count], high], 1))
        lows.append(low[count:])
    level0 = time_synthesis(pairs, time_t[...])
    level1 = synthesis_from_low(lows, time_low[...])
    scale = scale_ref[...]
    going = []
    for b in range(len(pairs)):
        where = slice(b * BLOCK, (b + 1) * BLOCK)
        states = jnp.concatenate([level0[b], level1[b]], 0)
        out_ref[:, where] = own_ref[:, where] + left_dot(state_t[...], states) * scale
        going.append(pltpu.make_async_copy(out_ref.at[:, where], out_far.at[:, where], sems.at[b]))
        going[-1].start()
    for copy in going:
        copy.wait()


def call(kernel, outs, *args, smem=(), far=(), far_outs=(), scratch=(), after=(), cost=None, limit=VMEM_LIMIT):
    spaces = [pltpu.SMEM if i in smem else pltpu.HBM if i in far else pltpu.VMEM for i in range(len(args))]
    spaces += [pl.ANY] * len(after)
    count = len(args)

    def body(*refs):
        kernel(*refs[:count], *refs[count + len(after) :])

    return pl.pallas_call(
        body,
        out_shape=[jax.ShapeDtypeStruct(shape, dtype) for shape, dtype in outs],
        in_specs=[pl.BlockSpec(memory_space=space) for space in spaces],
        out_specs=[
            pl.BlockSpec(memory_space=pltpu.HBM if i in far_outs else pltpu.VMEM) for i in range(len(outs))
        ],
        scratch_shapes=list(scratch),
        compiler_params=pltpu.CompilerParams(vmem_limit_bytes=limit),
        cost_estimate=None
        if cost is None
        else pl.CostEstimate(flops=int(cost), bytes_accessed=0, transcendentals=0),
    )(*args, *after)


def shift(block, inline_by, cross_by):
    inline_devs, cross_devs = lax.axis_size("inl"), lax.axis_size("xl")
    if not cross_by:
        return lax.ppermute(block, "inl", [((i + inline_by) % inline_devs, i) for i in range(inline_devs)])
    if not inline_by:
        return lax.ppermute(block, "xl", [((j + cross_by) % cross_devs, j) for j in range(cross_devs)])
    route = [
        ((i + inline_by) % inline_devs * cross_devs + (j + cross_by) % cross_devs, i * cross_devs + j)
        for i in range(inline_devs)
        for j in range(cross_devs)
    ]
    return lax.ppermute(block, ("inl", "xl"), route)


def exchange(states, ahead):
    corner = shift(states[2], ahead, ahead)
    column = shift(states[1], 0, ahead)
    return [shift(states[0], ahead, 0), column, corner]


def on_device(traces, dest_tile, bin_in_tile, fold, thresholds):
    devices = lax.axis_size("inl") * lax.axis_size("xl")
    trace_count, samples = traces.shape
    tile_rows, tile_cols = fold.shape
    bins = tile_rows * tile_cols
    width = SLOTS * samples // GROUP + LANES
    (outgoing,) = call(
        route_kernel,
        [((devices * GROUP, width), bf16)],
        dest_tile.reshape(1, trace_count),
        bin_in_tile.reshape(1, trace_count),
        traces,
        far=(0, 1, 2),
        far_outs=(0,),
        limit=LARGE_LIMIT,
        scratch=[
            pltpu.VMEM((1, trace_count), jnp.int32),
            pltpu.VMEM((1, trace_count), jnp.int32),
            pltpu.VMEM((trace_count, samples), bf16),
            pltpu.VMEM((devices * GROUP, width), bf16),
            pltpu.SemaphoreType.DMA((6,)),
            pltpu.SemaphoreType.DMA((4,)),
        ],
    )
    arrived = lax.all_to_all(
        outgoing.reshape(devices, GROUP, width), ("inl", "xl"), split_axis=0, concat_axis=0, tiled=True
    ).reshape(devices * GROUP, width)
    scale = (1.0 / jnp.sqrt(fold.astype(f32))).reshape(bins, 1)

    main, following = time_parts()
    time_matrix = np.concatenate([triple(main, 0), triple(following, 0)], 0)
    back_main, back_last = main.T, np.pad(following.T, ((0, 0), (0, BLOCK - LANES)))
    time_back = np.concatenate([triple(back_main, 0), triple(back_last, 0)], 0)
    twice, onward = np.zeros((2, BLOCK, 2 * BLOCK))
    twice[:LANES, :BLOCK] = twice[LANES:, BLOCK:] = back_main[:LANES]
    twice[:LANES, BLOCK:] = onward[LANES:, :BLOCK] = back_last[:LANES]
    last_two = back_last @ twice + back_main @ onward
    assert np.abs(back_last @ onward).max() == 0.0
    time_back_two = np.concatenate([triple(back_main @ twice, 0), triple(last_two, 0)], 0)
    time_back_low = np.concatenate([triple(back_main[:LANES], 0), triple(back_last[:LANES], 0)], 0)
    half, rows2, cols2 = samples // 2, tile_rows // 4, tile_cols // 4
    quarter, last = bins // 4, bins // 16
    own0, edge0, own1, edge1, states01, sizes = joint_matrices(tile_rows, tile_cols)
    assert rows2 == SIDE and cols2 >= SIDE
    bands2, back2 = side_matrices(rows2, cols2)
    count0 = sum(sizes[:3])
    joint_rows = [2 * sizes[0] + sizes[3], 2 * sizes[1] + sizes[4], sizes[2] + 8]
    joint_shapes = [((-(-rows // 16) * 16, half + LANES), jnp.int16) for rows in joint_rows]

    summed, *states = call(
        functools.partial(bin_kernel, sizes),
        [((bins, samples), f32)] + joint_shapes,
        arrived,
        scale,
        time_matrix,
        triple(states01, 1),
        far=(0,),
        limit=MIDDLE_LIMIT,
        scratch=[pltpu.VMEM((devices * GROUP, width), bf16), pltpu.SemaphoreType.DMA((4,))],
    )
    states = exchange(states, 1)
    own_low, own_high, own_next = call(
        own_kernel,
        [((bins, half), f32)] * 2 + [((quarter, half), f32)],
        summed,
        time_matrix,
        triple(own0, 1),
        triple(own1, 1),
        cost=1e9,
    )
    rows_all = rows2 + 2 * SIDE
    (timed,) = call(
        functools.partial(middle_kernel, sizes),
        [((last, half // 2), f32)],
        own_next,
        triple(edge1, 1),
        *states,
        time_matrix,
    )
    before, behind = shift(timed, -1, 0), shift(timed, 1, 0)
    low_details, high_details, low_states, high_states, next_details = call(
        functools.partial(details_kernel, sizes),
        [((bins - quarter, half), f32), ((bins, half), f32)]
        + [((sum(sizes), half), f32), ((count0, half), f32)]
        + [((quarter, half), f32)],
        thresholds,
        own_low,
        own_high,
        triple(edge0, 1),
        *states,
        triple(edge0[quarter:].T, 1),
        triple(edge0.T, 1),
        own_next,
        triple(edge1, 1),
        time_matrix,
        time_back,
        triple(edge1.T, 1),
        smem=(0,),
        after=(timed,),
        cost=1e9,
    )
    stack, firsts, lasts = call(
        functools.partial(sides_kernel, cols2),
        [((rows_all * size, samples // 4), f32) for size in (cols2, SIDE, SIDE)],
        before,
        timed,
        behind,
        after=(low_details,),
    )
    left, right = shift(lasts, 0, -1), shift(firsts, 0, 1)
    coarse1, *states = call(
        functools.partial(deepest_kernel, sizes),
        [((last, half), f32)] + joint_shapes,
        thresholds,
        left,
        stack,
        right,
        triple(bands2, 1),
        triple(np.concatenate([back2, edge1[:last].T @ back2], 0), 1),
        time_back_two,
        low_states,
        high_states,
        smem=(0,),
    )
    states = exchange(states, -1)
    (own_back,) = call(
        own_back_kernel,
        [((bins, samples), f32)],
        low_details,
        high_details,
        next_details,
        coarse1,
        triple(own0[quarter:].T, 1),
        triple(own0.T, 1),
        triple(own1.T, 1),
        time_back,
        scale,
        cost=1e9,
    )
    (denoised,) = call(
        functools.partial(final_kernel, sizes),
        [((bins, samples), f32)],
        own_back,
        *states,
        time_back,
        time_back_low,
        triple(states01.T, 1),
        scale,
        far_outs=(0,),
        scratch=[pltpu.VMEM((bins, samples), f32), pltpu.SemaphoreType.DMA((samples // BLOCK,))],
    )
    return denoised.reshape(tile_rows, tile_cols, samples)


def solution(mesh):
    placed = (P(("inl", "xl"), None), P(("inl", "xl"), None), P(("inl", "xl")), P("inl", "xl"), P())
    return jax.shard_map(
        on_device, mesh=mesh, in_specs=placed, out_specs=P("inl", "xl", None), check_vma=False
    )
```

```python
import functools

import jax
import jax.numpy as jnp
import ml_dtypes
import numpy as np
from jax import lax
from jax.experimental import pallas as pl
from jax.experimental.pallas import tpu as pltpu
from jax.sharding import PartitionSpec as P

LEVELS = 3
SLOTS = 6
GROUP = 8
LANES = 128
BLOCK = 256
VMEM_LIMIT = 32 * 1024 * 1024
LARGE_LIMIT = 62 * 1024 * 1024
MIDDLE_LIMIT = 48 * 1024 * 1024
TOP_CODE = 32767.0
LAST_MARK = 880.0
SIDE = 4

low_taps = [
    0.0352262918857095,
    -0.0854412738820267,
    -0.1350110200102546,
    0.4598775021184914,
    0.8068915093110924,
    0.3326705529500826,
]
high_taps = [(-1) ** offset * low_taps[5 - offset] for offset in range(6)]

bf16 = jnp.bfloat16
f32 = jnp.float32


def halves(matrix):
    top = np.asarray(matrix, np.float32).astype(ml_dtypes.bfloat16)
    rest = (np.asarray(matrix, np.float64) - top.astype(np.float64)).astype(ml_dtypes.bfloat16)
    return top, rest


def triple(matrix, axis):
    top, rest = halves(matrix)
    return np.concatenate([top, top, rest], axis)


def line_parts(length):
    half = length // 2
    whole = np.zeros((length, length + 4))
    for m in range(half):
        for k in range(6):
            whole[m, 2 * m + k] = low_taps[k]
            whole[half + m, 2 * m + k] = high_taps[k]
    left, sizes, right = np.linalg.svd(whole[:, length:])
    assert sizes[2] < 1e-9
    state = np.zeros((2, length))
    state[:, :4] = right[:2]
    return whole[:, :length], left[:, :2] * sizes[:2], state


def outer(on_rows, on_cols, banded):
    both = np.einsum("ar,bc->abrc", on_rows, on_cols)
    a, b, r, c = both.shape
    if banded:
        both = both.reshape(2, a // 2, 2, b // 2, r, c).transpose(2, 0, 1, 3, 4, 5)
    return both.reshape(a * b, r * c)


def two_levels(length):
    own0, edge0, state0 = line_parts(length)
    own1, edge1, state1 = line_parts(length // 2)
    low = slice(0, length // 2)
    assert np.abs(state1 @ edge0[low]).max() < 1e-9
    further = state1 @ own0[low]
    return dict(
        own0=own0,
        edge0=edge0,
        state0=state0,
        own1=own1 @ own0[low],
        far1=own1 @ edge0[low],
        edge1=edge1,
        further=further,
        states=np.concatenate([state0, further]),
    )


def joint_matrices(rows, cols):
    i, c = two_levels(rows), two_levels(cols)
    wide = [np.concatenate([d["edge0"], np.zeros_like(d["edge0"])], 1) for d in (i, c)]
    both = [np.concatenate([d["far1"], d["edge1"]], 1) for d in (i, c)]
    first = [0, 1, 4, 5] + [k for k in range(16) if k not in (0, 1, 4, 5)]
    own0 = outer(i["own0"], c["own0"], True)
    edge0 = [outer(i["edge0"], c["own0"], True), outer(i["own0"], c["edge0"], True), outer(*wide, True)[:, first]]
    own1 = outer(i["own1"], c["own1"], True)
    edge1 = [
        outer(i["far1"], c["own1"], True),
        outer(i["own1"], c["far1"], True),
        outer(*both, True)[:, first],
        outer(i["edge1"], np.eye(cols // 2), True),
        outer(np.eye(rows // 2), c["edge1"], True),
    ]
    states = [
        outer(i["state0"], np.eye(cols), False),
        outer(np.eye(rows), c["state0"], False),
        outer(i["states"], c["states"], False)[first],
        outer(i["further"], c["own1"], False),
        outer(i["own1"], c["further"], False),
    ]
    sizes = [len(part) for part in states]
    return own0, np.concatenate(edge0, 1), own1, np.concatenate(edge1, 1), np.concatenate(states, 0), sizes


def side_parts(length):
    firsts = range(-SIDE // 2, length // 2)
    count = len(firsts)
    bands = np.zeros((2 * count, length + 2 * SIDE))
    back = np.zeros((length, 2 * count))
    for m, first in enumerate(firsts):
        for k in range(6):
            for part, taps in ((0, low_taps), (count, high_taps)):
                bands[part + m, SIDE + 2 * first + k] = taps[k]
                if 0 <= 2 * first + k < length:
                    back[2 * first + k, part + m] = taps[k]
    return bands, back


def side_matrices(rows, cols):
    bands_i, back_i = side_parts(rows)
    bands_c, back_c = side_parts(cols)
    bands = outer(bands_i, bands_c, True)
    wide = cols + 2 * SIDE
    order = []
    for first, size in ((0, SIDE), (SIDE, cols), (SIDE + cols, SIDE)):
        order += [r * wide + first + c for r in range(rows + 2 * SIDE) for c in range(size)]
    back = outer(back_i.T, back_c.T, True).T
    return bands[:, order], back


def time_parts():
    whole = np.zeros((BLOCK + LANES, BLOCK))
    for m in range(LANES):
        for k in range(6):
            whole[2 * m + k, m] = low_taps[k]
            whole[2 * m + k, LANES + m] = high_taps[k]
    return whole[:BLOCK], whole[BLOCK:]


def split(value):
    top = value.astype(bf16)
    return top, (value - top.astype(f32)).astype(bf16)


def dot(left, right):
    return jnp.dot(left, right, preferred_element_type=f32)


def left_dot(matrix, value):
    top, rest = split(value)
    return dot(matrix, jnp.concatenate([top, rest, top], 0))


def time_analysis(blocks, matrix):
    parts = [split(block) for block in blocks]
    lows, highs = [], []
    for b in range(len(blocks)):
        top, rest = parts[b]
        next_top, next_rest = [part[:, :LANES] for part in parts[(b + 1) % len(blocks)]]
        joined = jnp.concatenate([top, rest, top, next_top, next_rest, next_top], 1)
        result = dot(joined, matrix)
        lows.append(result[:, :LANES])
        highs.append(result[:, LANES:])
    return lows, highs


def time_synthesis(blocks, matrix):
    parts = [split(block) for block in blocks]
    results = []
    for b in range(len(blocks)):
        top, rest = parts[b]
        last_top, last_rest = parts[b - 1]
        joined = jnp.concatenate([top, rest, top, last_top, last_rest, last_top], 1)
        results.append(dot(joined, matrix))
    return results


def synthesis_from_low(lows, matrix):
    parts = [split(low) for low in lows]
    results = []
    for b in range(len(lows)):
        top, rest = parts[b]
        last_top, last_rest = parts[b - 1]
        joined = jnp.concatenate([top, rest, top, last_top, last_rest, last_top], 1)
        results.append(dot(joined, matrix))
    return results


def shrink(value, limit):
    return value - jnp.clip(value, -limit, limit)


def spread_rows(value):
    count, width = value.shape
    tiles = value.reshape(count // GROUP, GROUP, width)
    turned = [tiles if q == 3 else pltpu.roll(tiles, SLOTS - 2 * q, 1) for q in range(4)]
    return jnp.stack(turned, 1).reshape(4 * count, width)


def gather_rows(value, first, second):
    count, width = value.shape
    tiles = value.reshape(count // (4 * GROUP), 4, GROUP, width)
    row = lax.broadcasted_iota(jnp.int32, (count // (4 * GROUP), GROUP, width), 1)
    result = None
    for q in range(4):
        for at, source in ((2 * q, first), (2 * q + 1, second)):
            turn = (at - source) % GROUP
            part = pltpu.roll(tiles[:, q], turn, 1) if turn else tiles[:, q]
            result = part if result is None else jnp.where(row == at, part, result)
    return result.reshape(count // 4, width)


def route_kernel(dest_far, bin_far, traces_far, out_far, dest_ref, bin_ref, traces_ref, out_ref, in_sems, out_sems):
    traces, samples = traces_ref.shape
    rows = out_ref.shape[0]
    tiles = rows // GROUP
    span = samples // 4
    coming = [
        pltpu.make_async_copy(dest_far, dest_ref, in_sems.at[4]),
        pltpu.make_async_copy(bin_far, bin_ref, in_sems.at[5]),
    ]
    for j in (3, 0, 1, 2):
        at = pl.ds(j * span, span)
        coming.append(pltpu.make_async_copy(traces_far.at[:, at], traces_ref.at[:, at], in_sems.at[j]))
    for copy in coming:
        copy.start()
    before = lax.broadcasted_iota(jnp.int32, (traces, traces), 0) <= lax.broadcasted_iota(
        jnp.int32, (traces, traces), 1
    )
    before = before.astype(f32).astype(bf16)
    coming[0].wait()
    coming[1].wait()
    dest = dest_ref[...]
    matches = lax.broadcasted_iota(jnp.int32, (tiles, traces), 0) == dest
    counts = dot(matches.astype(f32).astype(bf16), before)
    place = jnp.sum(jnp.where(matches, counts, 0.0), 0, keepdims=True).astype(jnp.int32) - 1
    row_at = lax.broadcasted_iota(jnp.int32, (rows, traces), 0)
    main = (row_at == dest * GROUP + place).astype(f32).astype(bf16)
    going = []

    def send(number, first, width):
        at = pl.ds(first, width)
        going.append(pltpu.make_async_copy(out_ref.at[:, at], out_far.at[:, at], out_sems.at[number]))
        going[-1].start()

    code = bin_ref[...] + 1
    lane = lax.broadcasted_iota(jnp.int32, (LANES, traces), 0)
    digits = jnp.where(lane == 0, code // 2, jnp.where(lane == 1, code % 2, 0))
    labels = lax.dot_general(
        main,
        digits.astype(f32).astype(bf16),
        (((1,), (1,)), ((), ())),
        preferred_element_type=f32,
    )
    out_ref[:, 3 * span :] = labels.astype(bf16)
    send(3, 3 * span, LANES)
    count = GROUP - SLOTS
    tail_at = lax.broadcasted_iota(jnp.int32, (count * tiles, traces), 0)
    is_tail = lax.broadcasted_iota(jnp.int32, (rows, span), 0) % GROUP >= SLOTS
    coming[2].wait()
    tail = traces_ref[:, 3 * span : samples]
    for j in range(3):
        tail_row = jnp.where(place == j, 0, jnp.where(place == 3 + j, 1, -rows))
        extra = (tail_at == dest * count + tail_row).astype(f32).astype(bf16)
        rest = spread_rows(dot(extra, tail))
        at = slice(j * span, (j + 1) * span)
        coming[3 + j].wait()
        out_ref[:, at] = jnp.where(is_tail, rest, dot(main, traces_ref[:, at])).astype(bf16)
        send(j, j * span, span)
    for copy in going:
        copy.wait()


def bin_kernel(sizes, arrived_far, scale_ref, time_ref, state_ref, summed_ref, s0, s1, s2, arrived_ref, sems):
    outs = (s0, s1, s2)
    width = summed_ref.shape[1] // 4
    coming = []
    for j, (first, size) in enumerate([(3 * width, LANES)] + [(j * width, width) for j in range(3)]):
        at = pl.ds(first, size)
        coming.append(pltpu.make_async_copy(arrived_far.at[:, at], arrived_ref.at[:, at], sems.at[j]))
        coming[-1].start()
    coming[0].wait()
    rows = arrived_ref.shape[0]
    bins, samples = summed_ref.shape
    span = samples // 4
    labels = arrived_ref[:, 3 * span :]
    lane = lax.broadcasted_iota(jnp.int32, (GROUP, LANES), 1)
    weights = jnp.where(lane == 0, 2.0, jnp.where(lane == 1, 1.0, 0.0)).astype(bf16)
    code = lax.dot_general(
        weights, labels, (((1,), (1,)), ((), ())), preferred_element_type=f32
    ).astype(jnp.int32)
    at = lax.broadcasted_iota(jnp.int32, (GROUP, rows), 1) % GROUP
    code = jnp.where(at < SLOTS, code, 0) - 1
    bin_at = lax.broadcasted_iota(jnp.int32, (bins, rows), 0)
    main = (bin_at == code[:1]).astype(f32).astype(bf16)
    scale = scale_ref[...]
    pieces = []
    for j in range(3):
        coming[1 + j].wait()
        pieces.append(dot(main, arrived_ref[:, j * span : (j + 1) * span]))
    onehots, tails = [], []
    wide = labels.astype(f32)
    tail_at = lax.broadcasted_iota(jnp.int32, (bins, rows // 4), 0)
    for j in range(3):
        tail_labels = gather_rows(wide, j, 3 + j).astype(bf16)
        tail_code = lax.dot_general(
            weights, tail_labels, (((1,), (1,)), ((), ())), preferred_element_type=f32
        ).astype(jnp.int32)
        onehots.append((tail_at == tail_code[:1] - 1).astype(f32).astype(bf16))
        tails.append(gather_rows(arrived_ref[:, j * span : (j + 1) * span].astype(f32), SLOTS, SLOTS + 1).astype(bf16))
    last = dot(jnp.concatenate(onehots, 1), jnp.concatenate(tails, 0))
    pieces.append(last)
    matrix = state_ref[...]
    blocks = []
    for p, piece in enumerate(pieces):
        piece = piece * scale
        summed_ref[:, p * span : (p + 1) * span] = piece
        states = left_dot(matrix, piece)
        blocks += [states[:, b : b + BLOCK] for b in range(0, span, BLOCK)]
    lows, highs = time_analysis(blocks, time_ref[...])
    put_joint(sizes, outs, lows, highs)


def encode(pieces, out):
    lane = lax.broadcasted_iota(jnp.int32, (out.shape[0], LANES), 1)
    marks = jnp.zeros((out.shape[0], LANES), f32)
    for b, piece in enumerate(pieces):
        largest = jnp.max(jnp.abs(piece), 1, keepdims=True)
        mark = jnp.clip(jnp.ceil(jnp.log2(largest) * 8.0), -LAST_MARK, LAST_MARK)
        code = jnp.clip(jnp.round(piece * (jnp.exp2(mark * -0.125) * TOP_CODE)), -TOP_CODE, TOP_CODE)
        out[:, b * LANES : (b + 1) * LANES] = code.astype(jnp.int32).astype(jnp.int16)
        marks = jnp.where(lane == b, mark, marks)
    out[:, len(pieces) * LANES :] = marks.astype(jnp.int32).astype(jnp.int16)


def scales_of(refs):
    marks = [ref[:, ref.shape[1] - LANES :].astype(jnp.int32).astype(f32) for ref in refs]
    return [jnp.exp2(mark * 0.125) * (1.0 / TOP_CODE) for mark in marks]


def decode(ref, scale, where):
    pieces = []
    for start in range(where.start, where.stop, LANES):
        b = start // LANES
        code = ref[:, start : start + LANES].astype(jnp.int32).astype(f32)
        pieces.append(code * scale[:, b : b + 1])
    return jnp.concatenate(pieces, 1)


def put_joint(sizes, outs, lows, highs):
    ends = np.cumsum([0] + sizes)
    part = [slice(int(ends[k]), int(ends[k + 1])) for k in range(5)]

    def message(rows, *pieces):
        spare = rows - sum(piece.shape[0] for piece in pieces)
        if spare:
            pieces += (jnp.zeros((spare, LANES), f32),)
        return jnp.concatenate(pieces, 0)

    rows = [out.shape[0] for out in outs]
    pairs = list(zip(lows, highs))
    encode([message(rows[0], low[part[0]], high[part[0]], low[part[3]]) for low, high in pairs], outs[0])
    encode([message(rows[1], low[part[1]], high[part[1]], low[part[4]]) for low, high in pairs], outs[1])
    encode([message(rows[2], low[part[2]], high[part[2]][:8]) for low, high in pairs], outs[2])


def take_joint(sizes, refs, scales, where):
    r, c, d, further_r, further_c = sizes
    m0, m1, m2 = [decode(ref, scale, where) for ref, scale in zip(refs, scales)]
    low = [m0[:r], m1[:c], m2[:d], m0[2 * r : 2 * r + further_r], m1[2 * c : 2 * c + further_c]]
    high = [m0[r : 2 * r], m1[c : 2 * c], m2[d : d + 8], jnp.zeros((d - 8, m2.shape[1]), f32)]
    return jnp.concatenate(low, 0), jnp.concatenate(high, 0)


def join_rows(refs, where):
    return jnp.concatenate([ref[:, where] for ref in refs], 0)


def steps(ref):
    return [slice(start, start + BLOCK) for start in range(0, ref.shape[1], BLOCK)]


def own_kernel(summed_ref, time_ref, own_ref, next_ref, low_ref, high_ref, next_out):
    blocks = [summed_ref[:, where] for where in steps(summed_ref)]
    lows, highs = time_analysis(blocks, time_ref[...])
    for b in range(0, len(blocks), 2):
        where = slice(b * LANES, (b + 2) * LANES)
        low = jnp.concatenate([lows[b], lows[b + 1]], 1)
        next_out[:, where] = left_dot(next_ref[...], low)
        low_ref[:, where] = left_dot(own_ref[...], low)
        high_ref[:, where] = left_dot(own_ref[...], jnp.concatenate([highs[b], highs[b + 1]], 1))


def middle_kernel(sizes, own_ref, edge_ref, s0, s1, s2, time_ref, timed_ref):
    rows, length = timed_ref.shape
    matrix = edge_ref[:rows]
    refs = (s0, s1, s2)
    scales = scales_of(refs)
    blocks = []
    for where in steps(own_ref):
        low, _ = take_joint(sizes, refs, scales, where)
        blocks.append(own_ref[:rows, where] + left_dot(matrix, low))
    lows, _ = time_analysis(blocks, time_ref[...])
    coarse = [jnp.concatenate([lows[b], lows[b + 1]], 1) for b in range(0, len(lows), 2)]
    lows, highs = time_analysis(coarse, time_ref[...])
    for b in range(len(coarse)):
        for base, piece in ((0, lows[b]), (length // 2, highs[b])):
            timed_ref[:, base + b * LANES : base + (b + 1) * LANES] = piece


def middle_details(thr_ref, blocks, time_matrix, time_t):
    lows, highs = time_analysis(blocks, time_matrix)
    quarter = blocks[0].shape[0] // 4
    pairs = []
    for b in range(len(blocks)):
        sides = []
        for piece, high in ((lows[b], 0), (highs[b], 1)):
            bands = [piece[q * quarter : (q + 1) * quarter] for q in range(4)]
            for q in range(4):
                bands[q] = shrink(bands[q], thr_ref[1, 2 * q + high - 1]) if q or high else jnp.zeros_like(bands[q])
            sides.append(jnp.concatenate(bands, 0))
        pairs.append(jnp.concatenate(sides, 1))
    return time_synthesis(pairs, time_t)


def sides_kernel(cols, before, own, after, stack_out, first_out, last_out):
    stack_out[...] = jnp.concatenate([before[...], own[...], after[...]], 0)
    starts = range(0, stack_out.shape[0], cols)
    first_out[...] = jnp.concatenate([stack_out[at : at + SIDE] for at in starts], 0)
    last_out[...] = jnp.concatenate([stack_out[at + cols - SIDE : at + cols] for at in starts], 0)


def details_kernel(
    sizes,
    thr_ref,
    low_in,
    high_in,
    edge_ref,
    s0,
    s1,
    s2,
    back_low,
    back_ref,
    next_in,
    next_edge,
    time_ref,
    time_t,
    next_back,
    low_out,
    high_out,
    low_states,
    high_states,
    next_out,
):
    quarter = low_in.shape[0] // 4
    refs = (s0, s1, s2)
    scales = scales_of(refs)
    blocks = []
    for where in steps(next_in):
        low, _ = take_joint(sizes, refs, scales, where)
        blocks.append(next_in[:, where] + left_dot(next_edge[...], low))
    next_states = []
    for b, block in enumerate(middle_details(thr_ref, blocks, time_ref[...], time_t[...])):
        next_out[:, b * BLOCK : (b + 1) * BLOCK] = block
        next_states.append(left_dot(next_back[...], block))
    for where in steps(low_in):
        low, high = take_joint(sizes, refs, scales, where)
        bands = low_in[quarter:, where] + left_dot(edge_ref[quarter:], low[: high.shape[0]])
        bands = [shrink(bands[(q - 1) * quarter : q * quarter], thr_ref[0, 2 * q - 1]) for q in range(1, 4)]
        bands = jnp.concatenate(bands, 0)
        low_out[:, where] = bands
        states = left_dot(back_low[...], bands)
        count = states.shape[0]
        more = next_states[where.start // BLOCK]
        low_states[:, where] = jnp.concatenate([states + more[:count], more[count:]], 0)
        bands = high_in[:, where] + left_dot(edge_ref[...], high)
        bands = [shrink(bands[q * quarter : (q + 1) * quarter], thr_ref[0, 2 * q]) for q in range(4)]
        bands = jnp.concatenate(bands, 0)
        high_out[:, where] = bands
        high_states[:, where] = left_dot(back_ref[...], bands)


def time_pairs(bands, matrix):
    half = bands.shape[1] // 2
    pairs = []
    for b in range(0, half, LANES):
        pairs.append(jnp.concatenate([bands[:, b : b + LANES], bands[:, half + b : half + b + LANES]], 1))
    return time_synthesis(pairs, matrix)


def deepest_kernel(
    sizes, thr_ref, before, own, after, bands_m, both_m, time_two, low_states, high_states, coarse_out, *outs
):
    stack = jnp.concatenate([before[...], own[...], after[...]], 0)
    bands = left_dot(bands_m[...], stack)
    row = lax.broadcasted_iota(jnp.int32, bands.shape, 0)
    high = lax.broadcasted_iota(jnp.int32, bands.shape, 1) >= bands.shape[1] // 2
    limit = jnp.where(high, thr_ref[2, 0], 0.0)
    quarter = bands.shape[0] // 4
    for q in range(1, 4):
        limit = jnp.where(row >= q * quarter, jnp.where(high, thr_ref[2, 2 * q], thr_ref[2, 2 * q - 1]), limit)
    state_lows, state_highs = [], []
    rows = coarse_out.shape[0]
    for b, block in enumerate(time_pairs(shrink(bands, limit), time_two[...])):
        where = slice(b * block.shape[1], (b + 1) * block.shape[1])
        both = left_dot(both_m[...], block)
        coarse_out[:, where] = both[:rows]
        low = both[rows:] + low_states[:, where]
        for at in range(0, block.shape[1], LANES):
            state_lows.append(low[:, at : at + LANES])
            state_highs.append(high_states[:, where.start + at : where.start + at + LANES])
    put_joint(sizes, outs, state_lows, state_highs)


def own_back_kernel(low_in, high_in, next_in, coarse_in, low_t, high_t, next_t, time_t, scale_ref, out_ref):
    blocks = []
    for where in steps(low_in):
        rows = coarse_in.shape[0]
        bands = jnp.concatenate([next_in[:rows, where] + coarse_in[:, where], next_in[rows:, where]], 0)
        low = left_dot(low_t[...], low_in[:, where]) + left_dot(next_t[...], bands)
        high = left_dot(high_t[...], high_in[:, where])
        for b in range(0, BLOCK, LANES):
            blocks.append(jnp.concatenate([low[:, b : b + LANES], high[:, b : b + LANES]], 1))
    scale = scale_ref[...]
    for b, block in enumerate(time_synthesis(blocks, time_t[...])):
        out_ref[:, b * BLOCK : (b + 1) * BLOCK] = block * scale


def final_kernel(sizes, own_ref, s0, s1, s2, time_t, time_low, state_t, scale_ref, out_far, out_ref, sems):
    pairs, lows = [], []
    refs = (s0, s1, s2)
    scales = scales_of(refs)
    for start in range(0, own_ref.shape[1] // 2, LANES):
        low, high = take_joint(sizes, refs, scales, slice(start, start + LANES))
        count = high.shape[0]
        pairs.append(jnp.concatenate([low[:count], high], 1))
        lows.append(low[count:])
    level0 = time_synthesis(pairs, time_t[...])
    level1 = synthesis_from_low(lows, time_low[...])
    scale = scale_ref[...]
    going = []
    for b in range(len(pairs)):
        where = slice(b * BLOCK, (b + 1) * BLOCK)
        states = jnp.concatenate([level0[b], level1[b]], 0)
        out_ref[:, where] = own_ref[:, where] + left_dot(state_t[...], states) * scale
        going.append(pltpu.make_async_copy(out_ref.at[:, where], out_far.at[:, where], sems.at[b]))
        going[-1].start()
    for copy in going:
        copy.wait()


def call(kernel, outs, *args, smem=(), far=(), far_outs=(), scratch=(), after=(), cost=None, limit=VMEM_LIMIT):
    spaces = [pltpu.SMEM if i in smem else pltpu.HBM if i in far else pltpu.VMEM for i in range(len(args))]
    spaces += [pl.ANY] * len(after)
    count = len(args)

    def body(*refs):
        kernel(*refs[:count], *refs[count + len(after) :])

    return pl.pallas_call(
        body,
        out_shape=[jax.ShapeDtypeStruct(shape, dtype) for shape, dtype in outs],
        in_specs=[pl.BlockSpec(memory_space=space) for space in spaces],
        out_specs=[
            pl.BlockSpec(memory_space=pltpu.HBM if i in far_outs else pltpu.VMEM) for i in range(len(outs))
        ],
        scratch_shapes=list(scratch),
        compiler_params=pltpu.CompilerParams(vmem_limit_bytes=limit),
        cost_estimate=None
        if cost is None
        else pl.CostEstimate(flops=int(cost), bytes_accessed=0, transcendentals=0),
    )(*args, *after)


def shift(block, inline_by, cross_by):
    inline_devs, cross_devs = lax.axis_size("inl"), lax.axis_size("xl")
    if not cross_by:
        return lax.ppermute(block, "inl", [((i + inline_by) % inline_devs, i) for i in range(inline_devs)])
    if not inline_by:
        return lax.ppermute(block, "xl", [((j + cross_by) % cross_devs, j) for j in range(cross_devs)])
    route = [
        ((i + inline_by) % inline_devs * cross_devs + (j + cross_by) % cross_devs, i * cross_devs + j)
        for i in range(inline_devs)
        for j in range(cross_devs)
    ]
    return lax.ppermute(block, ("inl", "xl"), route)


def exchange(states, ahead):
    corner = shift(states[2], ahead, ahead)
    column = shift(states[1], 0, ahead)
    return [shift(states[0], ahead, 0), column, corner]


def on_device(traces, dest_tile, bin_in_tile, fold, thresholds):
    devices = lax.axis_size("inl") * lax.axis_size("xl")
    trace_count, samples = traces.shape
    tile_rows, tile_cols = fold.shape
    bins = tile_rows * tile_cols
    width = SLOTS * samples // GROUP + LANES
    (outgoing,) = call(
        route_kernel,
        [((devices * GROUP, width), bf16)],
        dest_tile.reshape(1, trace_count),
        bin_in_tile.reshape(1, trace_count),
        traces,
        far=(0, 1, 2),
        far_outs=(0,),
        limit=LARGE_LIMIT,
        scratch=[
            pltpu.VMEM((1, trace_count), jnp.int32),
            pltpu.VMEM((1, trace_count), jnp.int32),
            pltpu.VMEM((trace_count, samples), bf16),
            pltpu.VMEM((devices * GROUP, width), bf16),
            pltpu.SemaphoreType.DMA((6,)),
            pltpu.SemaphoreType.DMA((4,)),
        ],
    )
    arrived = lax.all_to_all(
        outgoing.reshape(devices, GROUP, width), ("inl", "xl"), split_axis=0, concat_axis=0, tiled=True
    ).reshape(devices * GROUP, width)
    scale = (1.0 / jnp.sqrt(fold.astype(f32))).reshape(bins, 1)

    main, following = time_parts()
    time_matrix = np.concatenate([triple(main, 0), triple(following, 0)], 0)
    back_main, back_last = main.T, np.pad(following.T, ((0, 0), (0, BLOCK - LANES)))
    time_back = np.concatenate([triple(back_main, 0), triple(back_last, 0)], 0)
    twice, onward = np.zeros((2, BLOCK, 2 * BLOCK))
    twice[:LANES, :BLOCK] = twice[LANES:, BLOCK:] = back_main[:LANES]
    twice[:LANES, BLOCK:] = onward[LANES:, :BLOCK] = back_last[:LANES]
    last_two = back_last @ twice + back_main @ onward
    assert np.abs(back_last @ onward).max() == 0.0
    time_back_two = np.concatenate([triple(back_main @ twice, 0), triple(last_two, 0)], 0)
    time_back_low = np.concatenate([triple(back_main[:LANES], 0), triple(back_last[:LANES], 0)], 0)
    half, rows2, cols2 = samples // 2, tile_rows // 4, tile_cols // 4
    quarter, last = bins // 4, bins // 16
    own0, edge0, own1, edge1, states01, sizes = joint_matrices(tile_rows, tile_cols)
    assert rows2 == SIDE and cols2 >= SIDE
    bands2, back2 = side_matrices(rows2, cols2)
    count0 = sum(sizes[:3])
    joint_rows = [2 * sizes[0] + sizes[3], 2 * sizes[1] + sizes[4], sizes[2] + 8]
    joint_shapes = [((-(-rows // 16) * 16, half + LANES), jnp.int16) for rows in joint_rows]

    summed, *states = call(
        functools.partial(bin_kernel, sizes),
        [((bins, samples), f32)] + joint_shapes,
        arrived,
        scale,
        time_matrix,
        triple(states01, 1),
        far=(0,),
        limit=MIDDLE_LIMIT,
        scratch=[pltpu.VMEM((devices * GROUP, width), bf16), pltpu.SemaphoreType.DMA((4,))],
    )
    states = exchange(states, 1)
    own_low, own_high, own_next = call(
        own_kernel,
        [((bins, half), f32)] * 2 + [((quarter, half), f32)],
        summed,
        time_matrix,
        triple(own0, 1),
        triple(own1, 1),
        cost=1e9,
    )
    rows_all = rows2 + 2 * SIDE
    (timed,) = call(
        functools.partial(middle_kernel, sizes),
        [((last, half // 2), f32)],
        own_next,
        triple(edge1, 1),
        *states,
        time_matrix,
    )
    before, behind = shift(timed, -1, 0), shift(timed, 1, 0)
    low_details, high_details, low_states, high_states, next_details = call(
        functools.partial(details_kernel, sizes),
        [((bins - quarter, half), f32), ((bins, half), f32)]
        + [((sum(sizes), half), f32), ((count0, half), f32)]
        + [((quarter, half), f32)],
        thresholds,
        own_low,
        own_high,
        triple(edge0, 1),
        *states,
        triple(edge0[quarter:].T, 1),
        triple(edge0.T, 1),
        own_next,
        triple(edge1, 1),
        time_matrix,
        time_back,
        triple(edge1.T, 1),
        smem=(0,),
        after=(timed,),
        cost=1e9,
    )
    stack, firsts, lasts = call(
        functools.partial(sides_kernel, cols2),
        [((rows_all * size, samples // 4), f32) for size in (cols2, SIDE, SIDE)],
        before,
        timed,
        behind,
        after=(low_details,),
    )
    left, right = shift(lasts, 0, -1), shift(firsts, 0, 1)
    coarse1, *states = call(
        functools.partial(deepest_kernel, sizes),
        [((last, half), f32)] + joint_shapes,
        thresholds,
        left,
        stack,
        right,
        triple(bands2, 1),
        triple(np.concatenate([back2, edge1[:last].T @ back2], 0), 1),
        time_back_two,
        low_states,
        high_states,
        smem=(0,),
    )
    states = exchange(states, -1)
    (own_back,) = call(
        own_back_kernel,
        [((bins, samples), f32)],
        low_details,
        high_details,
        next_details,
        coarse1,
        triple(own0[quarter:].T, 1),
        triple(own0.T, 1),
        triple(own1.T, 1),
        time_back,
        scale,
        cost=1e9,
    )
    (denoised,) = call(
        functools.partial(final_kernel, sizes),
        [((bins, samples), f32)],
        own_back,
        *states,
        time_back,
        time_back_low,
        triple(states01.T, 1),
        scale,
        far_outs=(0,),
        scratch=[pltpu.VMEM((bins, samples), f32), pltpu.SemaphoreType.DMA((samples // BLOCK,))],
    )
    return denoised.reshape(tile_rows, tile_cols, samples)


def solution(mesh):
    placed = (P(("inl", "xl"), None), P(("inl", "xl"), None), P(("inl", "xl")), P("inl", "xl"), P())
    return jax.shard_map(
        on_device, mesh=mesh, in_specs=placed, out_specs=P("inl", "xl", None), check_vma=False
    )
```

```python
import functools

import jax
import jax.numpy as jnp
import ml_dtypes
import numpy as np
from jax import lax
from jax.experimental import pallas as pl
from jax.experimental.pallas import tpu as pltpu
from jax.sharding import PartitionSpec as P

LEVELS = 3
SLOTS = 6
GROUP = 8
LANES = 128
BLOCK = 256
VMEM_LIMIT = 32 * 1024 * 1024
LARGE_LIMIT = 62 * 1024 * 1024
MIDDLE_LIMIT = 48 * 1024 * 1024
TOP_CODE = 32767.0
FEW_ROWS = 160
LAST_MARK = 880.0
SIDE = 4

low_taps = [
    0.0352262918857095,
    -0.0854412738820267,
    -0.1350110200102546,
    0.4598775021184914,
    0.8068915093110924,
    0.3326705529500826,
]
high_taps = [(-1) ** offset * low_taps[5 - offset] for offset in range(6)]

bf16 = jnp.bfloat16
f32 = jnp.float32


def halves(matrix):
    top = np.asarray(matrix, np.float32).astype(ml_dtypes.bfloat16)
    rest = (np.asarray(matrix, np.float64) - top.astype(np.float64)).astype(ml_dtypes.bfloat16)
    return top, rest


def triple(matrix, axis):
    top, rest = halves(matrix)
    return np.concatenate([top, top, rest], axis)


def line_parts(length):
    half = length // 2
    whole = np.zeros((length, length + 4))
    for m in range(half):
        for k in range(6):
            whole[m, 2 * m + k] = low_taps[k]
            whole[half + m, 2 * m + k] = high_taps[k]
    left, sizes, right = np.linalg.svd(whole[:, length:])
    assert sizes[2] < 1e-9
    state = np.zeros((2, length))
    state[:, :4] = right[:2]
    return whole[:, :length], left[:, :2] * sizes[:2], state


def outer(on_rows, on_cols, banded):
    both = np.einsum("ar,bc->abrc", on_rows, on_cols)
    a, b, r, c = both.shape
    if banded:
        both = both.reshape(2, a // 2, 2, b // 2, r, c).transpose(2, 0, 1, 3, 4, 5)
    return both.reshape(a * b, r * c)


def two_levels(length):
    own0, edge0, state0 = line_parts(length)
    own1, edge1, state1 = line_parts(length // 2)
    low = slice(0, length // 2)
    assert np.abs(state1 @ edge0[low]).max() < 1e-9
    further = state1 @ own0[low]
    return dict(
        own0=own0,
        edge0=edge0,
        state0=state0,
        own1=own1 @ own0[low],
        far1=own1 @ edge0[low],
        edge1=edge1,
        further=further,
        states=np.concatenate([state0, further]),
    )


def joint_matrices(rows, cols):
    i, c = two_levels(rows), two_levels(cols)
    wide = [np.concatenate([d["edge0"], np.zeros_like(d["edge0"])], 1) for d in (i, c)]
    both = [np.concatenate([d["far1"], d["edge1"]], 1) for d in (i, c)]
    first = [0, 1, 4, 5] + [k for k in range(16) if k not in (0, 1, 4, 5)]
    own0 = outer(i["own0"], c["own0"], True)
    edge0 = [outer(i["edge0"], c["own0"], True), outer(i["own0"], c["edge0"], True), outer(*wide, True)[:, first]]
    own1 = outer(i["own1"], c["own1"], True)
    edge1 = [
        outer(i["far1"], c["own1"], True),
        outer(i["own1"], c["far1"], True),
        outer(*both, True)[:, first],
        outer(i["edge1"], np.eye(cols // 2), True),
        outer(np.eye(rows // 2), c["edge1"], True),
    ]
    states = [
        outer(i["state0"], np.eye(cols), False),
        outer(np.eye(rows), c["state0"], False),
        outer(i["states"], c["states"], False)[first],
        outer(i["further"], c["own1"], False),
        outer(i["own1"], c["further"], False),
    ]
    sizes = [len(part) for part in states]
    return own0, np.concatenate(edge0, 1), own1, np.concatenate(edge1, 1), np.concatenate(states, 0), sizes


def side_parts(length):
    firsts = range(-SIDE // 2, length // 2)
    count = len(firsts)
    bands = np.zeros((2 * count, length + 2 * SIDE))
    back = np.zeros((length, 2 * count))
    for m, first in enumerate(firsts):
        for k in range(6):
            for part, taps in ((0, low_taps), (count, high_taps)):
                bands[part + m, SIDE + 2 * first + k] = taps[k]
                if 0 <= 2 * first + k < length:
                    back[2 * first + k, part + m] = taps[k]
    return bands, back


def side_matrices(rows, cols):
    bands_i, back_i = side_parts(rows)
    bands_c, back_c = side_parts(cols)
    bands = outer(bands_i, bands_c, True)
    wide = cols + 2 * SIDE
    order = []
    for first, size in ((0, SIDE), (SIDE, cols), (SIDE + cols, SIDE)):
        order += [r * wide + first + c for r in range(rows + 2 * SIDE) for c in range(size)]
    back = outer(back_i.T, back_c.T, True).T
    return bands[:, order], back


def time_parts():
    whole = np.zeros((BLOCK + LANES, BLOCK))
    for m in range(LANES):
        for k in range(6):
            whole[2 * m + k, m] = low_taps[k]
            whole[2 * m + k, LANES + m] = high_taps[k]
    return whole[:BLOCK], whole[BLOCK:]


def split(value):
    top = value.astype(bf16)
    return top, (value - top.astype(f32)).astype(bf16)


def dot(left, right):
    return jnp.dot(left, right, preferred_element_type=f32)


def left_dot(matrix, value):
    top, rest = split(value)
    return dot(matrix, jnp.concatenate([top, rest, top], 0))


def beside(blocks, neighbours, matrix):
    count = blocks[0].shape[0]
    together = len(blocks) if count <= FEW_ROWS else 1
    results = []
    for b in range(0, len(blocks), together):
        top, rest = split(jnp.concatenate(blocks[b : b + together], 0))
        other, other_rest = split(jnp.concatenate(neighbours[b : b + together], 0))
        result = dot(jnp.concatenate([top, rest, top, other, other_rest, other], 1), matrix)
        results += [result[k * count : (k + 1) * count] for k in range(together)]
    return results


def time_analysis(blocks, matrix):
    results = beside(blocks, [block[:, :LANES] for block in blocks[1:] + blocks[:1]], matrix)
    return [result[:, :LANES] for result in results], [result[:, LANES:] for result in results]


def time_synthesis(blocks, matrix):
    return beside(blocks, blocks[-1:] + blocks[:-1], matrix)


def synthesis_from_low(lows, matrix):
    return beside(lows, lows[-1:] + lows[:-1], matrix)


def shrink(value, limit):
    return value - jnp.clip(value, -limit, limit)


def spread_rows(value):
    count, width = value.shape
    tiles = value.reshape(count // GROUP, GROUP, width)
    turned = [tiles if q == 3 else pltpu.roll(tiles, SLOTS - 2 * q, 1) for q in range(4)]
    return jnp.stack(turned, 1).reshape(4 * count, width)


def gather_rows(value, first, second):
    count, width = value.shape
    tiles = value.reshape(count // (4 * GROUP), 4, GROUP, width)
    row = lax.broadcasted_iota(jnp.int32, (count // (4 * GROUP), GROUP, width), 1)
    result = None
    for q in range(4):
        for at, source in ((2 * q, first), (2 * q + 1, second)):
            turn = (at - source) % GROUP
            part = pltpu.roll(tiles[:, q], turn, 1) if turn else tiles[:, q]
            result = part if result is None else jnp.where(row == at, part, result)
    return result.reshape(count // 4, width)


def route_kernel(dest_far, bin_far, traces_far, out_far, dest_ref, bin_ref, traces_ref, out_ref, in_sems, out_sems):
    traces, samples = traces_ref.shape
    rows = out_ref.shape[0]
    tiles = rows // GROUP
    span = samples // 4
    coming = [
        pltpu.make_async_copy(dest_far, dest_ref, in_sems.at[4]),
        pltpu.make_async_copy(bin_far, bin_ref, in_sems.at[5]),
    ]
    for j in (3, 0, 1, 2):
        at = pl.ds(j * span, span)
        coming.append(pltpu.make_async_copy(traces_far.at[:, at], traces_ref.at[:, at], in_sems.at[j]))
    for copy in coming:
        copy.start()
    before = lax.broadcasted_iota(jnp.int32, (traces, traces), 0) <= lax.broadcasted_iota(
        jnp.int32, (traces, traces), 1
    )
    before = before.astype(f32).astype(bf16)
    coming[0].wait()
    coming[1].wait()
    dest = dest_ref[...]
    matches = lax.broadcasted_iota(jnp.int32, (tiles, traces), 0) == dest
    counts = dot(matches.astype(f32).astype(bf16), before)
    place = jnp.sum(jnp.where(matches, counts, 0.0), 0, keepdims=True).astype(jnp.int32) - 1
    row_at = lax.broadcasted_iota(jnp.int32, (rows, traces), 0)
    main = (row_at == dest * GROUP + place).astype(f32).astype(bf16)
    going = []

    def send(number, first, width):
        at = pl.ds(first, width)
        going.append(pltpu.make_async_copy(out_ref.at[:, at], out_far.at[:, at], out_sems.at[number]))
        going[-1].start()

    code = bin_ref[...] + 1
    lane = lax.broadcasted_iota(jnp.int32, (LANES, traces), 0)
    digits = jnp.where(lane == 0, code // 2, jnp.where(lane == 1, code % 2, 0))
    labels = lax.dot_general(
        main,
        digits.astype(f32).astype(bf16),
        (((1,), (1,)), ((), ())),
        preferred_element_type=f32,
    )
    out_ref[:, 3 * span :] = labels.astype(bf16)
    send(3, 3 * span, LANES)
    count = GROUP - SLOTS
    tail_at = lax.broadcasted_iota(jnp.int32, (count * tiles, traces), 0)
    is_tail = lax.broadcasted_iota(jnp.int32, (rows, span), 0) % GROUP >= SLOTS
    coming[2].wait()
    tail = traces_ref[:, 3 * span : samples]
    for j in range(3):
        tail_row = jnp.where(place == j, 0, jnp.where(place == 3 + j, 1, -rows))
        extra = (tail_at == dest * count + tail_row).astype(f32).astype(bf16)
        rest = spread_rows(dot(extra, tail))
        at = slice(j * span, (j + 1) * span)
        coming[3 + j].wait()
        out_ref[:, at] = jnp.where(is_tail, rest, dot(main, traces_ref[:, at])).astype(bf16)
        send(j, j * span, span)
    for copy in going:
        copy.wait()


def bin_kernel(sizes, arrived_far, scale_ref, time_ref, state_ref, summed_ref, s0, s1, s2, arrived_ref, sems):
    outs = (s0, s1, s2)
    width = summed_ref.shape[1] // 4
    coming = []
    for j, (first, size) in enumerate([(3 * width, LANES)] + [(j * width, width) for j in range(3)]):
        at = pl.ds(first, size)
        coming.append(pltpu.make_async_copy(arrived_far.at[:, at], arrived_ref.at[:, at], sems.at[j]))
        coming[-1].start()
    coming[0].wait()
    rows = arrived_ref.shape[0]
    bins, samples = summed_ref.shape
    span = samples // 4
    labels = arrived_ref[:, 3 * span :]
    lane = lax.broadcasted_iota(jnp.int32, (GROUP, LANES), 1)
    weights = jnp.where(lane == 0, 2.0, jnp.where(lane == 1, 1.0, 0.0)).astype(bf16)
    code = lax.dot_general(
        weights, labels, (((1,), (1,)), ((), ())), preferred_element_type=f32
    ).astype(jnp.int32)
    at = lax.broadcasted_iota(jnp.int32, (GROUP, rows), 1) % GROUP
    code = jnp.where(at < SLOTS, code, 0) - 1
    bin_at = lax.broadcasted_iota(jnp.int32, (bins, rows), 0)
    main = (bin_at == code[:1]).astype(f32).astype(bf16)
    scale = scale_ref[...]
    pieces = []
    for j in range(3):
        coming[1 + j].wait()
        pieces.append(dot(main, arrived_ref[:, j * span : (j + 1) * span]))
    onehots, tails = [], []
    wide = labels.astype(f32)
    tail_at = lax.broadcasted_iota(jnp.int32, (bins, rows // 4), 0)
    for j in range(3):
        tail_labels = gather_rows(wide, j, 3 + j).astype(bf16)
        tail_code = lax.dot_general(
            weights, tail_labels, (((1,), (1,)), ((), ())), preferred_element_type=f32
        ).astype(jnp.int32)
        onehots.append((tail_at == tail_code[:1] - 1).astype(f32).astype(bf16))
        tails.append(gather_rows(arrived_ref[:, j * span : (j + 1) * span].astype(f32), SLOTS, SLOTS + 1).astype(bf16))
    last = dot(jnp.concatenate(onehots, 1), jnp.concatenate(tails, 0))
    pieces.append(last)
    matrix = state_ref[...]
    blocks = []
    for p, piece in enumerate(pieces):
        piece = piece * scale
        summed_ref[:, p * span : (p + 1) * span] = piece
        states = left_dot(matrix, piece)
        blocks += [states[:, b : b + BLOCK] for b in range(0, span, BLOCK)]
    lows, highs = time_analysis(blocks, time_ref[...])
    put_joint(sizes, outs, lows, highs)


def encode(pieces, out):
    lane = lax.broadcasted_iota(jnp.int32, (out.shape[0], LANES), 1)
    marks = jnp.zeros((out.shape[0], LANES), f32)
    for b, piece in enumerate(pieces):
        largest = jnp.max(jnp.abs(piece), 1, keepdims=True)
        mark = jnp.clip(jnp.ceil(jnp.log2(largest) * 8.0), -LAST_MARK, LAST_MARK)
        code = jnp.clip(jnp.round(piece * (jnp.exp2(mark * -0.125) * TOP_CODE)), -TOP_CODE, TOP_CODE)
        out[:, b * LANES : (b + 1) * LANES] = code.astype(jnp.int32).astype(jnp.int16)
        marks = jnp.where(lane == b, mark, marks)
    out[:, len(pieces) * LANES :] = marks.astype(jnp.int32).astype(jnp.int16)


def scales_of(refs):
    marks = [ref[:, ref.shape[1] - LANES :].astype(jnp.int32).astype(f32) for ref in refs]
    return [jnp.exp2(mark * 0.125) * (1.0 / TOP_CODE) for mark in marks]


def decode(ref, scale, where):
    pieces = []
    for start in range(where.start, where.stop, LANES):
        b = start // LANES
        code = ref[:, start : start + LANES].astype(jnp.int32).astype(f32)
        pieces.append(code * scale[:, b : b + 1])
    return jnp.concatenate(pieces, 1)


def put_joint(sizes, outs, lows, highs):
    ends = np.cumsum([0] + sizes)
    part = [slice(int(ends[k]), int(ends[k + 1])) for k in range(5)]

    def message(rows, *pieces):
        spare = rows - sum(piece.shape[0] for piece in pieces)
        if spare:
            pieces += (jnp.zeros((spare, LANES), f32),)
        return jnp.concatenate(pieces, 0)

    rows = [out.shape[0] for out in outs]
    pairs = list(zip(lows, highs))
    encode([message(rows[0], low[part[0]], high[part[0]], low[part[3]]) for low, high in pairs], outs[0])
    encode([message(rows[1], low[part[1]], high[part[1]], low[part[4]]) for low, high in pairs], outs[1])
    encode([message(rows[2], low[part[2]], high[part[2]][:8]) for low, high in pairs], outs[2])


def take_joint(sizes, refs, scales, where):
    r, c, d, further_r, further_c = sizes
    m0, m1, m2 = [decode(ref, scale, where) for ref, scale in zip(refs, scales)]
    low = [m0[:r], m1[:c], m2[:d], m0[2 * r : 2 * r + further_r], m1[2 * c : 2 * c + further_c]]
    high = [m0[r : 2 * r], m1[c : 2 * c], m2[d : d + 8], jnp.zeros((d - 8, m2.shape[1]), f32)]
    return jnp.concatenate(low, 0), jnp.concatenate(high, 0)


def join_rows(refs, where):
    return jnp.concatenate([ref[:, where] for ref in refs], 0)


def steps(ref):
    return [slice(start, start + BLOCK) for start in range(0, ref.shape[1], BLOCK)]


def own_kernel(summed_ref, time_ref, own_ref, next_ref, low_ref, high_ref, next_out):
    blocks = [summed_ref[:, where] for where in steps(summed_ref)]
    lows, highs = time_analysis(blocks, time_ref[...])
    for b in range(0, len(blocks), 2):
        where = slice(b * LANES, (b + 2) * LANES)
        low = jnp.concatenate([lows[b], lows[b + 1]], 1)
        next_out[:, where] = left_dot(next_ref[...], low)
        low_ref[:, where] = left_dot(own_ref[...], low)
        high_ref[:, where] = left_dot(own_ref[...], jnp.concatenate([highs[b], highs[b + 1]], 1))


def middle_kernel(sizes, own_ref, edge_ref, s0, s1, s2, time_ref, timed_ref):
    rows, length = timed_ref.shape
    matrix = edge_ref[:rows]
    refs = (s0, s1, s2)
    scales = scales_of(refs)
    blocks = []
    for where in steps(own_ref):
        low, _ = take_joint(sizes, refs, scales, where)
        blocks.append(own_ref[:rows, where] + left_dot(matrix, low))
    lows, _ = time_analysis(blocks, time_ref[...])
    coarse = [jnp.concatenate([lows[b], lows[b + 1]], 1) for b in range(0, len(lows), 2)]
    lows, highs = time_analysis(coarse, time_ref[...])
    for b in range(len(coarse)):
        for base, piece in ((0, lows[b]), (length // 2, highs[b])):
            timed_ref[:, base + b * LANES : base + (b + 1) * LANES] = piece


def middle_details(thr_ref, blocks, time_matrix, time_t):
    lows, highs = time_analysis(blocks, time_matrix)
    quarter = blocks[0].shape[0] // 4
    pairs = []
    for b in range(len(blocks)):
        sides = []
        for piece, high in ((lows[b], 0), (highs[b], 1)):
            bands = [piece[q * quarter : (q + 1) * quarter] for q in range(4)]
            for q in range(4):
                bands[q] = shrink(bands[q], thr_ref[1, 2 * q + high - 1]) if q or high else jnp.zeros_like(bands[q])
            sides.append(jnp.concatenate(bands, 0))
        pairs.append(jnp.concatenate(sides, 1))
    return time_synthesis(pairs, time_t)


def sides_kernel(cols, before, own, after, stack_out, first_out, last_out):
    stack_out[...] = jnp.concatenate([before[...], own[...], after[...]], 0)
    starts = range(0, stack_out.shape[0], cols)
    first_out[...] = jnp.concatenate([stack_out[at : at + SIDE] for at in starts], 0)
    last_out[...] = jnp.concatenate([stack_out[at + cols - SIDE : at + cols] for at in starts], 0)


def details_kernel(
    sizes,
    thr_ref,
    low_in,
    high_in,
    edge_ref,
    s0,
    s1,
    s2,
    back_low,
    back_ref,
    next_in,
    next_edge,
    time_ref,
    time_t,
    next_back,
    low_out,
    high_out,
    low_states,
    high_states,
    next_out,
):
    quarter = low_in.shape[0] // 4
    refs = (s0, s1, s2)
    scales = scales_of(refs)
    blocks = []
    for where in steps(next_in):
        low, _ = take_joint(sizes, refs, scales, where)
        blocks.append(next_in[:, where] + left_dot(next_edge[...], low))
    next_states = []
    for b, block in enumerate(middle_details(thr_ref, blocks, time_ref[...], time_t[...])):
        next_out[:, b * BLOCK : (b + 1) * BLOCK] = block
        next_states.append(left_dot(next_back[...], block))
    for where in steps(low_in):
        low, high = take_joint(sizes, refs, scales, where)
        bands = low_in[quarter:, where] + left_dot(edge_ref[quarter:], low[: high.shape[0]])
        bands = [shrink(bands[(q - 1) * quarter : q * quarter], thr_ref[0, 2 * q - 1]) for q in range(1, 4)]
        bands = jnp.concatenate(bands, 0)
        low_out[:, where] = bands
        states = left_dot(back_low[...], bands)
        count = states.shape[0]
        more = next_states[where.start // BLOCK]
        low_states[:, where] = jnp.concatenate([states + more[:count], more[count:]], 0)
        bands = high_in[:, where] + left_dot(edge_ref[...], high)
        bands = [shrink(bands[q * quarter : (q + 1) * quarter], thr_ref[0, 2 * q]) for q in range(4)]
        bands = jnp.concatenate(bands, 0)
        high_out[:, where] = bands
        high_states[:, where] = left_dot(back_ref[...], bands)


def time_pairs(bands, matrix):
    half = bands.shape[1] // 2
    pairs = []
    for b in range(0, half, LANES):
        pairs.append(jnp.concatenate([bands[:, b : b + LANES], bands[:, half + b : half + b + LANES]], 1))
    return time_synthesis(pairs, matrix)


def deepest_kernel(
    sizes, thr_ref, before, own, after, bands_m, both_m, time_two, low_states, high_states, coarse_out, *outs
):
    stack = jnp.concatenate([before[...], own[...], after[...]], 0)
    bands = left_dot(bands_m[...], stack)
    row = lax.broadcasted_iota(jnp.int32, bands.shape, 0)
    high = lax.broadcasted_iota(jnp.int32, bands.shape, 1) >= bands.shape[1] // 2
    limit = jnp.where(high, thr_ref[2, 0], 0.0)
    quarter = bands.shape[0] // 4
    for q in range(1, 4):
        limit = jnp.where(row >= q * quarter, jnp.where(high, thr_ref[2, 2 * q], thr_ref[2, 2 * q - 1]), limit)
    state_lows, state_highs = [], []
    rows = coarse_out.shape[0]
    for b, block in enumerate(time_pairs(shrink(bands, limit), time_two[...])):
        where = slice(b * block.shape[1], (b + 1) * block.shape[1])
        both = left_dot(both_m[...], block)
        coarse_out[:, where] = both[:rows]
        low = both[rows:] + low_states[:, where]
        for at in range(0, block.shape[1], LANES):
            state_lows.append(low[:, at : at + LANES])
            state_highs.append(high_states[:, where.start + at : where.start + at + LANES])
    put_joint(sizes, outs, state_lows, state_highs)


def own_back_kernel(low_in, high_in, next_in, coarse_in, low_t, high_t, next_t, time_t, scale_ref, out_ref):
    blocks = []
    for where in steps(low_in):
        rows = coarse_in.shape[0]
        bands = jnp.concatenate([next_in[:rows, where] + coarse_in[:, where], next_in[rows:, where]], 0)
        low = left_dot(low_t[...], low_in[:, where]) + left_dot(next_t[...], bands)
        high = left_dot(high_t[...], high_in[:, where])
        for b in range(0, BLOCK, LANES):
            blocks.append(jnp.concatenate([low[:, b : b + LANES], high[:, b : b + LANES]], 1))
    scale = scale_ref[...]
    for b, block in enumerate(time_synthesis(blocks, time_t[...])):
        out_ref[:, b * BLOCK : (b + 1) * BLOCK] = block * scale


def final_kernel(sizes, own_ref, s0, s1, s2, time_t, time_low, state_t, scale_ref, out_far, out_ref, sems):
    pairs, lows = [], []
    refs = (s0, s1, s2)
    scales = scales_of(refs)
    for start in range(0, own_ref.shape[1] // 2, LANES):
        low, high = take_joint(sizes, refs, scales, slice(start, start + LANES))
        count = high.shape[0]
        pairs.append(jnp.concatenate([low[:count], high], 1))
        lows.append(low[count:])
    level0 = time_synthesis(pairs, time_t[...])
    level1 = synthesis_from_low(lows, time_low[...])
    scale = scale_ref[...]
    going = []
    for b in range(len(pairs)):
        where = slice(b * BLOCK, (b + 1) * BLOCK)
        states = jnp.concatenate([level0[b], level1[b]], 0)
        out_ref[:, where] = own_ref[:, where] + left_dot(state_t[...], states) * scale
        going.append(pltpu.make_async_copy(out_ref.at[:, where], out_far.at[:, where], sems.at[b]))
        going[-1].start()
    for copy in going:
        copy.wait()


def call(kernel, outs, *args, smem=(), far=(), far_outs=(), scratch=(), after=(), cost=None, limit=VMEM_LIMIT):
    spaces = [pltpu.SMEM if i in smem else pltpu.HBM if i in far else pltpu.VMEM for i in range(len(args))]
    spaces += [pl.ANY] * len(after)
    count = len(args)

    def body(*refs):
        kernel(*refs[:count], *refs[count + len(after) :])

    return pl.pallas_call(
        body,
        out_shape=[jax.ShapeDtypeStruct(shape, dtype) for shape, dtype in outs],
        in_specs=[pl.BlockSpec(memory_space=space) for space in spaces],
        out_specs=[
            pl.BlockSpec(memory_space=pltpu.HBM if i in far_outs else pltpu.VMEM) for i in range(len(outs))
        ],
        scratch_shapes=list(scratch),
        compiler_params=pltpu.CompilerParams(vmem_limit_bytes=limit),
        cost_estimate=None
        if cost is None
        else pl.CostEstimate(flops=int(cost), bytes_accessed=0, transcendentals=0),
    )(*args, *after)


def shift(block, inline_by, cross_by):
    inline_devs, cross_devs = lax.axis_size("inl"), lax.axis_size("xl")
    if not cross_by:
        return lax.ppermute(block, "inl", [((i + inline_by) % inline_devs, i) for i in range(inline_devs)])
    if not inline_by:
        return lax.ppermute(block, "xl", [((j + cross_by) % cross_devs, j) for j in range(cross_devs)])
    route = [
        ((i + inline_by) % inline_devs * cross_devs + (j + cross_by) % cross_devs, i * cross_devs + j)
        for i in range(inline_devs)
        for j in range(cross_devs)
    ]
    return lax.ppermute(block, ("inl", "xl"), route)


def exchange(states, ahead):
    corner = shift(states[2], ahead, ahead)
    column = shift(states[1], 0, ahead)
    return [shift(states[0], ahead, 0), column, corner]


def on_device(traces, dest_tile, bin_in_tile, fold, thresholds):
    devices = lax.axis_size("inl") * lax.axis_size("xl")
    trace_count, samples = traces.shape
    tile_rows, tile_cols = fold.shape
    bins = tile_rows * tile_cols
    width = SLOTS * samples // GROUP + LANES
    (outgoing,) = call(
        route_kernel,
        [((devices * GROUP, width), bf16)],
        dest_tile.reshape(1, trace_count),
        bin_in_tile.reshape(1, trace_count),
        traces,
        far=(0, 1, 2),
        far_outs=(0,),
        limit=LARGE_LIMIT,
        scratch=[
            pltpu.VMEM((1, trace_count), jnp.int32),
            pltpu.VMEM((1, trace_count), jnp.int32),
            pltpu.VMEM((trace_count, samples), bf16),
            pltpu.VMEM((devices * GROUP, width), bf16),
            pltpu.SemaphoreType.DMA((6,)),
            pltpu.SemaphoreType.DMA((4,)),
        ],
    )
    arrived = lax.all_to_all(
        outgoing.reshape(devices, GROUP, width), ("inl", "xl"), split_axis=0, concat_axis=0, tiled=True
    ).reshape(devices * GROUP, width)
    scale = (1.0 / jnp.sqrt(fold.astype(f32))).reshape(bins, 1)

    main, following = time_parts()
    time_matrix = np.concatenate([triple(main, 0), triple(following, 0)], 0)
    back_main, back_last = main.T, np.pad(following.T, ((0, 0), (0, BLOCK - LANES)))
    time_back = np.concatenate([triple(back_main, 0), triple(back_last, 0)], 0)
    twice, onward = np.zeros((2, BLOCK, 2 * BLOCK))
    twice[:LANES, :BLOCK] = twice[LANES:, BLOCK:] = back_main[:LANES]
    twice[:LANES, BLOCK:] = onward[LANES:, :BLOCK] = back_last[:LANES]
    last_two = back_last @ twice + back_main @ onward
    assert np.abs(back_last @ onward).max() == 0.0
    time_back_two = np.concatenate([triple(back_main @ twice, 0), triple(last_two, 0)], 0)
    time_back_low = np.concatenate([triple(back_main[:LANES], 0), triple(back_last[:LANES], 0)], 0)
    half, rows2, cols2 = samples // 2, tile_rows // 4, tile_cols // 4
    quarter, last = bins // 4, bins // 16
    own0, edge0, own1, edge1, states01, sizes = joint_matrices(tile_rows, tile_cols)
    assert rows2 == SIDE and cols2 >= SIDE
    bands2, back2 = side_matrices(rows2, cols2)
    count0 = sum(sizes[:3])
    joint_rows = [2 * sizes[0] + sizes[3], 2 * sizes[1] + sizes[4], sizes[2] + 8]
    joint_shapes = [((-(-rows // 16) * 16, half + LANES), jnp.int16) for rows in joint_rows]

    summed, *states = call(
        functools.partial(bin_kernel, sizes),
        [((bins, samples), f32)] + joint_shapes,
        arrived,
        scale,
        time_matrix,
        triple(states01, 1),
        far=(0,),
        limit=MIDDLE_LIMIT,
        scratch=[pltpu.VMEM((devices * GROUP, width), bf16), pltpu.SemaphoreType.DMA((4,))],
    )
    states = exchange(states, 1)
    own_low, own_high, own_next = call(
        own_kernel,
        [((bins, half), f32)] * 2 + [((quarter, half), f32)],
        summed,
        time_matrix,
        triple(own0, 1),
        triple(own1, 1),
        cost=1e9,
    )
    rows_all = rows2 + 2 * SIDE
    (timed,) = call(
        functools.partial(middle_kernel, sizes),
        [((last, half // 2), f32)],
        own_next,
        triple(edge1, 1),
        *states,
        time_matrix,
    )
    before, behind = shift(timed, -1, 0), shift(timed, 1, 0)
    low_details, high_details, low_states, high_states, next_details = call(
        functools.partial(details_kernel, sizes),
        [((bins - quarter, half), f32), ((bins, half), f32)]
        + [((sum(sizes), half), f32), ((count0, half), f32)]
        + [((quarter, half), f32)],
        thresholds,
        own_low,
        own_high,
        triple(edge0, 1),
        *states,
        triple(edge0[quarter:].T, 1),
        triple(edge0.T, 1),
        own_next,
        triple(edge1, 1),
        time_matrix,
        time_back,
        triple(edge1.T, 1),
        smem=(0,),
        after=(timed,),
        cost=1e9,
    )
    stack, firsts, lasts = call(
        functools.partial(sides_kernel, cols2),
        [((rows_all * size, samples // 4), f32) for size in (cols2, SIDE, SIDE)],
        before,
        timed,
        behind,
        after=(low_details,),
    )
    left, right = shift(lasts, 0, -1), shift(firsts, 0, 1)
    coarse1, *states = call(
        functools.partial(deepest_kernel, sizes),
        [((last, half), f32)] + joint_shapes,
        thresholds,
        left,
        stack,
        right,
        triple(bands2, 1),
        triple(np.concatenate([back2, edge1[:last].T @ back2], 0), 1),
        time_back_two,
        low_states,
        high_states,
        smem=(0,),
    )
    states = exchange(states, -1)
    (own_back,) = call(
        own_back_kernel,
        [((bins, samples), f32)],
        low_details,
        high_details,
        next_details,
        coarse1,
        triple(own0[quarter:].T, 1),
        triple(own0.T, 1),
        triple(own1.T, 1),
        time_back,
        scale,
        cost=1e9,
    )
    (denoised,) = call(
        functools.partial(final_kernel, sizes),
        [((bins, samples), f32)],
        own_back,
        *states,
        time_back,
        time_back_low,
        triple(states01.T, 1),
        scale,
        far_outs=(0,),
        scratch=[pltpu.VMEM((bins, samples), f32), pltpu.SemaphoreType.DMA((samples // BLOCK,))],
    )
    return denoised.reshape(tile_rows, tile_cols, samples)


def solution(mesh):
    placed = (P(("inl", "xl"), None), P(("inl", "xl"), None), P(("inl", "xl")), P("inl", "xl"), P())
    return jax.shard_map(
        on_device, mesh=mesh, in_specs=placed, out_specs=P("inl", "xl", None), check_vma=False
    )
```

```python
import functools

import jax
import jax.numpy as jnp
import ml_dtypes
import numpy as np
from jax import lax
from jax.experimental import pallas as pl
from jax.experimental.pallas import tpu as pltpu
from jax.sharding import PartitionSpec as P

LEVELS = 3
SLOTS = 6
GROUP = 8
LANES = 128
BLOCK = 256
VMEM_LIMIT = 32 * 1024 * 1024
LARGE_LIMIT = 62 * 1024 * 1024
MIDDLE_LIMIT = 48 * 1024 * 1024
TOP_CODE = 32767.0
FEW_ROWS = 80
LAST_MARK = 880.0
SIDE = 4

low_taps = [
    0.0352262918857095,
    -0.0854412738820267,
    -0.1350110200102546,
    0.4598775021184914,
    0.8068915093110924,
    0.3326705529500826,
]
high_taps = [(-1) ** offset * low_taps[5 - offset] for offset in range(6)]

bf16 = jnp.bfloat16
f32 = jnp.float32


def halves(matrix):
    top = np.asarray(matrix, np.float32).astype(ml_dtypes.bfloat16)
    rest = (np.asarray(matrix, np.float64) - top.astype(np.float64)).astype(ml_dtypes.bfloat16)
    return top, rest


def triple(matrix, axis):
    top, rest = halves(matrix)
    return np.concatenate([top, top, rest], axis)


def line_parts(length):
    half = length // 2
    whole = np.zeros((length, length + 4))
    for m in range(half):
        for k in range(6):
            whole[m, 2 * m + k] = low_taps[k]
            whole[half + m, 2 * m + k] = high_taps[k]
    left, sizes, right = np.linalg.svd(whole[:, length:])
    assert sizes[2] < 1e-9
    state = np.zeros((2, length))
    state[:, :4] = right[:2]
    return whole[:, :length], left[:, :2] * sizes[:2], state


def outer(on_rows, on_cols, banded):
    both = np.einsum("ar,bc->abrc", on_rows, on_cols)
    a, b, r, c = both.shape
    if banded:
        both = both.reshape(2, a // 2, 2, b // 2, r, c).transpose(2, 0, 1, 3, 4, 5)
    return both.reshape(a * b, r * c)


def two_levels(length):
    own0, edge0, state0 = line_parts(length)
    own1, edge1, state1 = line_parts(length // 2)
    low = slice(0, length // 2)
    assert np.abs(state1 @ edge0[low]).max() < 1e-9
    further = state1 @ own0[low]
    return dict(
        own0=own0,
        edge0=edge0,
        state0=state0,
        own1=own1 @ own0[low],
        far1=own1 @ edge0[low],
        edge1=edge1,
        further=further,
        states=np.concatenate([state0, further]),
    )


def joint_matrices(rows, cols):
    i, c = two_levels(rows), two_levels(cols)
    wide = [np.concatenate([d["edge0"], np.zeros_like(d["edge0"])], 1) for d in (i, c)]
    both = [np.concatenate([d["far1"], d["edge1"]], 1) for d in (i, c)]
    first = [0, 1, 4, 5] + [k for k in range(16) if k not in (0, 1, 4, 5)]
    own0 = outer(i["own0"], c["own0"], True)
    edge0 = [outer(i["edge0"], c["own0"], True), outer(i["own0"], c["edge0"], True), outer(*wide, True)[:, first]]
    own1 = outer(i["own1"], c["own1"], True)
    edge1 = [
        outer(i["far1"], c["own1"], True),
        outer(i["own1"], c["far1"], True),
        outer(*both, True)[:, first],
        outer(i["edge1"], np.eye(cols // 2), True),
        outer(np.eye(rows // 2), c["edge1"], True),
    ]
    states = [
        outer(i["state0"], np.eye(cols), False),
        outer(np.eye(rows), c["state0"], False),
        outer(i["states"], c["states"], False)[first],
        outer(i["further"], c["own1"], False),
        outer(i["own1"], c["further"], False),
    ]
    sizes = [len(part) for part in states]
    return own0, np.concatenate(edge0, 1), own1, np.concatenate(edge1, 1), np.concatenate(states, 0), sizes


def side_parts(length):
    firsts = range(-SIDE // 2, length // 2)
    count = len(firsts)
    bands = np.zeros((2 * count, length + 2 * SIDE))
    back = np.zeros((length, 2 * count))
    for m, first in enumerate(firsts):
        for k in range(6):
            for part, taps in ((0, low_taps), (count, high_taps)):
                bands[part + m, SIDE + 2 * first + k] = taps[k]
                if 0 <= 2 * first + k < length:
                    back[2 * first + k, part + m] = taps[k]
    return bands, back


def side_matrices(rows, cols):
    bands_i, back_i = side_parts(rows)
    bands_c, back_c = side_parts(cols)
    bands = outer(bands_i, bands_c, True)
    wide = cols + 2 * SIDE
    order = []
    for first, size in ((0, SIDE), (SIDE, cols), (SIDE + cols, SIDE)):
        order += [r * wide + first + c for r in range(rows + 2 * SIDE) for c in range(size)]
    back = outer(back_i.T, back_c.T, True).T
    return bands[:, order], back


def time_parts():
    whole = np.zeros((BLOCK + LANES, BLOCK))
    for m in range(LANES):
        for k in range(6):
            whole[2 * m + k, m] = low_taps[k]
            whole[2 * m + k, LANES + m] = high_taps[k]
    return whole[:BLOCK], whole[BLOCK:]


def split(value):
    top = value.astype(bf16)
    return top, (value - top.astype(f32)).astype(bf16)


def dot(left, right):
    return jnp.dot(left, right, preferred_element_type=f32)


def left_dot(matrix, value):
    top, rest = split(value)
    return dot(matrix, jnp.concatenate([top, rest, top], 0))


def beside(blocks, neighbours, matrix):
    count = blocks[0].shape[0]
    together = len(blocks) if count <= FEW_ROWS else 1
    results = []
    for b in range(0, len(blocks), together):
        top, rest = split(jnp.concatenate(blocks[b : b + together], 0))
        other, other_rest = split(jnp.concatenate(neighbours[b : b + together], 0))
        result = dot(jnp.concatenate([top, rest, top, other, other_rest, other], 1), matrix)
        results += [result[k * count : (k + 1) * count] for k in range(together)]
    return results


def time_analysis(blocks, matrix):
    results = beside(blocks, [block[:, :LANES] for block in blocks[1:] + blocks[:1]], matrix)
    return [result[:, :LANES] for result in results], [result[:, LANES:] for result in results]


def time_synthesis(blocks, matrix):
    return beside(blocks, blocks[-1:] + blocks[:-1], matrix)


def synthesis_from_low(lows, matrix):
    return beside(lows, lows[-1:] + lows[:-1], matrix)


def shrink(value, limit):
    return value - jnp.clip(value, -limit, limit)


def spread_rows(value):
    count, width = value.shape
    tiles = value.reshape(count // GROUP, GROUP, width)
    turned = [tiles if q == 3 else pltpu.roll(tiles, SLOTS - 2 * q, 1) for q in range(4)]
    return jnp.stack(turned, 1).reshape(4 * count, width)


def gather_rows(value, first, second):
    count, width = value.shape
    tiles = value.reshape(count // (4 * GROUP), 4, GROUP, width)
    row = lax.broadcasted_iota(jnp.int32, (count // (4 * GROUP), GROUP, width), 1)
    result = None
    for q in range(4):
        for at, source in ((2 * q, first), (2 * q + 1, second)):
            turn = (at - source) % GROUP
            part = pltpu.roll(tiles[:, q], turn, 1) if turn else tiles[:, q]
            result = part if result is None else jnp.where(row == at, part, result)
    return result.reshape(count // 4, width)


def route_kernel(dest_far, bin_far, traces_far, out_far, dest_ref, bin_ref, traces_ref, out_ref, in_sems, out_sems):
    traces, samples = traces_ref.shape
    rows = out_ref.shape[0]
    tiles = rows // GROUP
    span = samples // 4
    coming = [
        pltpu.make_async_copy(dest_far, dest_ref, in_sems.at[4]),
        pltpu.make_async_copy(bin_far, bin_ref, in_sems.at[5]),
    ]
    for j in (3, 0, 1, 2):
        at = pl.ds(j * span, span)
        coming.append(pltpu.make_async_copy(traces_far.at[:, at], traces_ref.at[:, at], in_sems.at[j]))
    for copy in coming:
        copy.start()
    before = lax.broadcasted_iota(jnp.int32, (traces, traces), 0) <= lax.broadcasted_iota(
        jnp.int32, (traces, traces), 1
    )
    before = before.astype(f32).astype(bf16)
    coming[0].wait()
    coming[1].wait()
    dest = dest_ref[...]
    matches = lax.broadcasted_iota(jnp.int32, (tiles, traces), 0) == dest
    counts = dot(matches.astype(f32).astype(bf16), before)
    place = jnp.sum(jnp.where(matches, counts, 0.0), 0, keepdims=True).astype(jnp.int32) - 1
    row_at = lax.broadcasted_iota(jnp.int32, (rows, traces), 0)
    main = (row_at == dest * GROUP + place).astype(f32).astype(bf16)
    going = []

    def send(number, first, width):
        at = pl.ds(first, width)
        going.append(pltpu.make_async_copy(out_ref.at[:, at], out_far.at[:, at], out_sems.at[number]))
        going[-1].start()

    code = bin_ref[...] + 1
    lane = lax.broadcasted_iota(jnp.int32, (LANES, traces), 0)
    digits = jnp.where(lane == 0, code // 2, jnp.where(lane == 1, code % 2, 0))
    labels = lax.dot_general(
        main,
        digits.astype(f32).astype(bf16),
        (((1,), (1,)), ((), ())),
        preferred_element_type=f32,
    )
    out_ref[:, 3 * span :] = labels.astype(bf16)
    send(3, 3 * span, LANES)
    count = GROUP - SLOTS
    tail_at = lax.broadcasted_iota(jnp.int32, (count * tiles, traces), 0)
    is_tail = lax.broadcasted_iota(jnp.int32, (rows, span), 0) % GROUP >= SLOTS
    coming[2].wait()
    tail = traces_ref[:, 3 * span : samples]
    for j in range(3):
        tail_row = jnp.where(place == j, 0, jnp.where(place == 3 + j, 1, -rows))
        extra = (tail_at == dest * count + tail_row).astype(f32).astype(bf16)
        rest = spread_rows(dot(extra, tail))
        at = slice(j * span, (j + 1) * span)
        coming[3 + j].wait()
        out_ref[:, at] = jnp.where(is_tail, rest, dot(main, traces_ref[:, at])).astype(bf16)
        send(j, j * span, span)
    for copy in going:
        copy.wait()


def bin_kernel(sizes, arrived_far, scale_ref, time_ref, state_ref, summed_ref, s0, s1, s2, arrived_ref, sems):
    outs = (s0, s1, s2)
    width = summed_ref.shape[1] // 4
    coming = []
    for j, (first, size) in enumerate([(3 * width, LANES)] + [(j * width, width) for j in range(3)]):
        at = pl.ds(first, size)
        coming.append(pltpu.make_async_copy(arrived_far.at[:, at], arrived_ref.at[:, at], sems.at[j]))
        coming[-1].start()
    coming[0].wait()
    rows = arrived_ref.shape[0]
    bins, samples = summed_ref.shape
    span = samples // 4
    labels = arrived_ref[:, 3 * span :]
    lane = lax.broadcasted_iota(jnp.int32, (GROUP, LANES), 1)
    weights = jnp.where(lane == 0, 2.0, jnp.where(lane == 1, 1.0, 0.0)).astype(bf16)
    code = lax.dot_general(
        weights, labels, (((1,), (1,)), ((), ())), preferred_element_type=f32
    ).astype(jnp.int32)
    at = lax.broadcasted_iota(jnp.int32, (GROUP, rows), 1) % GROUP
    code = jnp.where(at < SLOTS, code, 0) - 1
    bin_at = lax.broadcasted_iota(jnp.int32, (bins, rows), 0)
    main = (bin_at == code[:1]).astype(f32).astype(bf16)
    scale = scale_ref[...]
    pieces = []
    for j in range(3):
        coming[1 + j].wait()
        pieces.append(dot(main, arrived_ref[:, j * span : (j + 1) * span]))
    onehots, tails = [], []
    wide = labels.astype(f32)
    tail_at = lax.broadcasted_iota(jnp.int32, (bins, rows // 4), 0)
    for j in range(3):
        tail_labels = gather_rows(wide, j, 3 + j).astype(bf16)
        tail_code = lax.dot_general(
            weights, tail_labels, (((1,), (1,)), ((), ())), preferred_element_type=f32
        ).astype(jnp.int32)
        onehots.append((tail_at == tail_code[:1] - 1).astype(f32).astype(bf16))
        tails.append(gather_rows(arrived_ref[:, j * span : (j + 1) * span].astype(f32), SLOTS, SLOTS + 1).astype(bf16))
    last = dot(jnp.concatenate(onehots, 1), jnp.concatenate(tails, 0))
    pieces.append(last)
    matrix = state_ref[...]
    blocks = []
    for p, piece in enumerate(pieces):
        piece = piece * scale
        summed_ref[:, p * span : (p + 1) * span] = piece
        states = left_dot(matrix, piece)
        blocks += [states[:, b : b + BLOCK] for b in range(0, span, BLOCK)]
    lows, highs = time_analysis(blocks, time_ref[...])
    put_joint(sizes, outs, lows, highs)


def encode(pieces, out):
    lane = lax.broadcasted_iota(jnp.int32, (out.shape[0], LANES), 1)
    marks = jnp.zeros((out.shape[0], LANES), f32)
    for b, piece in enumerate(pieces):
        largest = jnp.max(jnp.abs(piece), 1, keepdims=True)
        mark = jnp.clip(jnp.ceil(jnp.log2(largest) * 8.0), -LAST_MARK, LAST_MARK)
        code = jnp.clip(jnp.round(piece * (jnp.exp2(mark * -0.125) * TOP_CODE)), -TOP_CODE, TOP_CODE)
        out[:, b * LANES : (b + 1) * LANES] = code.astype(jnp.int32).astype(jnp.int16)
        marks = jnp.where(lane == b, mark, marks)
    out[:, len(pieces) * LANES :] = marks.astype(jnp.int32).astype(jnp.int16)


def scales_of(refs):
    marks = [ref[:, ref.shape[1] - LANES :].astype(jnp.int32).astype(f32) for ref in refs]
    return [jnp.exp2(mark * 0.125) * (1.0 / TOP_CODE) for mark in marks]


def decode(ref, scale, where):
    pieces = []
    for start in range(where.start, where.stop, LANES):
        b = start // LANES
        code = ref[:, start : start + LANES].astype(jnp.int32).astype(f32)
        pieces.append(code * scale[:, b : b + 1])
    return jnp.concatenate(pieces, 1)


def put_joint(sizes, outs, lows, highs):
    ends = np.cumsum([0] + sizes)
    part = [slice(int(ends[k]), int(ends[k + 1])) for k in range(5)]

    def message(rows, *pieces):
        spare = rows - sum(piece.shape[0] for piece in pieces)
        if spare:
            pieces += (jnp.zeros((spare, LANES), f32),)
        return jnp.concatenate(pieces, 0)

    rows = [out.shape[0] for out in outs]
    pairs = list(zip(lows, highs))
    encode([message(rows[0], low[part[0]], high[part[0]], low[part[3]]) for low, high in pairs], outs[0])
    encode([message(rows[1], low[part[1]], high[part[1]], low[part[4]]) for low, high in pairs], outs[1])
    encode([message(rows[2], low[part[2]], high[part[2]][:8]) for low, high in pairs], outs[2])


def take_joint(sizes, refs, scales, where):
    r, c, d, further_r, further_c = sizes
    m0, m1, m2 = [decode(ref, scale, where) for ref, scale in zip(refs, scales)]
    low = [m0[:r], m1[:c], m2[:d], m0[2 * r : 2 * r + further_r], m1[2 * c : 2 * c + further_c]]
    high = [m0[r : 2 * r], m1[c : 2 * c], m2[d : d + 8], jnp.zeros((d - 8, m2.shape[1]), f32)]
    return jnp.concatenate(low, 0), jnp.concatenate(high, 0)


def join_rows(refs, where):
    return jnp.concatenate([ref[:, where] for ref in refs], 0)


def steps(ref):
    return [slice(start, start + BLOCK) for start in range(0, ref.shape[1], BLOCK)]


def own_kernel(summed_ref, time_ref, own_ref, next_ref, low_ref, high_ref, next_out):
    blocks = [summed_ref[:, where] for where in steps(summed_ref)]
    lows, highs = time_analysis(blocks, time_ref[...])
    for b in range(0, len(blocks), 2):
        where = slice(b * LANES, (b + 2) * LANES)
        low = jnp.concatenate([lows[b], lows[b + 1]], 1)
        next_out[:, where] = left_dot(next_ref[...], low)
        low_ref[:, where] = left_dot(own_ref[...], low)
        high_ref[:, where] = left_dot(own_ref[...], jnp.concatenate([highs[b], highs[b + 1]], 1))


def middle_kernel(sizes, own_ref, edge_ref, s0, s1, s2, time_ref, timed_ref):
    rows, length = timed_ref.shape
    matrix = edge_ref[:rows]
    refs = (s0, s1, s2)
    scales = scales_of(refs)
    blocks = []
    for where in steps(own_ref):
        low, _ = take_joint(sizes, refs, scales, where)
        blocks.append(own_ref[:rows, where] + left_dot(matrix, low))
    lows, _ = time_analysis(blocks, time_ref[...])
    coarse = [jnp.concatenate([lows[b], lows[b + 1]], 1) for b in range(0, len(lows), 2)]
    lows, highs = time_analysis(coarse, time_ref[...])
    for b in range(len(coarse)):
        for base, piece in ((0, lows[b]), (length // 2, highs[b])):
            timed_ref[:, base + b * LANES : base + (b + 1) * LANES] = piece


def middle_details(thr_ref, blocks, time_matrix, time_t):
    lows, highs = time_analysis(blocks, time_matrix)
    quarter = blocks[0].shape[0] // 4
    pairs = []
    for b in range(len(blocks)):
        sides = []
        for piece, high in ((lows[b], 0), (highs[b], 1)):
            bands = [piece[q * quarter : (q + 1) * quarter] for q in range(4)]
            for q in range(4):
                bands[q] = shrink(bands[q], thr_ref[1, 2 * q + high - 1]) if q or high else jnp.zeros_like(bands[q])
            sides.append(jnp.concatenate(bands, 0))
        pairs.append(jnp.concatenate(sides, 1))
    return time_synthesis(pairs, time_t)


def sides_kernel(cols, before, own, after, stack_out, first_out, last_out):
    stack_out[...] = jnp.concatenate([before[...], own[...], after[...]], 0)
    starts = range(0, stack_out.shape[0], cols)
    first_out[...] = jnp.concatenate([stack_out[at : at + SIDE] for at in starts], 0)
    last_out[...] = jnp.concatenate([stack_out[at + cols - SIDE : at + cols] for at in starts], 0)


def details_kernel(
    sizes,
    thr_ref,
    low_in,
    high_in,
    edge_ref,
    s0,
    s1,
    s2,
    back_low,
    back_ref,
    next_in,
    next_edge,
    time_ref,
    time_t,
    next_back,
    low_out,
    high_out,
    low_states,
    high_states,
    next_out,
):
    quarter = low_in.shape[0] // 4
    refs = (s0, s1, s2)
    scales = scales_of(refs)
    blocks = []
    for where in steps(next_in):
        low, _ = take_joint(sizes, refs, scales, where)
        blocks.append(next_in[:, where] + left_dot(next_edge[...], low))
    next_states = []
    for b, block in enumerate(middle_details(thr_ref, blocks, time_ref[...], time_t[...])):
        next_out[:, b * BLOCK : (b + 1) * BLOCK] = block
        next_states.append(left_dot(next_back[...], block))
    for where in steps(low_in):
        low, high = take_joint(sizes, refs, scales, where)
        bands = low_in[quarter:, where] + left_dot(edge_ref[quarter:], low[: high.shape[0]])
        bands = [shrink(bands[(q - 1) * quarter : q * quarter], thr_ref[0, 2 * q - 1]) for q in range(1, 4)]
        bands = jnp.concatenate(bands, 0)
        low_out[:, where] = bands
        states = left_dot(back_low[...], bands)
        count = states.shape[0]
        more = next_states[where.start // BLOCK]
        low_states[:, where] = jnp.concatenate([states + more[:count], more[count:]], 0)
        bands = high_in[:, where] + left_dot(edge_ref[...], high)
        bands = [shrink(bands[q * quarter : (q + 1) * quarter], thr_ref[0, 2 * q]) for q in range(4)]
        bands = jnp.concatenate(bands, 0)
        high_out[:, where] = bands
        high_states[:, where] = left_dot(back_ref[...], bands)


def time_pairs(bands, matrix):
    half = bands.shape[1] // 2
    pairs = []
    for b in range(0, half, LANES):
        pairs.append(jnp.concatenate([bands[:, b : b + LANES], bands[:, half + b : half + b + LANES]], 1))
    return time_synthesis(pairs, matrix)


def deepest_kernel(
    sizes, thr_ref, before, own, after, bands_m, both_m, time_two, low_states, high_states, coarse_out, *outs
):
    stack = jnp.concatenate([before[...], own[...], after[...]], 0)
    bands = left_dot(bands_m[...], stack)
    row = lax.broadcasted_iota(jnp.int32, bands.shape, 0)
    high = lax.broadcasted_iota(jnp.int32, bands.shape, 1) >= bands.shape[1] // 2
    limit = jnp.where(high, thr_ref[2, 0], 0.0)
    quarter = bands.shape[0] // 4
    for q in range(1, 4):
        limit = jnp.where(row >= q * quarter, jnp.where(high, thr_ref[2, 2 * q], thr_ref[2, 2 * q - 1]), limit)
    state_lows, state_highs = [], []
    rows = coarse_out.shape[0]
    for b, block in enumerate(time_pairs(shrink(bands, limit), time_two[...])):
        where = slice(b * block.shape[1], (b + 1) * block.shape[1])
        both = left_dot(both_m[...], block)
        coarse_out[:, where] = both[:rows]
        low = both[rows:] + low_states[:, where]
        for at in range(0, block.shape[1], LANES):
            state_lows.append(low[:, at : at + LANES])
            state_highs.append(high_states[:, where.start + at : where.start + at + LANES])
    put_joint(sizes, outs, state_lows, state_highs)


def own_back_kernel(low_in, high_in, next_in, coarse_in, low_t, high_t, next_t, time_t, scale_ref, out_ref):
    blocks = []
    for where in steps(low_in):
        rows = coarse_in.shape[0]
        bands = jnp.concatenate([next_in[:rows, where] + coarse_in[:, where], next_in[rows:, where]], 0)
        low = left_dot(low_t[...], low_in[:, where]) + left_dot(next_t[...], bands)
        high = left_dot(high_t[...], high_in[:, where])
        for b in range(0, BLOCK, LANES):
            blocks.append(jnp.concatenate([low[:, b : b + LANES], high[:, b : b + LANES]], 1))
    scale = scale_ref[...]
    for b, block in enumerate(time_synthesis(blocks, time_t[...])):
        out_ref[:, b * BLOCK : (b + 1) * BLOCK] = block * scale


def final_kernel(sizes, own_ref, s0, s1, s2, time_t, time_low, state_t, scale_ref, out_far, out_ref, sems):
    pairs, lows = [], []
    refs = (s0, s1, s2)
    scales = scales_of(refs)
    for start in range(0, own_ref.shape[1] // 2, LANES):
        low, high = take_joint(sizes, refs, scales, slice(start, start + LANES))
        count = high.shape[0]
        pairs.append(jnp.concatenate([low[:count], high], 1))
        lows.append(low[count:])
    level0 = time_synthesis(pairs, time_t[...])
    level1 = synthesis_from_low(lows, time_low[...])
    scale = scale_ref[...]
    going = []
    for b in range(len(pairs)):
        where = slice(b * BLOCK, (b + 1) * BLOCK)
        states = jnp.concatenate([level0[b], level1[b]], 0)
        out_ref[:, where] = own_ref[:, where] + left_dot(state_t[...], states) * scale
        going.append(pltpu.make_async_copy(out_ref.at[:, where], out_far.at[:, where], sems.at[b]))
        going[-1].start()
    for copy in going:
        copy.wait()


def call(kernel, outs, *args, smem=(), far=(), far_outs=(), scratch=(), after=(), cost=None, limit=VMEM_LIMIT):
    spaces = [pltpu.SMEM if i in smem else pltpu.HBM if i in far else pltpu.VMEM for i in range(len(args))]
    spaces += [pl.ANY] * len(after)
    count = len(args)

    def body(*refs):
        kernel(*refs[:count], *refs[count + len(after) :])

    return pl.pallas_call(
        body,
        out_shape=[jax.ShapeDtypeStruct(shape, dtype) for shape, dtype in outs],
        in_specs=[pl.BlockSpec(memory_space=space) for space in spaces],
        out_specs=[
            pl.BlockSpec(memory_space=pltpu.HBM if i in far_outs else pltpu.VMEM) for i in range(len(outs))
        ],
        scratch_shapes=list(scratch),
        compiler_params=pltpu.CompilerParams(vmem_limit_bytes=limit),
        cost_estimate=None
        if cost is None
        else pl.CostEstimate(flops=int(cost), bytes_accessed=0, transcendentals=0),
    )(*args, *after)


def shift(block, inline_by, cross_by):
    inline_devs, cross_devs = lax.axis_size("inl"), lax.axis_size("xl")
    if not cross_by:
        return lax.ppermute(block, "inl", [((i + inline_by) % inline_devs, i) for i in range(inline_devs)])
    if not inline_by:
        return lax.ppermute(block, "xl", [((j + cross_by) % cross_devs, j) for j in range(cross_devs)])
    route = [
        ((i + inline_by) % inline_devs * cross_devs + (j + cross_by) % cross_devs, i * cross_devs + j)
        for i in range(inline_devs)
        for j in range(cross_devs)
    ]
    return lax.ppermute(block, ("inl", "xl"), route)


def exchange(states, ahead):
    corner = shift(states[2], ahead, ahead)
    column = shift(states[1], 0, ahead)
    return [shift(states[0], ahead, 0), column, corner]


def on_device(traces, dest_tile, bin_in_tile, fold, thresholds):
    devices = lax.axis_size("inl") * lax.axis_size("xl")
    trace_count, samples = traces.shape
    tile_rows, tile_cols = fold.shape
    bins = tile_rows * tile_cols
    width = SLOTS * samples // GROUP + LANES
    (outgoing,) = call(
        route_kernel,
        [((devices * GROUP, width), bf16)],
        dest_tile.reshape(1, trace_count),
        bin_in_tile.reshape(1, trace_count),
        traces,
        far=(0, 1, 2),
        far_outs=(0,),
        limit=LARGE_LIMIT,
        scratch=[
            pltpu.VMEM((1, trace_count), jnp.int32),
            pltpu.VMEM((1, trace_count), jnp.int32),
            pltpu.VMEM((trace_count, samples), bf16),
            pltpu.VMEM((devices * GROUP, width), bf16),
            pltpu.SemaphoreType.DMA((6,)),
            pltpu.SemaphoreType.DMA((4,)),
        ],
    )
    arrived = lax.all_to_all(
        outgoing.reshape(devices, GROUP, width), ("inl", "xl"), split_axis=0, concat_axis=0, tiled=True
    ).reshape(devices * GROUP, width)
    scale = (1.0 / jnp.sqrt(fold.astype(f32))).reshape(bins, 1)

    main, following = time_parts()
    time_matrix = np.concatenate([triple(main, 0), triple(following, 0)], 0)
    back_main, back_last = main.T, np.pad(following.T, ((0, 0), (0, BLOCK - LANES)))
    time_back = np.concatenate([triple(back_main, 0), triple(back_last, 0)], 0)
    twice, onward = np.zeros((2, BLOCK, 2 * BLOCK))
    twice[:LANES, :BLOCK] = twice[LANES:, BLOCK:] = back_main[:LANES]
    twice[:LANES, BLOCK:] = onward[LANES:, :BLOCK] = back_last[:LANES]
    last_two = back_last @ twice + back_main @ onward
    assert np.abs(back_last @ onward).max() == 0.0
    time_back_two = np.concatenate([triple(back_main @ twice, 0), triple(last_two, 0)], 0)
    time_back_low = np.concatenate([triple(back_main[:LANES], 0), triple(back_last[:LANES], 0)], 0)
    half, rows2, cols2 = samples // 2, tile_rows // 4, tile_cols // 4
    quarter, last = bins // 4, bins // 16
    own0, edge0, own1, edge1, states01, sizes = joint_matrices(tile_rows, tile_cols)
    assert rows2 == SIDE and cols2 >= SIDE
    bands2, back2 = side_matrices(rows2, cols2)
    count0 = sum(sizes[:3])
    joint_rows = [2 * sizes[0] + sizes[3], 2 * sizes[1] + sizes[4], sizes[2] + 8]
    joint_shapes = [((-(-rows // 16) * 16, half + LANES), jnp.int16) for rows in joint_rows]

    summed, *states = call(
        functools.partial(bin_kernel, sizes),
        [((bins, samples), f32)] + joint_shapes,
        arrived,
        scale,
        time_matrix,
        triple(states01, 1),
        far=(0,),
        limit=MIDDLE_LIMIT,
        scratch=[pltpu.VMEM((devices * GROUP, width), bf16), pltpu.SemaphoreType.DMA((4,))],
    )
    states = exchange(states, 1)
    own_low, own_high, own_next = call(
        own_kernel,
        [((bins, half), f32)] * 2 + [((quarter, half), f32)],
        summed,
        time_matrix,
        triple(own0, 1),
        triple(own1, 1),
        cost=1e9,
    )
    rows_all = rows2 + 2 * SIDE
    (timed,) = call(
        functools.partial(middle_kernel, sizes),
        [((last, half // 2), f32)],
        own_next,
        triple(edge1, 1),
        *states,
        time_matrix,
    )
    before, behind = shift(timed, -1, 0), shift(timed, 1, 0)
    low_details, high_details, low_states, high_states, next_details = call(
        functools.partial(details_kernel, sizes),
        [((bins - quarter, half), f32), ((bins, half), f32)]
        + [((sum(sizes), half), f32), ((count0, half), f32)]
        + [((quarter, half), f32)],
        thresholds,
        own_low,
        own_high,
        triple(edge0, 1),
        *states,
        triple(edge0[quarter:].T, 1),
        triple(edge0.T, 1),
        own_next,
        triple(edge1, 1),
        time_matrix,
        time_back,
        triple(edge1.T, 1),
        smem=(0,),
        after=(timed,),
        cost=1e9,
    )
    stack, firsts, lasts = call(
        functools.partial(sides_kernel, cols2),
        [((rows_all * size, samples // 4), f32) for size in (cols2, SIDE, SIDE)],
        before,
        timed,
        behind,
        after=(low_details,),
    )
    left, right = shift(lasts, 0, -1), shift(firsts, 0, 1)
    coarse1, *states = call(
        functools.partial(deepest_kernel, sizes),
        [((last, half), f32)] + joint_shapes,
        thresholds,
        left,
        stack,
        right,
        triple(bands2, 1),
        triple(np.concatenate([back2, edge1[:last].T @ back2], 0), 1),
        time_back_two,
        low_states,
        high_states,
        smem=(0,),
    )
    states = exchange(states, -1)
    (own_back,) = call(
        own_back_kernel,
        [((bins, samples), f32)],
        low_details,
        high_details,
        next_details,
        coarse1,
        triple(own0[quarter:].T, 1),
        triple(own0.T, 1),
        triple(own1.T, 1),
        time_back,
        scale,
        cost=1e9,
    )
    (denoised,) = call(
        functools.partial(final_kernel, sizes),
        [((bins, samples), f32)],
        own_back,
        *states,
        time_back,
        time_back_low,
        triple(states01.T, 1),
        scale,
        far_outs=(0,),
        scratch=[pltpu.VMEM((bins, samples), f32), pltpu.SemaphoreType.DMA((samples // BLOCK,))],
    )
    return denoised.reshape(tile_rows, tile_cols, samples)


def solution(mesh):
    placed = (P(("inl", "xl"), None), P(("inl", "xl"), None), P(("inl", "xl")), P("inl", "xl"), P())
    return jax.shard_map(
        on_device, mesh=mesh, in_specs=placed, out_specs=P("inl", "xl", None), check_vma=False
    )
```

```python
import functools

import jax
import jax.numpy as jnp
import ml_dtypes
import numpy as np
from jax import lax
from jax.experimental import pallas as pl
from jax.experimental.pallas import tpu as pltpu
from jax.sharding import PartitionSpec as P

LEVELS = 3
SLOTS = 6
GROUP = 8
LANES = 128
BLOCK = 256
VMEM_LIMIT = 32 * 1024 * 1024
LARGE_LIMIT = 62 * 1024 * 1024
MIDDLE_LIMIT = 48 * 1024 * 1024
TOP_CODE = 32767.0
FEW_ROWS = 160
LAST_MARK = 880.0
SIDE = 4

low_taps = [
    0.0352262918857095,
    -0.0854412738820267,
    -0.1350110200102546,
    0.4598775021184914,
    0.8068915093110924,
    0.3326705529500826,
]
high_taps = [(-1) ** offset * low_taps[5 - offset] for offset in range(6)]

bf16 = jnp.bfloat16
f32 = jnp.float32


def halves(matrix):
    top = np.asarray(matrix, np.float32).astype(ml_dtypes.bfloat16)
    rest = (np.asarray(matrix, np.float64) - top.astype(np.float64)).astype(ml_dtypes.bfloat16)
    return top, rest


def triple(matrix, axis):
    top, rest = halves(matrix)
    return np.concatenate([top, top, rest], axis)


def line_parts(length):
    half = length // 2
    whole = np.zeros((length, length + 4))
    for m in range(half):
        for k in range(6):
            whole[m, 2 * m + k] = low_taps[k]
            whole[half + m, 2 * m + k] = high_taps[k]
    left, sizes, right = np.linalg.svd(whole[:, length:])
    assert sizes[2] < 1e-9
    state = np.zeros((2, length))
    state[:, :4] = right[:2]
    return whole[:, :length], left[:, :2] * sizes[:2], state


def outer(on_rows, on_cols, banded):
    both = np.einsum("ar,bc->abrc", on_rows, on_cols)
    a, b, r, c = both.shape
    if banded:
        both = both.reshape(2, a // 2, 2, b // 2, r, c).transpose(2, 0, 1, 3, 4, 5)
    return both.reshape(a * b, r * c)


def two_levels(length):
    own0, edge0, state0 = line_parts(length)
    own1, edge1, state1 = line_parts(length // 2)
    low = slice(0, length // 2)
    assert np.abs(state1 @ edge0[low]).max() < 1e-9
    further = state1 @ own0[low]
    return dict(
        own0=own0,
        edge0=edge0,
        state0=state0,
        own1=own1 @ own0[low],
        far1=own1 @ edge0[low],
        edge1=edge1,
        further=further,
        states=np.concatenate([state0, further]),
    )


def joint_matrices(rows, cols):
    i, c = two_levels(rows), two_levels(cols)
    wide = [np.concatenate([d["edge0"], np.zeros_like(d["edge0"])], 1) for d in (i, c)]
    both = [np.concatenate([d["far1"], d["edge1"]], 1) for d in (i, c)]
    first = [0, 1, 4, 5] + [k for k in range(16) if k not in (0, 1, 4, 5)]
    own0 = outer(i["own0"], c["own0"], True)
    edge0 = [outer(i["edge0"], c["own0"], True), outer(i["own0"], c["edge0"], True), outer(*wide, True)[:, first]]
    own1 = outer(i["own1"], c["own1"], True)
    edge1 = [
        outer(i["far1"], c["own1"], True),
        outer(i["own1"], c["far1"], True),
        outer(*both, True)[:, first],
        outer(i["edge1"], np.eye(cols // 2), True),
        outer(np.eye(rows // 2), c["edge1"], True),
    ]
    states = [
        outer(i["state0"], np.eye(cols), False),
        outer(np.eye(rows), c["state0"], False),
        outer(i["states"], c["states"], False)[first],
        outer(i["further"], c["own1"], False),
        outer(i["own1"], c["further"], False),
    ]
    sizes = [len(part) for part in states]
    return own0, np.concatenate(edge0, 1), own1, np.concatenate(edge1, 1), np.concatenate(states, 0), sizes


def side_parts(length):
    firsts = range(-SIDE // 2, length // 2)
    count = len(firsts)
    bands = np.zeros((2 * count, length + 2 * SIDE))
    back = np.zeros((length, 2 * count))
    for m, first in enumerate(firsts):
        for k in range(6):
            for part, taps in ((0, low_taps), (count, high_taps)):
                bands[part + m, SIDE + 2 * first + k] = taps[k]
                if 0 <= 2 * first + k < length:
                    back[2 * first + k, part + m] = taps[k]
    return bands, back


def side_matrices(rows, cols):
    bands_i, back_i = side_parts(rows)
    bands_c, back_c = side_parts(cols)
    bands = outer(bands_i, bands_c, True)
    wide = cols + 2 * SIDE
    order = []
    for first, size in ((0, SIDE), (SIDE, cols), (SIDE + cols, SIDE)):
        order += [r * wide + first + c for r in range(rows + 2 * SIDE) for c in range(size)]
    back = outer(back_i.T, back_c.T, True).T
    return bands[:, order], back


def time_parts():
    whole = np.zeros((BLOCK + LANES, BLOCK))
    for m in range(LANES):
        for k in range(6):
            whole[2 * m + k, m] = low_taps[k]
            whole[2 * m + k, LANES + m] = high_taps[k]
    return whole[:BLOCK], whole[BLOCK:]


def split(value):
    top = value.astype(bf16)
    return top, (value - top.astype(f32)).astype(bf16)


def dot(left, right):
    return jnp.dot(left, right, preferred_element_type=f32)


def left_dot(matrix, value):
    top, rest = split(value)
    return dot(matrix, jnp.concatenate([top, rest, top], 0))


def beside(blocks, neighbours, matrix):
    count = blocks[0].shape[0]
    together = len(blocks) if count <= FEW_ROWS else 1
    results = []
    for b in range(0, len(blocks), together):
        top, rest = split(jnp.concatenate(blocks[b : b + together], 0))
        other, other_rest = split(jnp.concatenate(neighbours[b : b + together], 0))
        result = dot(jnp.concatenate([top, rest, top, other, other_rest, other], 1), matrix)
        results += [result[k * count : (k + 1) * count] for k in range(together)]
    return results


def time_analysis(blocks, matrix):
    results = beside(blocks, [block[:, :LANES] for block in blocks[1:] + blocks[:1]], matrix)
    return [result[:, :LANES] for result in results], [result[:, LANES:] for result in results]


def time_synthesis(blocks, matrix):
    return beside(blocks, blocks[-1:] + blocks[:-1], matrix)


def synthesis_from_low(lows, matrix):
    return beside(lows, lows[-1:] + lows[:-1], matrix)


def shrink(value, limit):
    return value - jnp.clip(value, -limit, limit)


def spread_rows(value):
    count, width = value.shape
    tiles = value.reshape(count // GROUP, GROUP, width)
    turned = [tiles if q == 3 else pltpu.roll(tiles, SLOTS - 2 * q, 1) for q in range(4)]
    return jnp.stack(turned, 1).reshape(4 * count, width)


def gather_rows(value, first, second):
    count, width = value.shape
    tiles = value.reshape(count // (4 * GROUP), 4, GROUP, width)
    row = lax.broadcasted_iota(jnp.int32, (count // (4 * GROUP), GROUP, width), 1)
    result = None
    for q in range(4):
        for at, source in ((2 * q, first), (2 * q + 1, second)):
            turn = (at - source) % GROUP
            part = pltpu.roll(tiles[:, q], turn, 1) if turn else tiles[:, q]
            result = part if result is None else jnp.where(row == at, part, result)
    return result.reshape(count // 4, width)


def route_kernel(dest_far, bin_far, traces_far, out_far, dest_ref, bin_ref, traces_ref, out_ref, in_sems, out_sems):
    traces, samples = traces_ref.shape
    rows = out_ref.shape[0]
    tiles = rows // GROUP
    span = samples // 4
    coming = [
        pltpu.make_async_copy(dest_far, dest_ref, in_sems.at[4]),
        pltpu.make_async_copy(bin_far, bin_ref, in_sems.at[5]),
    ]
    for j in (3, 0, 1, 2):
        at = pl.ds(j * span, span)
        coming.append(pltpu.make_async_copy(traces_far.at[:, at], traces_ref.at[:, at], in_sems.at[j]))
    for copy in coming:
        copy.start()
    before = lax.broadcasted_iota(jnp.int32, (traces, traces), 0) <= lax.broadcasted_iota(
        jnp.int32, (traces, traces), 1
    )
    before = before.astype(f32).astype(bf16)
    coming[0].wait()
    coming[1].wait()
    dest = dest_ref[...]
    matches = lax.broadcasted_iota(jnp.int32, (tiles, traces), 0) == dest
    counts = dot(matches.astype(f32).astype(bf16), before)
    place = jnp.sum(jnp.where(matches, counts, 0.0), 0, keepdims=True).astype(jnp.int32) - 1
    row_at = lax.broadcasted_iota(jnp.int32, (rows, traces), 0)
    main = (row_at == dest * GROUP + place).astype(f32).astype(bf16)
    going = []

    def send(number, first, width):
        at = pl.ds(first, width)
        going.append(pltpu.make_async_copy(out_ref.at[:, at], out_far.at[:, at], out_sems.at[number]))
        going[-1].start()

    count = GROUP - SLOTS
    tail_at = lax.broadcasted_iota(jnp.int32, (count * tiles, traces), 0)
    is_tail = lax.broadcasted_iota(jnp.int32, (rows, span), 0) % GROUP >= SLOTS
    coming[2].wait()
    tail = traces_ref[:, 3 * span : samples]
    for j in range(3):
        tail_row = jnp.where(place == j, 0, jnp.where(place == 3 + j, 1, -rows))
        extra = (tail_at == dest * count + tail_row).astype(f32).astype(bf16)
        rest = spread_rows(dot(extra, tail))
        at = slice(j * span, (j + 1) * span)
        coming[3 + j].wait()
        out_ref[:, at] = jnp.where(is_tail, rest, dot(main, traces_ref[:, at])).astype(bf16)
        send(j, j * span, span)
    code = bin_ref[...] + 1
    lane = lax.broadcasted_iota(jnp.int32, (LANES, traces), 0)
    digits = jnp.where(lane == 0, code // 2, jnp.where(lane == 1, code % 2, 0))
    labels = lax.dot_general(
        main,
        digits.astype(f32).astype(bf16),
        (((1,), (1,)), ((), ())),
        preferred_element_type=f32,
    )
    out_ref[:, 3 * span :] = labels.astype(bf16)
    send(3, 3 * span, LANES)
    for copy in going:
        copy.wait()


def bin_kernel(sizes, arrived_far, scale_ref, time_ref, state_ref, summed_ref, s0, s1, s2, arrived_ref, sems):
    outs = (s0, s1, s2)
    width = summed_ref.shape[1] // 4
    coming = []
    for j, (first, size) in enumerate([(3 * width, LANES)] + [(j * width, width) for j in range(3)]):
        at = pl.ds(first, size)
        coming.append(pltpu.make_async_copy(arrived_far.at[:, at], arrived_ref.at[:, at], sems.at[j]))
        coming[-1].start()
    coming[0].wait()
    rows = arrived_ref.shape[0]
    bins, samples = summed_ref.shape
    span = samples // 4
    labels = arrived_ref[:, 3 * span :]
    lane = lax.broadcasted_iota(jnp.int32, (GROUP, LANES), 1)
    weights = jnp.where(lane == 0, 2.0, jnp.where(lane == 1, 1.0, 0.0)).astype(bf16)
    code = lax.dot_general(
        weights, labels, (((1,), (1,)), ((), ())), preferred_element_type=f32
    ).astype(jnp.int32)
    at = lax.broadcasted_iota(jnp.int32, (GROUP, rows), 1) % GROUP
    code = jnp.where(at < SLOTS, code, 0) - 1
    bin_at = lax.broadcasted_iota(jnp.int32, (bins, rows), 0)
    main = (bin_at == code[:1]).astype(f32).astype(bf16)
    scale = scale_ref[...]
    pieces = []
    for j in range(3):
        coming[1 + j].wait()
        pieces.append(dot(main, arrived_ref[:, j * span : (j + 1) * span]))
    onehots, tails = [], []
    wide = labels.astype(f32)
    tail_at = lax.broadcasted_iota(jnp.int32, (bins, rows // 4), 0)
    for j in range(3):
        tail_labels = gather_rows(wide, j, 3 + j).astype(bf16)
        tail_code = lax.dot_general(
            weights, tail_labels, (((1,), (1,)), ((), ())), preferred_element_type=f32
        ).astype(jnp.int32)
        onehots.append((tail_at == tail_code[:1] - 1).astype(f32).astype(bf16))
        tails.append(gather_rows(arrived_ref[:, j * span : (j + 1) * span].astype(f32), SLOTS, SLOTS + 1).astype(bf16))
    last = dot(jnp.concatenate(onehots, 1), jnp.concatenate(tails, 0))
    pieces.append(last)
    matrix = state_ref[...]
    blocks = []
    for p, piece in enumerate(pieces):
        piece = piece * scale
        summed_ref[:, p * span : (p + 1) * span] = piece
        states = left_dot(matrix, piece)
        blocks += [states[:, b : b + BLOCK] for b in range(0, span, BLOCK)]
    lows, highs = time_analysis(blocks, time_ref[...])
    put_joint(sizes, outs, lows, highs)


def encode(pieces, out):
    lane = lax.broadcasted_iota(jnp.int32, (out.shape[0], LANES), 1)
    marks = jnp.zeros((out.shape[0], LANES), f32)
    for b, piece in enumerate(pieces):
        largest = jnp.max(jnp.abs(piece), 1, keepdims=True)
        mark = jnp.clip(jnp.ceil(jnp.log2(largest) * 8.0), -LAST_MARK, LAST_MARK)
        code = jnp.clip(jnp.round(piece * (jnp.exp2(mark * -0.125) * TOP_CODE)), -TOP_CODE, TOP_CODE)
        out[:, b * LANES : (b + 1) * LANES] = code.astype(jnp.int32).astype(jnp.int16)
        marks = jnp.where(lane == b, mark, marks)
    out[:, len(pieces) * LANES :] = marks.astype(jnp.int32).astype(jnp.int16)


def scales_of(refs):
    marks = [ref[:, ref.shape[1] - LANES :].astype(jnp.int32).astype(f32) for ref in refs]
    return [jnp.exp2(mark * 0.125) * (1.0 / TOP_CODE) for mark in marks]


def decode(ref, scale, where):
    pieces = []
    for start in range(where.start, where.stop, LANES):
        b = start // LANES
        code = ref[:, start : start + LANES].astype(jnp.int32).astype(f32)
        pieces.append(code * scale[:, b : b + 1])
    return jnp.concatenate(pieces, 1)


def put_joint(sizes, outs, lows, highs):
    ends = np.cumsum([0] + sizes)
    part = [slice(int(ends[k]), int(ends[k + 1])) for k in range(5)]

    def message(rows, *pieces):
        spare = rows - sum(piece.shape[0] for piece in pieces)
        if spare:
            pieces += (jnp.zeros((spare, LANES), f32),)
        return jnp.concatenate(pieces, 0)

    rows = [out.shape[0] for out in outs]
    pairs = list(zip(lows, highs))
    encode([message(rows[0], low[part[0]], high[part[0]], low[part[3]]) for low, high in pairs], outs[0])
    encode([message(rows[1], low[part[1]], high[part[1]], low[part[4]]) for low, high in pairs], outs[1])
    encode([message(rows[2], low[part[2]], high[part[2]][:8]) for low, high in pairs], outs[2])


def take_joint(sizes, refs, scales, where):
    r, c, d, further_r, further_c = sizes
    m0, m1, m2 = [decode(ref, scale, where) for ref, scale in zip(refs, scales)]
    low = [m0[:r], m1[:c], m2[:d], m0[2 * r : 2 * r + further_r], m1[2 * c : 2 * c + further_c]]
    high = [m0[r : 2 * r], m1[c : 2 * c], m2[d : d + 8], jnp.zeros((d - 8, m2.shape[1]), f32)]
    return jnp.concatenate(low, 0), jnp.concatenate(high, 0)


def join_rows(refs, where):
    return jnp.concatenate([ref[:, where] for ref in refs], 0)


def steps(ref):
    return [slice(start, start + BLOCK) for start in range(0, ref.shape[1], BLOCK)]


def own_kernel(summed_ref, time_ref, own_ref, next_ref, low_ref, high_ref, next_out):
    blocks = [summed_ref[:, where] for where in steps(summed_ref)]
    lows, highs = time_analysis(blocks, time_ref[...])
    for b in range(0, len(blocks), 2):
        where = slice(b * LANES, (b + 2) * LANES)
        low = jnp.concatenate([lows[b], lows[b + 1]], 1)
        next_out[:, where] = left_dot(next_ref[...], low)
        low_ref[:, where] = left_dot(own_ref[...], low)
        high_ref[:, where] = left_dot(own_ref[...], jnp.concatenate([highs[b], highs[b + 1]], 1))


def middle_kernel(sizes, own_ref, edge_ref, s0, s1, s2, time_ref, timed_ref):
    rows, length = timed_ref.shape
    matrix = edge_ref[:rows]
    refs = (s0, s1, s2)
    scales = scales_of(refs)
    blocks = []
    for where in steps(own_ref):
        low, _ = take_joint(sizes, refs, scales, where)
        blocks.append(own_ref[:rows, where] + left_dot(matrix, low))
    lows, _ = time_analysis(blocks, time_ref[...])
    coarse = [jnp.concatenate([lows[b], lows[b + 1]], 1) for b in range(0, len(lows), 2)]
    lows, highs = time_analysis(coarse, time_ref[...])
    for b in range(len(coarse)):
        for base, piece in ((0, lows[b]), (length // 2, highs[b])):
            timed_ref[:, base + b * LANES : base + (b + 1) * LANES] = piece


def middle_details(thr_ref, blocks, time_matrix, time_t):
    lows, highs = time_analysis(blocks, time_matrix)
    quarter = blocks[0].shape[0] // 4
    pairs = []
    for b in range(len(blocks)):
        sides = []
        for piece, high in ((lows[b], 0), (highs[b], 1)):
            bands = [piece[q * quarter : (q + 1) * quarter] for q in range(4)]
            for q in range(4):
                bands[q] = shrink(bands[q], thr_ref[1, 2 * q + high - 1]) if q or high else jnp.zeros_like(bands[q])
            sides.append(jnp.concatenate(bands, 0))
        pairs.append(jnp.concatenate(sides, 1))
    return time_synthesis(pairs, time_t)


def sides_kernel(cols, before, own, after, stack_out, first_out, last_out):
    stack_out[...] = jnp.concatenate([before[...], own[...], after[...]], 0)
    starts = range(0, stack_out.shape[0], cols)
    first_out[...] = jnp.concatenate([stack_out[at : at + SIDE] for at in starts], 0)
    last_out[...] = jnp.concatenate([stack_out[at + cols - SIDE : at + cols] for at in starts], 0)


def details_kernel(
    sizes,
    thr_ref,
    low_in,
    high_in,
    edge_ref,
    s0,
    s1,
    s2,
    back_low,
    back_ref,
    next_in,
    next_edge,
    time_ref,
    time_t,
    next_back,
    low_out,
    high_out,
    low_states,
    high_states,
    next_out,
):
    quarter = low_in.shape[0] // 4
    refs = (s0, s1, s2)
    scales = scales_of(refs)
    blocks = []
    for where in steps(next_in):
        low, _ = take_joint(sizes, refs, scales, where)
        blocks.append(next_in[:, where] + left_dot(next_edge[...], low))
    next_states = []
    for b, block in enumerate(middle_details(thr_ref, blocks, time_ref[...], time_t[...])):
        next_out[:, b * BLOCK : (b + 1) * BLOCK] = block
        next_states.append(left_dot(next_back[...], block))
    for where in steps(low_in):
        low, high = take_joint(sizes, refs, scales, where)
        bands = low_in[quarter:, where] + left_dot(edge_ref[quarter:], low[: high.shape[0]])
        bands = [shrink(bands[(q - 1) * quarter : q * quarter], thr_ref[0, 2 * q - 1]) for q in range(1, 4)]
        bands = jnp.concatenate(bands, 0)
        low_out[:, where] = bands
        states = left_dot(back_low[...], bands)
        count = states.shape[0]
        more = next_states[where.start // BLOCK]
        low_states[:, where] = jnp.concatenate([states + more[:count], more[count:]], 0)
        bands = high_in[:, where] + left_dot(edge_ref[...], high)
        bands = [shrink(bands[q * quarter : (q + 1) * quarter], thr_ref[0, 2 * q]) for q in range(4)]
        bands = jnp.concatenate(bands, 0)
        high_out[:, where] = bands
        high_states[:, where] = left_dot(back_ref[...], bands)


def time_pairs(bands, matrix):
    half = bands.shape[1] // 2
    pairs = []
    for b in range(0, half, LANES):
        pairs.append(jnp.concatenate([bands[:, b : b + LANES], bands[:, half + b : half + b + LANES]], 1))
    return time_synthesis(pairs, matrix)


def deepest_kernel(
    sizes, thr_ref, before, own, after, bands_m, both_m, time_two, low_states, high_states, coarse_out, *outs
):
    stack = jnp.concatenate([before[...], own[...], after[...]], 0)
    bands = left_dot(bands_m[...], stack)
    row = lax.broadcasted_iota(jnp.int32, bands.shape, 0)
    high = lax.broadcasted_iota(jnp.int32, bands.shape, 1) >= bands.shape[1] // 2
    limit = jnp.where(high, thr_ref[2, 0], 0.0)
    quarter = bands.shape[0] // 4
    for q in range(1, 4):
        limit = jnp.where(row >= q * quarter, jnp.where(high, thr_ref[2, 2 * q], thr_ref[2, 2 * q - 1]), limit)
    state_lows, state_highs = [], []
    rows = coarse_out.shape[0]
    for b, block in enumerate(time_pairs(shrink(bands, limit), time_two[...])):
        where = slice(b * block.shape[1], (b + 1) * block.shape[1])
        both = left_dot(both_m[...], block)
        coarse_out[:, where] = both[:rows]
        low = both[rows:] + low_states[:, where]
        for at in range(0, block.shape[1], LANES):
            state_lows.append(low[:, at : at + LANES])
            state_highs.append(high_states[:, where.start + at : where.start + at + LANES])
    put_joint(sizes, outs, state_lows, state_highs)


def own_back_kernel(low_in, high_in, next_in, coarse_in, low_t, high_t, next_t, time_t, scale_ref, out_ref):
    blocks = []
    for where in steps(low_in):
        rows = coarse_in.shape[0]
        bands = jnp.concatenate([next_in[:rows, where] + coarse_in[:, where], next_in[rows:, where]], 0)
        low = left_dot(low_t[...], low_in[:, where]) + left_dot(next_t[...], bands)
        high = left_dot(high_t[...], high_in[:, where])
        for b in range(0, BLOCK, LANES):
            blocks.append(jnp.concatenate([low[:, b : b + LANES], high[:, b : b + LANES]], 1))
    scale = scale_ref[...]
    for b, block in enumerate(time_synthesis(blocks, time_t[...])):
        out_ref[:, b * BLOCK : (b + 1) * BLOCK] = block * scale


def final_kernel(sizes, own_ref, s0, s1, s2, time_t, time_low, state_t, scale_ref, out_far, out_ref, sems):
    pairs, lows = [], []
    refs = (s0, s1, s2)
    scales = scales_of(refs)
    for start in range(0, own_ref.shape[1] // 2, LANES):
        low, high = take_joint(sizes, refs, scales, slice(start, start + LANES))
        count = high.shape[0]
        pairs.append(jnp.concatenate([low[:count], high], 1))
        lows.append(low[count:])
    level0 = time_synthesis(pairs, time_t[...])
    level1 = synthesis_from_low(lows, time_low[...])
    scale = scale_ref[...]
    going = []
    for b in range(len(pairs)):
        where = slice(b * BLOCK, (b + 1) * BLOCK)
        states = jnp.concatenate([level0[b], level1[b]], 0)
        out_ref[:, where] = own_ref[:, where] + left_dot(state_t[...], states) * scale
        going.append(pltpu.make_async_copy(out_ref.at[:, where], out_far.at[:, where], sems.at[b]))
        going[-1].start()
    for copy in going:
        copy.wait()


def call(kernel, outs, *args, smem=(), far=(), far_outs=(), scratch=(), after=(), cost=None, limit=VMEM_LIMIT):
    spaces = [pltpu.SMEM if i in smem else pltpu.HBM if i in far else pltpu.VMEM for i in range(len(args))]
    spaces += [pl.ANY] * len(after)
    count = len(args)

    def body(*refs):
        kernel(*refs[:count], *refs[count + len(after) :])

    return pl.pallas_call(
        body,
        out_shape=[jax.ShapeDtypeStruct(shape, dtype) for shape, dtype in outs],
        in_specs=[pl.BlockSpec(memory_space=space) for space in spaces],
        out_specs=[
            pl.BlockSpec(memory_space=pltpu.HBM if i in far_outs else pltpu.VMEM) for i in range(len(outs))
        ],
        scratch_shapes=list(scratch),
        compiler_params=pltpu.CompilerParams(vmem_limit_bytes=limit),
        cost_estimate=None
        if cost is None
        else pl.CostEstimate(flops=int(cost), bytes_accessed=0, transcendentals=0),
    )(*args, *after)


def shift(block, inline_by, cross_by):
    inline_devs, cross_devs = lax.axis_size("inl"), lax.axis_size("xl")
    if not cross_by:
        return lax.ppermute(block, "inl", [((i + inline_by) % inline_devs, i) for i in range(inline_devs)])
    if not inline_by:
        return lax.ppermute(block, "xl", [((j + cross_by) % cross_devs, j) for j in range(cross_devs)])
    route = [
        ((i + inline_by) % inline_devs * cross_devs + (j + cross_by) % cross_devs, i * cross_devs + j)
        for i in range(inline_devs)
        for j in range(cross_devs)
    ]
    return lax.ppermute(block, ("inl", "xl"), route)


def exchange(states, ahead):
    corner = shift(states[2], ahead, ahead)
    column = shift(states[1], 0, ahead)
    return [shift(states[0], ahead, 0), column, corner]


def on_device(traces, dest_tile, bin_in_tile, fold, thresholds):
    devices = lax.axis_size("inl") * lax.axis_size("xl")
    trace_count, samples = traces.shape
    tile_rows, tile_cols = fold.shape
    bins = tile_rows * tile_cols
    width = SLOTS * samples // GROUP + LANES
    (outgoing,) = call(
        route_kernel,
        [((devices * GROUP, width), bf16)],
        dest_tile.reshape(1, trace_count),
        bin_in_tile.reshape(1, trace_count),
        traces,
        far=(0, 1, 2),
        far_outs=(0,),
        limit=LARGE_LIMIT,
        scratch=[
            pltpu.VMEM((1, trace_count), jnp.int32),
            pltpu.VMEM((1, trace_count), jnp.int32),
            pltpu.VMEM((trace_count, samples), bf16),
            pltpu.VMEM((devices * GROUP, width), bf16),
            pltpu.SemaphoreType.DMA((6,)),
            pltpu.SemaphoreType.DMA((4,)),
        ],
    )
    arrived = lax.all_to_all(
        outgoing.reshape(devices, GROUP, width), ("inl", "xl"), split_axis=0, concat_axis=0, tiled=True
    ).reshape(devices * GROUP, width)
    scale = (1.0 / jnp.sqrt(fold.astype(f32))).reshape(bins, 1)

    main, following = time_parts()
    time_matrix = np.concatenate([triple(main, 0), triple(following, 0)], 0)
    back_main, back_last = main.T, np.pad(following.T, ((0, 0), (0, BLOCK - LANES)))
    time_back = np.concatenate([triple(back_main, 0), triple(back_last, 0)], 0)
    twice, onward = np.zeros((2, BLOCK, 2 * BLOCK))
    twice[:LANES, :BLOCK] = twice[LANES:, BLOCK:] = back_main[:LANES]
    twice[:LANES, BLOCK:] = onward[LANES:, :BLOCK] = back_last[:LANES]
    last_two = back_last @ twice + back_main @ onward
    assert np.abs(back_last @ onward).max() == 0.0
    time_back_two = np.concatenate([triple(back_main @ twice, 0), triple(last_two, 0)], 0)
    time_back_low = np.concatenate([triple(back_main[:LANES], 0), triple(back_last[:LANES], 0)], 0)
    half, rows2, cols2 = samples // 2, tile_rows // 4, tile_cols // 4
    quarter, last = bins // 4, bins // 16
    own0, edge0, own1, edge1, states01, sizes = joint_matrices(tile_rows, tile_cols)
    assert rows2 == SIDE and cols2 >= SIDE
    bands2, back2 = side_matrices(rows2, cols2)
    count0 = sum(sizes[:3])
    joint_rows = [2 * sizes[0] + sizes[3], 2 * sizes[1] + sizes[4], sizes[2] + 8]
    joint_shapes = [((-(-rows // 16) * 16, half + LANES), jnp.int16) for rows in joint_rows]

    summed, *states = call(
        functools.partial(bin_kernel, sizes),
        [((bins, samples), f32)] + joint_shapes,
        arrived,
        scale,
        time_matrix,
        triple(states01, 1),
        far=(0,),
        limit=MIDDLE_LIMIT,
        scratch=[pltpu.VMEM((devices * GROUP, width), bf16), pltpu.SemaphoreType.DMA((4,))],
    )
    states = exchange(states, 1)
    own_low, own_high, own_next = call(
        own_kernel,
        [((bins, half), f32)] * 2 + [((quarter, half), f32)],
        summed,
        time_matrix,
        triple(own0, 1),
        triple(own1, 1),
        cost=1e9,
    )
    rows_all = rows2 + 2 * SIDE
    (timed,) = call(
        functools.partial(middle_kernel, sizes),
        [((last, half // 2), f32)],
        own_next,
        triple(edge1, 1),
        *states,
        time_matrix,
    )
    before, behind = shift(timed, -1, 0), shift(timed, 1, 0)
    low_details, high_details, low_states, high_states, next_details = call(
        functools.partial(details_kernel, sizes),
        [((bins - quarter, half), f32), ((bins, half), f32)]
        + [((sum(sizes), half), f32), ((count0, half), f32)]
        + [((quarter, half), f32)],
        thresholds,
        own_low,
        own_high,
        triple(edge0, 1),
        *states,
        triple(edge0[quarter:].T, 1),
        triple(edge0.T, 1),
        own_next,
        triple(edge1, 1),
        time_matrix,
        time_back,
        triple(edge1.T, 1),
        smem=(0,),
        after=(timed,),
        cost=1e9,
    )
    stack, firsts, lasts = call(
        functools.partial(sides_kernel, cols2),
        [((rows_all * size, samples // 4), f32) for size in (cols2, SIDE, SIDE)],
        before,
        timed,
        behind,
        after=(low_details,),
    )
    left, right = shift(lasts, 0, -1), shift(firsts, 0, 1)
    coarse1, *states = call(
        functools.partial(deepest_kernel, sizes),
        [((last, half), f32)] + joint_shapes,
        thresholds,
        left,
        stack,
        right,
        triple(bands2, 1),
        triple(np.concatenate([back2, edge1[:last].T @ back2], 0), 1),
        time_back_two,
        low_states,
        high_states,
        smem=(0,),
    )
    states = exchange(states, -1)
    (own_back,) = call(
        own_back_kernel,
        [((bins, samples), f32)],
        low_details,
        high_details,
        next_details,
        coarse1,
        triple(own0[quarter:].T, 1),
        triple(own0.T, 1),
        triple(own1.T, 1),
        time_back,
        scale,
        cost=1e9,
    )
    (denoised,) = call(
        functools.partial(final_kernel, sizes),
        [((bins, samples), f32)],
        own_back,
        *states,
        time_back,
        time_back_low,
        triple(states01.T, 1),
        scale,
        far_outs=(0,),
        scratch=[pltpu.VMEM((bins, samples), f32), pltpu.SemaphoreType.DMA((samples // BLOCK,))],
    )
    return denoised.reshape(tile_rows, tile_cols, samples)


def solution(mesh):
    placed = (P(("inl", "xl"), None), P(("inl", "xl"), None), P(("inl", "xl")), P("inl", "xl"), P())
    return jax.shard_map(
        on_device, mesh=mesh, in_specs=placed, out_specs=P("inl", "xl", None), check_vma=False
    )
```
